32 devices in a mesh: grp: 2 (over x), blk: 16 (over z, y, core).
Axes of the slice: x: 2, y: 2, z: 4, core: 2. Of those that a mesh axis runs over, the one named last changes fastest.
Arguments:
- edge_state: bfloat16 [12288, 512], P(('grp', 'blk')), may hold values from -6 to 6
- basis: bfloat16 [768, 16, 16], P(('grp', 'blk')), may hold values from -1.5 to 1.5
- weights: bfloat16 [3, 512, 512], replicated, may hold values from -0.25 to 0.25
- partner: int32 [96], P(('grp', 'blk')), may hold values from 0 to 5, as said below
- cotangent: bfloat16 [12288, 512], P(('grp', 'blk')), may hold values from -6 to 6
Outputs:
- edge_out: bfloat16 [12288, 512], P(('grp', 'blk'))
- grad_state: bfloat16 [12288, 512], P(('grp', 'blk'))
- weight_grad: float32 [1536, 512], P(('grp', 'blk'))
The draws below stay inside these ranges and needn't reach their ends.
Inputs may be any that keep to these rules, and one draw needn't show every extreme that they name: partner pairs the blocks of each group: partner[partner[k]] = k within the group, and a block may be its own partner. A device pairs at most 1 of its blocks with blocks of any one other device of its group, and exactly 1 with those of one of them.
All inputs are finite; a program needn't handle non-finite values.
Results may differ from the reference program's by a relative error of at most 0.008.
Values may be sent and summed in bfloat16 or wider, within the bound.
A program may use at most 64 MiB of HBM per device.

```python
import math
import jax
import jax.numpy as jnp
from jax import lax

D = 512
NBR = 16
BLOCK = 128
CAP = 1
NB = 3
EDGES = 12288
ATOMS = 768
N_GRP = 2
N_BLK = 16


def draw_partner(key, part):

    def one_group(group_key):
        star_key, count_key, perm_key = jax.random.split(group_key, 3)
        star = jax.random.randint(star_key, (), 1, N_GRP)
        extra = jax.random.randint(count_key, (N_GRP,), 0, CAP + 1)
        masks = jnp.arange(N_GRP, dtype=jnp.int32)
        counts = jnp.where(masks == star, CAP, extra)
        counts = jnp.where(masks == 0, 0, counts)
        ends = jnp.cumsum(counts)
        starts = ends - counts
        rounds = jnp.arange(NB, dtype=jnp.int32)
        inside = (rounds[:, None] >= starts[None, :]) & (rounds[:, None] < ends[None, :])
        round_mask = jnp.sum(jnp.where(inside, masks[None, :], 0), axis=1).astype(jnp.int32)
        perm_keys = jax.random.split(perm_key, N_GRP)
        perms = jax.vmap(lambda single: jax.random.permutation(single, NB))(perm_keys).astype(jnp.int32)
        peer = jnp.bitwise_xor(masks[:, None], round_mask[None, :])
        peer_block = perms[peer, rounds[None, :]]
        value = (peer * NB + peer_block).astype(jnp.int32)
        inverse = jnp.argsort(perms, axis=1).astype(jnp.int32)
        return jnp.take_along_axis(value, inverse, axis=1)
    groups = jax.vmap(one_group)(jax.random.split(key, N_BLK))
    return jnp.swapaxes(groups, 0, 1).reshape(-1).astype(jnp.int32)


def with_spikes(entries, own_key, source, target, parts, factor):
    def block_of(dim):
        return (jnp.arange(entries.shape[dim]) // (entries.shape[dim] // parts)).reshape((-1,) + (1,) * (entries.ndim - 1 - dim))

    one_side = jax.random.permutation(own_key, parts)[block_of(target)]
    far = (block_of(target) + parts // 2) % parts
    return jnp.where((block_of(source) == one_side) | (block_of(source) == far), factor * entries, entries)


def steps_of(rng, dims, shards, smallest, top_value):
    def one(position, blocks):
        heights = jax.random.uniform(jax.random.fold_in(jax.random.fold_in(rng, 6), position), (blocks,), jnp.float32, smallest / len(shards), top_value / len(shards))
        return jnp.repeat(jnp.exp(heights), dims[position] // blocks).reshape((-1,) + (1,) * (len(dims) - position - 1))

    level = one(*shards[0])
    for cut in shards[1:]:
        level = level * one(*cut)
    return level


def bell_draw(rng, dims, scale, bound, shards=(), kind=jnp.bfloat16):
    values = jax.random.normal(rng, dims, jnp.float32) * scale
    if len(shards) > 0:
        values = steps_of(rng, dims, shards, -0.22, 0.18) * values
    return jnp.clip(values, min=-bound, max=bound).astype(kind)


def heavy_noise(stream_key, extent, scale, reach, cuts, heavy, kind=jnp.bfloat16):
    array = scale * jax.random.normal(stream_key, extent, jnp.float32)
    if cuts:
        array = array * steps_of(stream_key, extent, cuts, -0.22, 0.18)
    return jnp.clip(with_spikes(array, jax.random.fold_in(stream_key, 3), *heavy), -reach, reach).astype(kind)


def setup_inputs(seed: int = 0) -> dict:
    arg_keys = jax.random.split(jax.random.key(seed), 6)
    edge_state = bell_draw(arg_keys[0], (EDGES, D), 1.0, 6.0, ((0, 32),))
    basis = bell_draw(arg_keys[1], (ATOMS, NBR, NBR), 0.25, 1.5, ((0, 32),))
    weights = bell_draw(arg_keys[2], (3, D, D), D ** -0.5, 0.25)
    partner = draw_partner(jax.random.fold_in(arg_keys[5], 71), 0)
    cotangent = heavy_noise(arg_keys[4], (EDGES, D), 1.0, 6.0, ((0, 32),), (0, 1, 32, 2.75))
    return {"edge_state": edge_state, "basis": basis, "weights": weights, "partner": partner, "cotangent": cotangent}


def norm_rows(hidden):
    return hidden * lax.rsqrt(lax.optimization_barrier(jnp.mean(hidden * hidden, axis=-1, keepdims=True)) + 1e-06)

def layer_forward(hidden, weight):
    normed = norm_rows(hidden).astype(jnp.bfloat16)
    preact = jnp.dot(normed, weight, preferred_element_type=jnp.float32)
    return (hidden + jax.nn.silu(preact), normed, preact)

def layer_backward(hidden, normed, preact, weight, upstream):
    sigma = jax.nn.sigmoid(preact)
    grad_pre = (upstream * sigma * (1.0 + preact * (1.0 - sigma))).astype(jnp.bfloat16)
    grad_weight = lax.dot_general(normed, grad_pre, (((0,), (0,)), ((), ())), preferred_element_type=jnp.float32)
    grad_normed = lax.dot_general(grad_pre, weight, (((1,), (1,)), ((), ())), preferred_element_type=jnp.float32)
    inverse = lax.rsqrt(lax.optimization_barrier(jnp.mean(hidden * hidden, axis=-1, keepdims=True)) + 1e-06)
    unit = hidden * inverse
    inner = lax.optimization_barrier(jnp.mean(grad_normed * unit, axis=-1, keepdims=True))
    return (upstream + inverse * (grad_normed - unit * inner), grad_weight)

def flip_rows(blocks):
    count, height, width = blocks.shape
    return blocks.reshape(count, height // 2, 2, width)[:, :, ::-1, :].reshape(count, height, width)

def reverse_group(values, group_partner):
    blocks = values.reshape(-1, BLOCK, D)
    return flip_rows(blocks[group_partner]).reshape(-1, D)

def reference(edge_state, basis, weights, partner, cotangent):
    edges_dev = NB * BLOCK
    state_grid = edge_state.reshape(N_GRP, N_BLK, edges_dev, D)
    basis_grid = basis.reshape(N_GRP, N_BLK, edges_dev // NBR, NBR, NBR)
    cot_grid = cotangent.reshape(N_GRP, N_BLK, edges_dev, D)
    partner_grid = partner.reshape(N_GRP, N_BLK, NB)

    def one_group(total, group_index):
        states = lax.dynamic_index_in_dim(state_grid, group_index, 1, keepdims=False)
        bases = lax.dynamic_index_in_dim(basis_grid, group_index, 1, keepdims=False).reshape(-1, NBR, NBR)
        upstream = lax.dynamic_index_in_dim(cot_grid, group_index, 1, keepdims=False).reshape(-1, D)
        group_partner = lax.dynamic_index_in_dim(partner_grid, group_index, 1, keepdims=False).reshape(-1)
        bases_wide = bases.astype(jnp.float32)
        mixed = jnp.einsum('aij,ajd->aid', bases_wide, states.reshape(-1, NBR, D).astype(jnp.float32)).reshape(-1, D)
        first, normed_one, pre_one = layer_forward(mixed, weights[0])
        second, normed_two, pre_two = layer_forward(first, weights[1])
        sent = second.astype(jnp.bfloat16)
        reversed_state = reverse_group(sent, group_partner)
        summed = second + reversed_state.astype(jnp.float32)
        final, normed_three, pre_three = layer_forward(summed, weights[2])
        grad_summed, grad_three = layer_backward(summed, normed_three, pre_three, weights[2], upstream.astype(jnp.float32))
        grad_reversed = grad_summed.astype(jnp.bfloat16)
        grad_sent = reverse_group(grad_reversed, group_partner)
        grad_second = grad_summed + grad_sent.astype(jnp.float32)
        grad_first, grad_two = layer_backward(first, normed_two, pre_two, weights[1], grad_second)
        grad_mixed, grad_one = layer_backward(mixed, normed_one, pre_one, weights[0], grad_first)
        grad_round = grad_mixed.astype(jnp.bfloat16).reshape(-1, NBR, D)
        grad_input = jnp.einsum('aij,aid->ajd', bases_wide, grad_round.astype(jnp.float32))
        outputs = final.astype(jnp.bfloat16).reshape(N_GRP, edges_dev, D)
        grads = grad_input.astype(jnp.bfloat16).reshape(N_GRP, edges_dev, D)
        total = total + jnp.concatenate([grad_one, grad_two, grad_three], axis=0)
        return (total, (outputs, grads))
    start = jnp.zeros((3 * D, D), jnp.float32)
    total, (outputs, grads) = lax.scan(one_group, start, jnp.arange(N_BLK))
    edge_out = jnp.swapaxes(outputs, 0, 1).reshape(EDGES, D)
    grad_state = jnp.swapaxes(grads, 0, 1).reshape(EDGES, D)
    weight_grad = total * (1.0 / math.sqrt(EDGES))
    return (edge_out, grad_state, weight_grad)
```

```python
import functools
import math

import jax
import jax.numpy as jnp
from jax import lax
from jax.experimental import pallas as pl
from jax.experimental.pallas import tpu as pltpu
from jax.sharding import PartitionSpec as P

NBR = 16
CAP = 1
BLOCK = 128
CHUNK = 16
EPS = 1e-06
MESH = pl.DeviceIdType.MESH
BF16 = jnp.bfloat16
F32 = jnp.float32


def dot(a, b, ca=1, cb=0):
    return lax.dot_general(a, b, (((ca,), (cb,)), ((), ())), preferred_element_type=F32)


def inverse_rms(h):
    return lax.rsqrt(jnp.mean(h * h, axis=-1, keepdims=True) + EPS)


def flip(x):
    rows = x.shape[0]
    even = lax.broadcasted_iota(jnp.int32, x.shape, 0) % 2 == 0
    return jnp.where(even, pltpu.roll(x, rows - 1, 0), pltpu.roll(x, 1, 0))


def mixing_matrix(basis):
    rows = basis.shape[0]
    spread = (
        lax.broadcasted_iota(jnp.int32, (NBR, rows), 1) % NBR
        == lax.broadcasted_iota(jnp.int32, (NBR, rows), 0)
    ).astype(F32).astype(BF16)
    wide = dot(basis, spread)
    same = (
        lax.broadcasted_iota(jnp.int32, (rows, rows), 0) // NBR
        == lax.broadcasted_iota(jnp.int32, (rows, rows), 1) // NBR
    )
    return jnp.where(same, wide, 0.0).astype(BF16)


def forward(h, w_ref, layer, n_ref, rows):
    inv = inverse_rms(h)
    normed = (h * inv).astype(BF16)
    n_ref[layer, rows, :] = normed
    pre = dot(normed, w_ref[layer])
    s = 0.5 * jnp.tanh(0.5 * pre) + 0.5
    slope = s * (1.0 + pre * (1.0 - s))
    return h + pre * s, (inv, slope)


def backward(h, saved, w_ref, layer, g, d_ref, rows):
    inv, slope = saved
    dpre = (g * slope).astype(BF16)
    d_ref[layer, rows, :] = dpre
    dn = dot(dpre, w_ref[layer], 1, 1)
    u = h * inv
    inner = jnp.mean(dn * u, axis=-1, keepdims=True)
    return g + inv * (dn - u * inner)


def kernel(
    n_blk,
    scale,
    partner_ref,
    state_ref,
    basis_ref,
    w_ref,
    cot_ref,
    out_ref,
    gstate_ref,
    wgrad_ref,
    n_ref,
    d_ref,
    eout_ref,
    gout_ref,
    sent_ref,
    give_ref,
    take_ref,
    half_ref,
    own_ref,
    half_in_ref,
    part_ref,
    part_in_ref,
    piece_ref,
    final_ref,
    give_sem,
    take_sem,
    half_sem,
    half_in_sem,
    part_sem,
    part_in_sem,
    piece_sem,
    final_sem,
):
    x = lax.axis_index("grp")
    b = lax.axis_index("blk")
    me = x * n_blk + b
    core = b % 2
    y = (b // 2) % 2
    z = b // 4
    count = 2 * n_blk
    width = w_ref.shape[2]

    barrier = pltpu.get_barrier_semaphore()

    def greet(step, carry):
        other = (me + step) % count
        pl.semaphore_signal(
            barrier, inc=1, device_id=(other // n_blk, other % n_blk), device_id_type=MESH
        )
        return carry

    lax.fori_loop(1, count, greet, 0)

    base = x * 3
    p0, p1, p2 = partner_ref[0], partner_ref[1], partner_ref[2]
    sides = [jnp.minimum(jnp.maximum(p - 2, 0), 1) - x for p in (p0, p1, p2)]
    away0, away1, away2 = (side * side for side in sides)
    first_pos = jnp.minimum(away1 + 2 * away2, 2)
    pos1 = away0
    pos2 = 2 - away2
    shift = away0 * p1 + (1 - away0) * p0 - base - pos1
    swapped = jnp.minimum(shift * shift, 1)
    place = (1 - away0, jnp.minimum(away0 + 2 * away2, 2), 2 - 2 * away2)

    def pair(ref):
        return jnp.concatenate([ref[pos1], ref[pos2]], axis=0)

    a_rows, b_rows = pl.ds(0, BLOCK), pl.ds(BLOCK, 2 * BLOCK)

    def exchange(step):
        return pltpu.make_async_remote_copy(
            src_ref=give_ref.at[step],
            dst_ref=take_ref.at[step],
            send_sem=give_sem.at[step],
            recv_sem=take_sem.at[step],
            device_id=(1 - x, b),
            device_id_type=MESH,
        )

    def local_reverse(v, step):
        sent_ref[step] = v.astype(BF16).reshape(2, BLOCK, width)
        other = jnp.concatenate(
            [sent_ref[step, swapped], sent_ref[step, 1 - swapped]], axis=0
        )
        return flip(other.astype(F32))

    def half_copy(layer):
        return pltpu.make_async_remote_copy(
            src_ref=half_ref.at[layer],
            dst_ref=half_in_ref.at[layer],
            send_sem=half_sem.at[layer],
            recv_sem=half_in_sem.at[layer],
            device_id=(x, b + 1 - 2 * core),
            device_id_type=MESH,
        )

    half_rows = width // 2
    quarter = half_rows // 4

    def send_half(layer):
        def columns(c):
            return n_ref[layer, :, pl.ds(pl.multiple_of(c * half_rows, half_rows), half_rows)]

        d = d_ref[layer]
        half_ref[layer] = dot(columns(1 - core), d, 0, 0).astype(BF16)
        half_copy(layer).start()
        own_ref[layer] = dot(columns(core), d, 0, 0)

    def part_copy(layer, r):
        px = 1 - x if r >= 2 else x
        py = 1 - y if r % 2 else y
        return pltpu.make_async_remote_copy(
            src_ref=part_ref.at[layer, 2 * px + py],
            dst_ref=part_in_ref.at[layer, r - 1],
            send_sem=part_sem.at[layer, r - 1],
            recv_sem=part_in_sem.at[layer, r - 1],
            device_id=(px, 4 * z + 2 * py + core),
            device_id_type=MESH,
        )

    def send_parts(layer):
        half_copy(layer).wait_recv()
        total = own_ref[layer] + half_in_ref[layer].astype(F32)
        part_ref[layer] = total.astype(BF16).reshape(4, quarter, width)
        for r in (3, 2, 1):
            part_copy(layer, r).start()

    def piece_copy(layer, t):
        c = 32 * layer + 16 * core + 4 * (2 * x + y) + t
        dest = c // 3
        copy = pltpu.make_async_remote_copy(
            src_ref=piece_ref.at[layer, t],
            dst_ref=final_ref.at[c % 3, z],
            send_sem=piece_sem.at[layer, t],
            recv_sem=final_sem.at[c % 3, z],
            device_id=(dest // n_blk, dest % n_blk),
            device_id_type=MESH,
        )
        return c, dest, copy

    def send_pieces(layer):
        for r in (1, 2, 3):
            part_copy(layer, r).wait_recv()
        total = part_ref[layer, 2 * x + y].astype(F32)
        for r in (1, 2, 3):
            total = total + part_in_ref[layer, r - 1].astype(F32)
        piece_ref[layer] = total.astype(BF16).reshape(4, CHUNK, width)
        for t in range(4):
            c, dest, copy = piece_copy(layer, t)

            @pl.when(dest != me)
            def _():
                copy.start()

            @pl.when(dest == me)
            def _():
                final_ref[c % 3, z] = piece_ref[layer, t]

    mix_a = mixing_matrix(basis_ref[first_pos])
    mixed_a = dot(mix_a, state_ref[first_pos])
    first_a, saved_a1 = forward(mixed_a, w_ref, 0, n_ref, a_rows)
    second_a, saved_a2 = forward(first_a, w_ref, 1, n_ref, a_rows)
    give_ref[0] = second_a.astype(BF16)
    pl.semaphore_wait(barrier, count - 1)
    exchange(0).start()

    mix_b = mixing_matrix(pair(basis_ref))
    mixed_b = dot(mix_b, pair(state_ref))
    first_b, saved_b1 = forward(mixed_b, w_ref, 0, n_ref, b_rows)
    second_b, saved_b2 = forward(first_b, w_ref, 1, n_ref, b_rows)
    summed_b = second_b + local_reverse(second_b, 0)
    final_b, saved_b3 = forward(summed_b, w_ref, 2, n_ref, b_rows)
    eout_ref[pl.ds(1, 2)] = final_b.astype(BF16).reshape(2, BLOCK, width)
    gs_b = backward(summed_b, saved_b3, w_ref, 2, pair(cot_ref).astype(F32), d_ref, b_rows)

    exchange(0).wait_recv()
    summed_a = second_a + flip(take_ref[0].astype(F32))
    final_a, saved_a3 = forward(summed_a, w_ref, 2, n_ref, a_rows)
    eout_ref[0] = final_a.astype(BF16)
    gs_a = backward(
        summed_a, saved_a3, w_ref, 2, cot_ref[first_pos].astype(F32), d_ref, a_rows
    )
    give_ref[1] = gs_a.astype(BF16)
    exchange(1).start()

    send_half(2)

    gsec_b = gs_b + local_reverse(gs_b, 1)
    gf_b = backward(first_b, saved_b2, w_ref, 1, gsec_b, d_ref, b_rows)
    send_parts(2)
    gm_b = backward(mixed_b, saved_b1, w_ref, 0, gf_b, d_ref, b_rows)
    gout_ref[pl.ds(1, 2)] = dot(mix_b, gm_b.astype(BF16), 0, 0).astype(BF16).reshape(
        2, BLOCK, width
    )

    exchange(1).wait_recv()
    gsec_a = gs_a + flip(take_ref[1].astype(F32))
    gf_a = backward(first_a, saved_a2, w_ref, 1, gsec_a, d_ref, a_rows)
    send_half(1)
    gm_a = backward(mixed_a, saved_a1, w_ref, 0, gf_a, d_ref, a_rows)
    send_half(0)
    send_parts(1)
    send_pieces(2)
    send_parts(0)
    gout_ref[0] = dot(mix_a, gm_a.astype(BF16), 0, 0).astype(BF16)

    for k in range(3):
        out_ref[k] = eout_ref[place[k]]
        gstate_ref[k] = gout_ref[place[k]]

    send_pieces(1)
    send_pieces(0)

    for j in range(3):
        c = 3 * me + j
        i = c % 32
        q = (i % 16) // 4
        for plane in range(4):
            source = (q // 2) * n_blk + 4 * plane + 2 * (q % 2) + i // 16

            @pl.when(source != me)
            def _():
                pltpu.make_async_remote_copy(
                    src_ref=piece_ref.at[0, 0],
                    dst_ref=final_ref.at[j, plane],
                    send_sem=piece_sem.at[0, 0],
                    recv_sem=final_sem.at[j, plane],
                    device_id=(1 - x, b),
                    device_id_type=MESH,
                ).wait_recv()

    for j in range(3):
        total = final_ref[j, 0].astype(F32)
        for plane in range(1, 4):
            total = total + final_ref[j, plane].astype(F32)
        wgrad_ref[pl.ds(j * CHUNK, CHUNK), :] = total * scale

    for step in range(2):
        exchange(step).wait_send()
    for layer in range(3):
        half_copy(layer).wait_send()
        for r in (1, 2, 3):
            part_copy(layer, r).wait_send()
        for t in range(4):
            c, dest, copy = piece_copy(layer, t)

            @pl.when(dest != me)
            def _():
                copy.wait_send()


def local_fast(n_blk, edge_state, basis, weights, partner, cotangent):
    rows, width = edge_state.shape
    total_edges = rows * 2 * n_blk
    half = width // 2
    blocks = (rows // BLOCK, BLOCK, width)
    vmem = pl.BlockSpec(memory_space=pltpu.VMEM)
    dma = pltpu.SemaphoreType.DMA
    out, gstate, wgrad = pl.pallas_call(
        functools.partial(kernel, n_blk, 1.0 / math.sqrt(total_edges)),
        out_shape=(
            jax.ShapeDtypeStruct(blocks, BF16),
            jax.ShapeDtypeStruct(blocks, BF16),
            jax.ShapeDtypeStruct((3 * CHUNK, width), F32),
        ),
        in_specs=[pl.BlockSpec(memory_space=pltpu.SMEM)] + [vmem] * 4,
        out_specs=(vmem, vmem, vmem),
        scratch_shapes=[
            pltpu.VMEM((3, rows, width), BF16),
            pltpu.VMEM((3, rows, width), BF16),
            pltpu.VMEM(blocks, BF16),
            pltpu.VMEM(blocks, BF16),
            pltpu.VMEM((2, 2, BLOCK, width), BF16),
            pltpu.VMEM((2, BLOCK, width), BF16),
            pltpu.VMEM((2, BLOCK, width), BF16),
            pltpu.VMEM((3, half, width), BF16),
            pltpu.VMEM((3, half, width), F32),
            pltpu.VMEM((3, half, width), BF16),
            pltpu.VMEM((3, 4, half // 4, width), BF16),
            pltpu.VMEM((3, 3, half // 4, width), BF16),
            pltpu.VMEM((3, 4, CHUNK, width), BF16),
            pltpu.VMEM((3, 4, CHUNK, width), BF16),
            dma((2,)),
            dma((2,)),
            dma((3,)),
            dma((3,)),
            dma((3, 3)),
            dma((3, 3)),
            dma((3, 4)),
            dma((3, 4)),
        ],
        compiler_params=pltpu.CompilerParams(
            collective_id=0, has_side_effects=True, vmem_limit_bytes=40 * 2**20
        ),
    )(
        partner,
        edge_state.reshape(blocks),
        basis.reshape(-1, BLOCK, NBR),
        weights,
        cotangent.reshape(blocks),
    )
    return out.reshape(rows, width), gstate.reshape(rows, width), wgrad


def norm_rows(hidden):
    return hidden * lax.rsqrt(jnp.mean(hidden * hidden, axis=-1, keepdims=True) + 1e-06)


def layer_forward(hidden, weight):
    normed = norm_rows(hidden).astype(jnp.bfloat16)
    preact = jnp.dot(normed, weight, preferred_element_type=jnp.float32)
    return (hidden + jax.nn.silu(preact), normed, preact)


def layer_backward(hidden, normed, preact, weight, upstream):
    sigma = jax.nn.sigmoid(preact)
    grad_pre = (upstream * sigma * (1.0 + preact * (1.0 - sigma))).astype(jnp.bfloat16)
    grad_weight = lax.dot_general(
        normed, grad_pre, (((0,), (0,)), ((), ())), preferred_element_type=jnp.float32
    )
    grad_normed = lax.dot_general(
        grad_pre, weight, (((1,), (1,)), ((), ())), preferred_element_type=jnp.float32
    )
    inverse = lax.rsqrt(jnp.mean(hidden * hidden, axis=-1, keepdims=True) + 1e-06)
    unit = hidden * inverse
    inner = jnp.mean(grad_normed * unit, axis=-1, keepdims=True)
    return (upstream + inverse * (grad_normed - unit * inner), grad_weight)


def flip_rows(blocks):
    count, height, width = blocks.shape
    return blocks.reshape(count, height // 2, 2, width)[:, :, ::-1, :].reshape(count, height, width)


def route_plan(partner, own_index, group_count):
    block_count = partner.shape[0]
    target = partner // block_count
    remote = partner % block_count
    order = jnp.arange(block_count)
    same = target[:, None] == target[None, :]
    send_rank = jnp.sum(same & (order[None, :] < order[:, None]), axis=1)
    recv_rank = jnp.sum(same & (remote[None, :] < remote[:, None]), axis=1)
    local_pair = target == own_index
    slots = jnp.arange(group_count * CAP)
    send_slot = target * CAP + send_rank
    recv_slot = target * CAP + recv_rank
    pack_matrix = ((slots[:, None] == send_slot[None, :]) & ~local_pair[None, :]).astype(
        jnp.bfloat16
    )
    unpack_matrix = ((recv_slot[:, None] == slots[None, :]) & ~local_pair[:, None]).astype(
        jnp.bfloat16
    )
    return (pack_matrix, unpack_matrix, local_pair)


def pack_blocks(values, pack_matrix, block_count):
    blocks = values.reshape(block_count, -1, values.shape[1])
    return jnp.einsum("sn,nrd->srd", pack_matrix, blocks, preferred_element_type=jnp.bfloat16)


def unpack_blocks(arrived, unpack_matrix, local_pair, values, block_count):
    blocks = values.reshape(block_count, -1, values.shape[1])
    distant = jnp.einsum("ns,srd->nrd", unpack_matrix, arrived, preferred_element_type=jnp.bfloat16)
    joined = jnp.where(local_pair[:, None, None], blocks, distant)
    return flip_rows(joined).reshape(values.shape)


def local(edge_state, basis, weights, partner, cotangent):
    row_count, width = edge_state.shape
    block_count = partner.shape[0]
    group_count = lax.axis_size("grp")
    own_index = lax.axis_index("grp")
    total_edges = row_count * group_count * lax.axis_size("blk")
    pack_matrix, unpack_matrix, local_pair = route_plan(partner, own_index, group_count)
    mixed = jnp.einsum(
        "aij,ajd->aid",
        basis,
        edge_state.reshape(-1, NBR, width),
        preferred_element_type=jnp.float32,
    ).reshape(row_count, width)
    first, normed_one, pre_one = layer_forward(mixed, weights[0])
    second, normed_two, pre_two = layer_forward(first, weights[1])
    sent = second.astype(jnp.bfloat16)
    arrived = lax.all_to_all(
        pack_blocks(sent, pack_matrix, block_count), "grp", split_axis=0, concat_axis=0, tiled=True
    )
    reversed_state = unpack_blocks(arrived, unpack_matrix, local_pair, sent, block_count)
    summed = second + reversed_state.astype(jnp.float32)
    final, normed_three, pre_three = layer_forward(summed, weights[2])
    edge_out = final.astype(jnp.bfloat16)
    grad_summed, grad_three = layer_backward(
        summed, normed_three, pre_three, weights[2], cotangent.astype(jnp.float32)
    )
    grad_reversed = grad_summed.astype(jnp.bfloat16)
    returned = lax.all_to_all(
        pack_blocks(grad_reversed, pack_matrix, block_count),
        "grp",
        split_axis=0,
        concat_axis=0,
        tiled=True,
    )
    grad_sent = unpack_blocks(returned, unpack_matrix, local_pair, grad_reversed, block_count)
    grad_second = grad_summed + grad_sent.astype(jnp.float32)
    grad_first, grad_two = layer_backward(first, normed_two, pre_two, weights[1], grad_second)
    grad_mixed, grad_one = layer_backward(mixed, normed_one, pre_one, weights[0], grad_first)
    grad_round = grad_mixed.astype(jnp.bfloat16).reshape(-1, NBR, width)
    grad_state = (
        jnp.einsum("aij,aid->ajd", basis, grad_round, preferred_element_type=jnp.float32)
        .reshape(row_count, width)
        .astype(jnp.bfloat16)
    )
    local_grads = jnp.concatenate([grad_one, grad_two, grad_three], axis=0)
    group_part = lax.psum_scatter(
        local_grads.astype(jnp.bfloat16), "grp", scatter_dimension=0, tiled=True
    ).astype(jnp.float32)
    summed_grads = lax.psum_scatter(group_part, "blk", scatter_dimension=0, tiled=True)
    weight_grad = summed_grads * (1.0 / math.sqrt(total_edges))
    return (edge_out, grad_state, weight_grad)


def solution(mesh):
    spread = P(("grp", "blk"))
    wide = P(("grp", "blk"), None)
    in_specs = (wide, P(("grp", "blk"), None, None), P(), spread, wide)
    body = local
    if mesh.shape["grp"] == 2 and mesh.shape["blk"] == 16:
        body = functools.partial(local_fast, mesh.shape["blk"])
    return jax.shard_map(
        body, mesh=mesh, in_specs=in_specs, out_specs=(wide, wide, wide), check_vma=False
    )
```

```python
import functools
import math

import jax
import jax.numpy as jnp
from jax import lax
from jax.experimental import pallas as pl
from jax.experimental.pallas import tpu as pltpu
from jax.sharding import PartitionSpec as P

NBR = 16
CAP = 1
BLOCK = 128
CHUNK = 16
EPS = 1e-06
MESH = pl.DeviceIdType.MESH
BF16 = jnp.bfloat16
F32 = jnp.float32


def dot(a, b, ca=1, cb=0):
    return lax.dot_general(a, b, (((ca,), (cb,)), ((), ())), preferred_element_type=F32)


def inverse_rms(h):
    return lax.rsqrt(jnp.mean(h * h, axis=-1, keepdims=True) + EPS)


def flip(x):
    rows = x.shape[0]
    even = lax.broadcasted_iota(jnp.int32, x.shape, 0) % 2 == 0
    return jnp.where(even, pltpu.roll(x, rows - 1, 0), pltpu.roll(x, 1, 0))


def mixing_matrix(basis, blocks):
    flat = basis.reshape(NBR * NBR, basis.shape[2])
    rows = BLOCK * len(blocks)

    def iota(shape, dim):
        return lax.broadcasted_iota(jnp.int32, shape, dim)

    def mask(hit):
        return hit.astype(F32).astype(BF16)

    atom_shape = (rows, basis.shape[2])
    row = iota(atom_shape, 0)
    first_atom = blocks[0] * (BLOCK // NBR)
    if len(blocks) == 2:
        first_atom = first_atom + (row // BLOCK) * ((blocks[1] - blocks[0]) * (BLOCK // NBR))
    pick = mask(first_atom + (row % BLOCK) // NBR == iota(atom_shape, 1))
    own = dot(pick, flat, 1, 1)
    own_shape = (rows, NBR * NBR)
    own = jnp.where(iota(own_shape, 0) % NBR == iota(own_shape, 1) // NBR, own, 0.0).astype(BF16)
    spread_shape = (NBR * NBR, rows)
    spread = mask(iota(spread_shape, 0) % NBR == iota(spread_shape, 1) % NBR)
    wide = dot(own, spread)
    same = iota((rows, rows), 0) // NBR == iota((rows, rows), 1) // NBR
    return jnp.where(same, wide, 0.0).astype(BF16)


def forward(h, w_ref, layer, n_ref, rows):
    inv = inverse_rms(h)
    normed = (h * inv).astype(BF16)
    n_ref[layer, rows, :] = normed
    pre = dot(normed, w_ref[layer])
    s = 0.5 * jnp.tanh(0.5 * pre) + 0.5
    slope = s * (1.0 + pre * (1.0 - s))
    return h + pre * s, (inv, slope)


def backward(h, saved, w_ref, layer, g, d_ref, rows):
    inv, slope = saved
    dpre = (g * slope).astype(BF16)
    d_ref[layer, rows, :] = dpre
    dn = dot(dpre, w_ref[layer], 1, 1)
    u = h * inv
    inner = jnp.mean(dn * u, axis=-1, keepdims=True)
    return g + inv * (dn - u * inner)


def kernel(
    n_blk,
    scale,
    partner_hbm,
    state_hbm,
    basis_hbm,
    w_hbm,
    cot_hbm,
    out_ref,
    gstate_ref,
    wgrad_ref,
    partner_ref,
    state_ref,
    basis_ref,
    w_ref,
    cot_ref,
    n_ref,
    d_ref,
    eout_ref,
    gout_ref,
    sent_ref,
    give_ref,
    take_ref,
    half_ref,
    own_ref,
    half_in_ref,
    part_ref,
    part_in_ref,
    quad_ref,
    quad_in_ref,
    piece_ref,
    final_ref,
    in_sem,
    give_sem,
    take_sem,
    half_sem,
    half_in_sem,
    part_sem,
    part_in_sem,
    piece_sem,
    final_sem,
):
    x = lax.axis_index("grp")
    b = lax.axis_index("blk")
    me = x * n_blk + b
    core = b % 2
    y = (b // 2) % 2
    z = b // 4
    count = 2 * n_blk
    width = w_ref.shape[2]

    loads = [
        pltpu.make_async_copy(src, dst, in_sem.at[number])
        for number, (src, dst) in enumerate(
            [
                (partner_hbm, partner_ref),
                (basis_hbm, basis_ref),
                (state_hbm, state_ref),
                (w_hbm.at[0], w_ref.at[0]),
                (w_hbm.at[1], w_ref.at[1]),
                (w_hbm.at[2], w_ref.at[2]),
                (cot_hbm, cot_ref),
            ]
        )
    ]
    for load in loads:
        load.start()

    barrier = pltpu.get_barrier_semaphore()

    def greet(step, carry):
        other = (me + step) % count
        pl.semaphore_signal(
            barrier, inc=1, device_id=(other // n_blk, other % n_blk), device_id_type=MESH
        )
        return carry

    lax.fori_loop(1, count, greet, 0)

    base = x * 3
    loads[0].wait()
    p0, p1, p2 = partner_ref[0], partner_ref[1], partner_ref[2]
    sides = [jnp.minimum(jnp.maximum(p - 2, 0), 1) - x for p in (p0, p1, p2)]
    away0, away1, away2 = (side * side for side in sides)
    first_pos = jnp.minimum(away1 + 2 * away2, 2)
    pos1 = away0
    pos2 = 2 - away2
    shift = away0 * p1 + (1 - away0) * p0 - base - pos1
    swapped = jnp.minimum(shift * shift, 1)
    place = (1 - away0, jnp.minimum(away0 + 2 * away2, 2), 2 - 2 * away2)

    def pair(ref):
        return jnp.concatenate([ref[pos1], ref[pos2]], axis=0)

    a_rows, b_rows = pl.ds(0, BLOCK), pl.ds(BLOCK, 2 * BLOCK)

    def exchange(step):
        return pltpu.make_async_remote_copy(
            src_ref=give_ref.at[step],
            dst_ref=take_ref.at[step],
            send_sem=give_sem.at[step],
            recv_sem=take_sem.at[step],
            device_id=(1 - x, b),
            device_id_type=MESH,
        )

    def local_reverse(v, step):
        sent_ref[step] = v.astype(BF16).reshape(2, BLOCK, width)
        other = jnp.concatenate(
            [sent_ref[step, swapped], sent_ref[step, 1 - swapped]], axis=0
        )
        return flip(other.astype(F32))

    def half_copy(layer):
        return pltpu.make_async_remote_copy(
            src_ref=half_ref.at[layer],
            dst_ref=half_in_ref.at[layer],
            send_sem=half_sem.at[layer],
            recv_sem=half_in_sem.at[layer],
            device_id=(x, b + 1 - 2 * core),
            device_id_type=MESH,
        )

    half_rows = width // 2
    eighth = half_rows // 8

    def send_half(layer):
        def columns(c):
            return n_ref[layer, :, pl.ds(pl.multiple_of(c * half_rows, half_rows), half_rows)]

        d = d_ref[layer]
        half_ref[layer] = dot(columns(1 - core), d, 0, 0).astype(BF16)
        half_copy(layer).start()
        own_ref[layer] = dot(columns(core), d, 0, 0)

    def sides(layer, piece):
        return (x, y) if piece == 1 and layer < 2 else (y, x)

    def part_copy(layer, piece, hop):
        along_x = (piece == 1 and layer < 2) == (hop == 0)
        near, far = sides(layer, piece)
        if hop == 0:
            src, dst = part_ref.at[layer, piece, 1 - near], part_in_ref.at[layer, piece]
        else:
            src, dst = quad_ref.at[layer, piece, 1 - far], quad_in_ref.at[layer, piece]
        return pltpu.make_async_remote_copy(
            src_ref=src,
            dst_ref=dst,
            send_sem=part_sem.at[layer, piece, hop],
            recv_sem=part_in_sem.at[layer, piece, hop],
            device_id=(1 - x, b) if along_x else (x, b + 2 - 4 * y),
            device_id_type=MESH,
        )

    def send_parts(layer):
        half_copy(layer).wait_recv()
        total = own_ref[layer] + half_in_ref[layer].astype(F32)
        part_ref[layer] = total.astype(BF16).reshape(2, 2, 2, eighth, width)
        for piece in range(2):
            part_copy(layer, piece, 0).start()

    def send_quads(layer):
        for piece in range(2):
            part_copy(layer, piece, 0).wait_recv()
            near, _ = sides(layer, piece)
            total = part_ref[layer, piece, near].astype(F32)
            total = total + part_in_ref[layer, piece].astype(F32)
            quad_ref[layer, piece] = total.astype(BF16)
            part_copy(layer, piece, 1).start()

    def piece_copy(layer, t):
        near, far = sides(layer, t // 2)
        c = 32 * layer + 16 * core + 8 * (t // 2) + 4 * near + 2 * far + t % 2
        dest = c // 3
        copy = pltpu.make_async_remote_copy(
            src_ref=piece_ref.at[layer, t],
            dst_ref=final_ref.at[c % 3, z],
            send_sem=piece_sem.at[layer, t],
            recv_sem=final_sem.at[c % 3, z],
            device_id=(dest // n_blk, dest % n_blk),
            device_id_type=MESH,
        )
        return c, dest, copy

    def send_pieces(layer):
        for piece in range(2):
            part_copy(layer, piece, 1).wait_recv()
            _, far = sides(layer, piece)
            total = quad_ref[layer, piece, far].astype(F32)
            total = total + quad_in_ref[layer, piece].astype(F32)
            piece_ref[layer, pl.ds(2 * piece, 2)] = total.astype(BF16).reshape(2, CHUNK, width)
        for t in range(4):
            c, dest, copy = piece_copy(layer, t)

            @pl.when(dest != me)
            def _():
                copy.start()

            @pl.when(dest == me)
            def _():
                final_ref[c % 3, z] = piece_ref[layer, t]

    loads[1].wait()
    loads[2].wait()
    mix_a = mixing_matrix(basis_ref[...], (first_pos,))
    mixed_a = dot(mix_a, state_ref[first_pos])
    loads[3].wait()
    first_a, saved_a1 = forward(mixed_a, w_ref, 0, n_ref, a_rows)
    loads[4].wait()
    second_a, saved_a2 = forward(first_a, w_ref, 1, n_ref, a_rows)
    give_ref[0] = second_a.astype(BF16)
    pl.semaphore_wait(barrier, count - 1)
    exchange(0).start()

    mix_b = mixing_matrix(basis_ref[...], (pos1, pos2))
    mixed_b = dot(mix_b, pair(state_ref))
    first_b, saved_b1 = forward(mixed_b, w_ref, 0, n_ref, b_rows)
    second_b, saved_b2 = forward(first_b, w_ref, 1, n_ref, b_rows)
    summed_b = second_b + local_reverse(second_b, 0)
    loads[5].wait()
    final_b, saved_b3 = forward(summed_b, w_ref, 2, n_ref, b_rows)
    eout_ref[pl.ds(1, 2)] = final_b.astype(BF16).reshape(2, BLOCK, width)

    exchange(0).wait_recv()
    summed_a = second_a + flip(take_ref[0].astype(F32))
    final_a, saved_a3 = forward(summed_a, w_ref, 2, n_ref, a_rows)
    eout_ref[0] = final_a.astype(BF16)
    loads[6].wait()
    gs_a = backward(
        summed_a, saved_a3, w_ref, 2, cot_ref[first_pos].astype(F32), d_ref, a_rows
    )
    give_ref[1] = gs_a.astype(BF16)
    exchange(1).start()

    gs_b = backward(summed_b, saved_b3, w_ref, 2, pair(cot_ref).astype(F32), d_ref, b_rows)
    send_half(2)
    gsec_b = gs_b + local_reverse(gs_b, 1)
    gf_b = backward(first_b, saved_b2, w_ref, 1, gsec_b, d_ref, b_rows)
    send_parts(2)
    gm_b = backward(mixed_b, saved_b1, w_ref, 0, gf_b, d_ref, b_rows)
    gout_ref[pl.ds(1, 2)] = dot(mix_b, gm_b.astype(BF16), 0, 0).astype(BF16).reshape(
        2, BLOCK, width
    )

    exchange(1).wait_recv()
    gsec_a = gs_a + flip(take_ref[1].astype(F32))
    gf_a = backward(first_a, saved_a2, w_ref, 1, gsec_a, d_ref, a_rows)
    send_half(1)
    gm_a = backward(mixed_a, saved_a1, w_ref, 0, gf_a, d_ref, a_rows)
    send_half(0)
    send_parts(1)
    send_quads(2)
    send_parts(0)
    gout_ref[0] = dot(mix_a, gm_a.astype(BF16), 0, 0).astype(BF16)
    send_quads(1)
    send_pieces(2)
    send_quads(0)

    for k in range(3):
        out_ref[k] = eout_ref[place[k]]
        gstate_ref[k] = gout_ref[place[k]]

    send_pieces(1)
    send_pieces(0)

    for j in range(3):
        c = 3 * me + j
        i = c % 32
        near, far = (i // 4) % 2, (i // 2) % 2
        x_first = ((i // 8) % 2) * (1 - c // 64)
        from_y = near + x_first * (far - near)
        from_x = far + x_first * (near - far)
        for plane in range(4):
            source = from_x * n_blk + 4 * plane + 2 * from_y + i // 16

            @pl.when(source != me)
            def _():
                pltpu.make_async_remote_copy(
                    src_ref=piece_ref.at[0, 0],
                    dst_ref=final_ref.at[j, plane],
                    send_sem=piece_sem.at[0, 0],
                    recv_sem=final_sem.at[j, plane],
                    device_id=(1 - x, b),
                    device_id_type=MESH,
                ).wait_recv()

    for j in range(3):
        total = final_ref[j, 0].astype(F32)
        for plane in range(1, 4):
            total = total + final_ref[j, plane].astype(F32)
        wgrad_ref[pl.ds(j * CHUNK, CHUNK), :] = total * scale

    for step in range(2):
        exchange(step).wait_send()
    for layer in range(3):
        half_copy(layer).wait_send()
        for piece in range(2):
            for hop in range(2):
                part_copy(layer, piece, hop).wait_send()
        for t in range(4):
            c, dest, copy = piece_copy(layer, t)

            @pl.when(dest != me)
            def _():
                copy.wait_send()


def local_fast(n_blk, edge_state, basis, weights, partner, cotangent):
    rows, width = edge_state.shape
    total_edges = rows * 2 * n_blk
    half = width // 2
    blocks = (rows // BLOCK, BLOCK, width)
    vmem = pl.BlockSpec(memory_space=pltpu.VMEM)
    dma = pltpu.SemaphoreType.DMA
    out, gstate, wgrad = pl.pallas_call(
        functools.partial(kernel, n_blk, 1.0 / math.sqrt(total_edges)),
        out_shape=(
            jax.ShapeDtypeStruct(blocks, BF16),
            jax.ShapeDtypeStruct(blocks, BF16),
            jax.ShapeDtypeStruct((3 * CHUNK, width), F32),
        ),
        in_specs=[pl.BlockSpec(memory_space=pl.ANY)] * 5,
        out_specs=(vmem, vmem, vmem),
        scratch_shapes=[
            pltpu.SMEM(partner.shape, jnp.int32),
            pltpu.VMEM(blocks, BF16),
            pltpu.VMEM((NBR, NBR, basis.shape[0]), BF16),
            pltpu.VMEM(weights.shape, BF16),
            pltpu.VMEM(blocks, BF16),
            pltpu.VMEM((3, rows, width), BF16),
            pltpu.VMEM((3, rows, width), BF16),
            pltpu.VMEM(blocks, BF16),
            pltpu.VMEM(blocks, BF16),
            pltpu.VMEM((2, 2, BLOCK, width), BF16),
            pltpu.VMEM((2, BLOCK, width), BF16),
            pltpu.VMEM((2, BLOCK, width), BF16),
            pltpu.VMEM((3, half, width), BF16),
            pltpu.VMEM((3, half, width), F32),
            pltpu.VMEM((3, half, width), BF16),
            pltpu.VMEM((3, 2, 2, 2, half // 8, width), BF16),
            pltpu.VMEM((3, 2, 2, half // 8, width), BF16),
            pltpu.VMEM((3, 2, 2, half // 8, width), BF16),
            pltpu.VMEM((3, 2, half // 8, width), BF16),
            pltpu.VMEM((3, 4, CHUNK, width), BF16),
            pltpu.VMEM((3, 4, CHUNK, width), BF16),
            dma((7,)),
            dma((2,)),
            dma((2,)),
            dma((3,)),
            dma((3,)),
            dma((3, 2, 2)),
            dma((3, 2, 2)),
            dma((3, 4)),
            dma((3, 4)),
        ],
        compiler_params=pltpu.CompilerParams(
            collective_id=0, has_side_effects=True, vmem_limit_bytes=56 * 2**20
        ),
    )(
        partner,
        edge_state.reshape(blocks),
        basis.transpose(1, 2, 0),
        weights,
        cotangent.reshape(blocks),
    )
    return out.reshape(rows, width), gstate.reshape(rows, width), wgrad


def norm_rows(hidden):
    return hidden * lax.rsqrt(jnp.mean(hidden * hidden, axis=-1, keepdims=True) + 1e-06)


def layer_forward(hidden, weight):
    normed = norm_rows(hidden).astype(jnp.bfloat16)
    preact = jnp.dot(normed, weight, preferred_element_type=jnp.float32)
    return (hidden + jax.nn.silu(preact), normed, preact)


def layer_backward(hidden, normed, preact, weight, upstream):
    sigma = jax.nn.sigmoid(preact)
    grad_pre = (upstream * sigma * (1.0 + preact * (1.0 - sigma))).astype(jnp.bfloat16)
    grad_weight = lax.dot_general(
        normed, grad_pre, (((0,), (0,)), ((), ())), preferred_element_type=jnp.float32
    )
    grad_normed = lax.dot_general(
        grad_pre, weight, (((1,), (1,)), ((), ())), preferred_element_type=jnp.float32
    )
    inverse = lax.rsqrt(jnp.mean(hidden * hidden, axis=-1, keepdims=True) + 1e-06)
    unit = hidden * inverse
    inner = jnp.mean(grad_normed * unit, axis=-1, keepdims=True)
    return (upstream + inverse * (grad_normed - unit * inner), grad_weight)


def flip_rows(blocks):
    count, height, width = blocks.shape
    return blocks.reshape(count, height // 2, 2, width)[:, :, ::-1, :].reshape(count, height, width)


def route_plan(partner, own_index, group_count):
    block_count = partner.shape[0]
    target = partner // block_count
    remote = partner % block_count
    order = jnp.arange(block_count)
    same = target[:, None] == target[None, :]
    send_rank = jnp.sum(same & (order[None, :] < order[:, None]), axis=1)
    recv_rank = jnp.sum(same & (remote[None, :] < remote[:, None]), axis=1)
    local_pair = target == own_index
    slots = jnp.arange(group_count * CAP)
    send_slot = target * CAP + send_rank
    recv_slot = target * CAP + recv_rank
    pack_matrix = ((slots[:, None] == send_slot[None, :]) & ~local_pair[None, :]).astype(
        jnp.bfloat16
    )
    unpack_matrix = ((recv_slot[:, None] == slots[None, :]) & ~local_pair[:, None]).astype(
        jnp.bfloat16
    )
    return (pack_matrix, unpack_matrix, local_pair)


def pack_blocks(values, pack_matrix, block_count):
    blocks = values.reshape(block_count, -1, values.shape[1])
    return jnp.einsum("sn,nrd->srd", pack_matrix, blocks, preferred_element_type=jnp.bfloat16)


def unpack_blocks(arrived, unpack_matrix, local_pair, values, block_count):
    blocks = values.reshape(block_count, -1, values.shape[1])
    distant = jnp.einsum("ns,srd->nrd", unpack_matrix, arrived, preferred_element_type=jnp.bfloat16)
    joined = jnp.where(local_pair[:, None, None], blocks, distant)
    return flip_rows(joined).reshape(values.shape)


def local(edge_state, basis, weights, partner, cotangent):
    row_count, width = edge_state.shape
    block_count = partner.shape[0]
    group_count = lax.axis_size("grp")
    own_index = lax.axis_index("grp")
    total_edges = row_count * group_count * lax.axis_size("blk")
    pack_matrix, unpack_matrix, local_pair = route_plan(partner, own_index, group_count)
    mixed = jnp.einsum(
        "aij,ajd->aid",
        basis,
        edge_state.reshape(-1, NBR, width),
        preferred_element_type=jnp.float32,
    ).reshape(row_count, width)
    first, normed_one, pre_one = layer_forward(mixed, weights[0])
    second, normed_two, pre_two = layer_forward(first, weights[1])
    sent = second.astype(jnp.bfloat16)
    arrived = lax.all_to_all(
        pack_blocks(sent, pack_matrix, block_count), "grp", split_axis=0, concat_axis=0, tiled=True
    )
    reversed_state = unpack_blocks(arrived, unpack_matrix, local_pair, sent, block_count)
    summed = second + reversed_state.astype(jnp.float32)
    final, normed_three, pre_three = layer_forward(summed, weights[2])
    edge_out = final.astype(jnp.bfloat16)
    grad_summed, grad_three = layer_backward(
        summed, normed_three, pre_three, weights[2], cotangent.astype(jnp.float32)
    )
    grad_reversed = grad_summed.astype(jnp.bfloat16)
    returned = lax.all_to_all(
        pack_blocks(grad_reversed, pack_matrix, block_count),
        "grp",
        split_axis=0,
        concat_axis=0,
        tiled=True,
    )
    grad_sent = unpack_blocks(returned, unpack_matrix, local_pair, grad_reversed, block_count)
    grad_second = grad_summed + grad_sent.astype(jnp.float32)
    grad_first, grad_two = layer_backward(first, normed_two, pre_two, weights[1], grad_second)
    grad_mixed, grad_one = layer_backward(mixed, normed_one, pre_one, weights[0], grad_first)
    grad_round = grad_mixed.astype(jnp.bfloat16).reshape(-1, NBR, width)
    grad_state = (
        jnp.einsum("aij,aid->ajd", basis, grad_round, preferred_element_type=jnp.float32)
        .reshape(row_count, width)
        .astype(jnp.bfloat16)
    )
    local_grads = jnp.concatenate([grad_one, grad_two, grad_three], axis=0)
    group_part = lax.psum_scatter(
        local_grads.astype(jnp.bfloat16), "grp", scatter_dimension=0, tiled=True
    ).astype(jnp.float32)
    summed_grads = lax.psum_scatter(group_part, "blk", scatter_dimension=0, tiled=True)
    weight_grad = summed_grads * (1.0 / math.sqrt(total_edges))
    return (edge_out, grad_state, weight_grad)


def solution(mesh):
    spread = P(("grp", "blk"))
    wide = P(("grp", "blk"), None)
    in_specs = (wide, P(("grp", "blk"), None, None), P(), spread, wide)
    body = local
    if mesh.shape["grp"] == 2 and mesh.shape["blk"] == 16:
        body = functools.partial(local_fast, mesh.shape["blk"])
    return jax.shard_map(
        body, mesh=mesh, in_specs=in_specs, out_specs=(wide, wide, wide), check_vma=False
    )
```

```python
import functools
import math

import jax
import jax.numpy as jnp
from jax import lax
from jax.experimental import pallas as pl
from jax.experimental.pallas import tpu as pltpu
from jax.sharding import PartitionSpec as P

NBR = 16
CAP = 1
BLOCK = 128
CHUNK = 16
EPS = 1e-06
MESH = pl.DeviceIdType.MESH
BF16 = jnp.bfloat16
F32 = jnp.float32


def dot(a, b, ca=1, cb=0):
    return lax.dot_general(a, b, (((ca,), (cb,)), ((), ())), preferred_element_type=F32)


def inverse_rms(h):
    return lax.rsqrt(jnp.mean(h * h, axis=-1, keepdims=True) + EPS)


def flip(x):
    rows = x.shape[0]
    even = lax.broadcasted_iota(jnp.int32, x.shape, 0) % 2 == 0
    return jnp.where(even, pltpu.roll(x, rows - 1, 0), pltpu.roll(x, 1, 0))


def mixing_matrix(basis, blocks):
    flat = basis.reshape(NBR * NBR, basis.shape[2])
    rows = BLOCK * len(blocks)

    def iota(shape, dim):
        return lax.broadcasted_iota(jnp.int32, shape, dim)

    def mask(hit):
        return hit.astype(F32).astype(BF16)

    atom_shape = (rows, basis.shape[2])
    row = iota(atom_shape, 0)
    first_atom = blocks[0] * (BLOCK // NBR)
    if len(blocks) == 2:
        first_atom = first_atom + (row // BLOCK) * ((blocks[1] - blocks[0]) * (BLOCK // NBR))
    pick = mask(first_atom + (row % BLOCK) // NBR == iota(atom_shape, 1))
    own = dot(pick, flat, 1, 1)
    own_shape = (rows, NBR * NBR)
    own = jnp.where(iota(own_shape, 0) % NBR == iota(own_shape, 1) // NBR, own, 0.0).astype(BF16)
    spread_shape = (NBR * NBR, rows)
    spread = mask(iota(spread_shape, 0) % NBR == iota(spread_shape, 1) % NBR)
    wide = dot(own, spread)
    same = iota((rows, rows), 0) // NBR == iota((rows, rows), 1) // NBR
    return jnp.where(same, wide, 0.0).astype(BF16)


def forward(h, w_ref, layer, n_ref, rows):
    inv = inverse_rms(h)
    normed = (h * inv).astype(BF16)
    n_ref[layer, rows, :] = normed
    pre = dot(normed, w_ref[layer])
    s = 0.5 * jnp.tanh(0.5 * pre) + 0.5
    slope = s * (1.0 + pre * (1.0 - s))
    return h + pre * s, (inv, slope)


def backward(h, saved, w_ref, layer, g, d_ref, rows):
    inv, slope = saved
    dpre = (g * slope).astype(BF16)
    d_ref[layer, rows, :] = dpre
    dn = dot(dpre, w_ref[layer], 1, 1)
    u = h * inv
    inner = jnp.mean(dn * u, axis=-1, keepdims=True)
    return g + inv * (dn - u * inner)


def kernel(
    n_blk,
    partner_hbm,
    state_hbm,
    basis_hbm,
    w_hbm,
    cot_hbm,
    out_ref,
    gstate_ref,
    wgrad_ref,
    partner_ref,
    state_ref,
    basis_ref,
    w_ref,
    cot_ref,
    n_ref,
    d_ref,
    eout_ref,
    gout_ref,
    sent_ref,
    give_ref,
    take_ref,
    half_ref,
    own_ref,
    half_in_ref,
    part_ref,
    part_in_ref,
    quad_ref,
    quad_in_ref,
    piece_ref,
    piece_in_ref,
    chunk_ref,
    final_ref,
    in_sem,
    give_sem,
    take_sem,
    half_sem,
    half_in_sem,
    part_sem,
    part_in_sem,
    piece_sem,
    piece_in_sem,
    chunk_sem,
    final_sem,
):
    x = lax.axis_index("grp")
    b = lax.axis_index("blk")
    me = x * n_blk + b
    core = b % 2
    y = (b // 2) % 2
    z = b // 4
    count = 2 * n_blk
    width = w_ref.shape[2]

    loads = [
        pltpu.make_async_copy(src, dst, in_sem.at[number])
        for number, (src, dst) in enumerate(
            [
                (partner_hbm, partner_ref),
                (basis_hbm, basis_ref),
                (state_hbm, state_ref),
                (w_hbm.at[0], w_ref.at[0]),
                (w_hbm.at[1], w_ref.at[1]),
                (w_hbm.at[2], w_ref.at[2]),
                (cot_hbm, cot_ref),
            ]
        )
    ]
    for load in loads:
        load.start()

    barrier = pltpu.get_barrier_semaphore()

    def greet(step, carry):
        other = (me + step) % count
        pl.semaphore_signal(
            barrier, inc=1, device_id=(other // n_blk, other % n_blk), device_id_type=MESH
        )
        return carry

    lax.fori_loop(1, count, greet, 0)

    base = x * 3
    loads[0].wait()
    p0, p1, p2 = partner_ref[0], partner_ref[1], partner_ref[2]
    sides = [jnp.minimum(jnp.maximum(p - 2, 0), 1) - x for p in (p0, p1, p2)]
    away0, away1, away2 = (side * side for side in sides)
    first_pos = jnp.minimum(away1 + 2 * away2, 2)
    pos1 = away0
    pos2 = 2 - away2
    shift = away0 * p1 + (1 - away0) * p0 - base - pos1
    swapped = jnp.minimum(shift * shift, 1)
    place = (1 - away0, jnp.minimum(away0 + 2 * away2, 2), 2 - 2 * away2)

    def pair(ref):
        return jnp.concatenate([ref[pos1], ref[pos2]], axis=0)

    a_rows, b_rows = pl.ds(0, BLOCK), pl.ds(BLOCK, 2 * BLOCK)

    def exchange(step):
        return pltpu.make_async_remote_copy(
            src_ref=give_ref.at[step],
            dst_ref=take_ref.at[step],
            send_sem=give_sem.at[step],
            recv_sem=take_sem.at[step],
            device_id=(1 - x, b),
            device_id_type=MESH,
        )

    def local_reverse(v, step):
        sent_ref[step] = v.astype(BF16).reshape(2, BLOCK, width)
        other = jnp.concatenate(
            [sent_ref[step, swapped], sent_ref[step, 1 - swapped]], axis=0
        )
        return flip(other.astype(F32))

    def half_copy(layer):
        return pltpu.make_async_remote_copy(
            src_ref=half_ref.at[layer],
            dst_ref=half_in_ref.at[layer],
            send_sem=half_sem.at[layer],
            recv_sem=half_in_sem.at[layer],
            device_id=(x, b + 1 - 2 * core),
            device_id_type=MESH,
        )

    half_rows = width // 2
    eighth = half_rows // 8

    def send_half(layer):
        def columns(c):
            return n_ref[layer, :, pl.ds(pl.multiple_of(c * half_rows, half_rows), half_rows)]

        d = d_ref[layer]
        half_ref[layer] = dot(columns(1 - core), d, 0, 0).astype(BF16)
        half_copy(layer).start()
        own_ref[layer] = dot(columns(core), d, 0, 0)

    def sides(layer, piece):
        return (x, y) if piece == 1 and layer < 2 else (y, x)

    def part_copy(layer, piece, hop):
        along_x = (piece == 1 and layer < 2) == (hop == 0)
        near, far = sides(layer, piece)
        if hop == 0:
            src, dst = part_ref.at[layer, piece, 1 - near], part_in_ref.at[layer, piece]
        else:
            src, dst = quad_ref.at[layer, piece, 1 - far], quad_in_ref.at[layer, piece]
        return pltpu.make_async_remote_copy(
            src_ref=src,
            dst_ref=dst,
            send_sem=part_sem.at[layer, piece, hop],
            recv_sem=part_in_sem.at[layer, piece, hop],
            device_id=(1 - x, b) if along_x else (x, b + 2 - 4 * y),
            device_id_type=MESH,
        )

    def send_parts(layer):
        half_copy(layer).wait_recv()
        total = own_ref[layer] + half_in_ref[layer].astype(F32)
        part_ref[layer] = total.astype(BF16).reshape(2, 2, 2, eighth, width)
        for piece in range(2):
            part_copy(layer, piece, 0).start()

    def send_quads(layer):
        for piece in range(2):
            part_copy(layer, piece, 0).wait_recv()
            near, _ = sides(layer, piece)
            total = part_ref[layer, piece, near].astype(F32)
            total = total + part_in_ref[layer, piece].astype(F32)
            quad_ref[layer, piece] = total.astype(BF16)
            part_copy(layer, piece, 1).start()

    def piece_copy(layer, hop):
        plane = (z + hop) % 4
        return pltpu.make_async_remote_copy(
            src_ref=piece_ref.at[layer, plane],
            dst_ref=piece_in_ref.at[layer, hop - 1],
            send_sem=piece_sem.at[layer, hop - 1],
            recv_sem=piece_in_sem.at[layer, hop - 1],
            device_id=(x, (b + 4 * hop) % n_blk),
            device_id_type=MESH,
        )

    def send_pieces(layer):
        for piece in range(2):
            part_copy(layer, piece, 1).wait_recv()
            _, far = sides(layer, piece)
            total = quad_ref[layer, piece, far].astype(F32)
            total = total + quad_in_ref[layer, piece].astype(F32)
            piece_ref[layer, pl.ds(2 * piece, 2)] = total.astype(BF16).reshape(2, CHUNK, width)
        for hop in (2, 1, 3):
            piece_copy(layer, hop).start()

    def chunk_copy(layer):
        piece = z // 2
        x_first = piece if layer < 2 else 0
        near = y + x_first * (x - y)
        far = x + x_first * (y - x)
        c = 32 * layer + 16 * core + 8 * piece + 4 * near + 2 * far + z % 2
        dest = c // 3
        copy = pltpu.make_async_remote_copy(
            src_ref=chunk_ref.at[layer],
            dst_ref=final_ref.at[c % 3],
            send_sem=chunk_sem.at[layer],
            recv_sem=final_sem.at[c % 3],
            device_id=(dest // n_blk, dest % n_blk),
            device_id_type=MESH,
        )
        return c, dest, copy

    def send_chunk(layer):
        total = piece_ref[layer, z].astype(F32)
        for hop in (1, 2, 3):
            piece_copy(layer, hop).wait_recv()
            total = total + piece_in_ref[layer, hop - 1].astype(F32)
        chunk_ref[layer] = total.astype(BF16)
        c, dest, copy = chunk_copy(layer)

        @pl.when(dest != me)
        def _():
            copy.start()

        @pl.when(dest == me)
        def _():
            final_ref[c % 3] = chunk_ref[layer]

    loads[1].wait()
    loads[2].wait()
    mix_a = mixing_matrix(basis_ref[...], (first_pos,))
    mixed_a = dot(mix_a, state_ref[first_pos])
    loads[3].wait()
    first_a, saved_a1 = forward(mixed_a, w_ref, 0, n_ref, a_rows)
    loads[4].wait()
    second_a, saved_a2 = forward(first_a, w_ref, 1, n_ref, a_rows)
    give_ref[0] = second_a.astype(BF16)
    pl.semaphore_wait(barrier, count - 1)
    exchange(0).start()

    mix_b = mixing_matrix(basis_ref[...], (pos1, pos2))
    mixed_b = dot(mix_b, pair(state_ref))
    first_b, saved_b1 = forward(mixed_b, w_ref, 0, n_ref, b_rows)
    second_b, saved_b2 = forward(first_b, w_ref, 1, n_ref, b_rows)
    summed_b = second_b + local_reverse(second_b, 0)
    loads[5].wait()
    final_b, saved_b3 = forward(summed_b, w_ref, 2, n_ref, b_rows)
    eout_ref[pl.ds(1, 2)] = final_b.astype(BF16).reshape(2, BLOCK, width)

    exchange(0).wait_recv()
    summed_a = second_a + flip(take_ref[0].astype(F32))
    final_a, saved_a3 = forward(summed_a, w_ref, 2, n_ref, a_rows)
    eout_ref[0] = final_a.astype(BF16)
    loads[6].wait()
    gs_a = backward(
        summed_a, saved_a3, w_ref, 2, cot_ref[first_pos].astype(F32), d_ref, a_rows
    )
    give_ref[1] = gs_a.astype(BF16)
    exchange(1).start()

    gs_b = backward(summed_b, saved_b3, w_ref, 2, pair(cot_ref).astype(F32), d_ref, b_rows)
    send_half(2)
    gsec_b = gs_b + local_reverse(gs_b, 1)
    gf_b = backward(first_b, saved_b2, w_ref, 1, gsec_b, d_ref, b_rows)
    send_parts(2)
    gm_b = backward(mixed_b, saved_b1, w_ref, 0, gf_b, d_ref, b_rows)
    gout_ref[pl.ds(1, 2)] = dot(mix_b, gm_b.astype(BF16), 0, 0).astype(BF16).reshape(
        2, BLOCK, width
    )

    exchange(1).wait_recv()
    gsec_a = gs_a + flip(take_ref[1].astype(F32))
    gf_a = backward(first_a, saved_a2, w_ref, 1, gsec_a, d_ref, a_rows)
    send_half(1)
    send_quads(2)
    gm_a = backward(mixed_a, saved_a1, w_ref, 0, gf_a, d_ref, a_rows)
    send_half(0)
    send_parts(1)
    send_pieces(2)
    send_parts(0)
    gout_ref[0] = dot(mix_a, gm_a.astype(BF16), 0, 0).astype(BF16)
    send_quads(1)
    send_quads(0)
    send_chunk(2)

    for k in range(3):
        out_ref[k] = eout_ref[place[k]]
        gstate_ref[k] = gout_ref[place[k]]

    send_pieces(1)
    send_pieces(0)
    send_chunk(1)
    send_chunk(0)

    for j in range(3):
        c = 3 * me + j
        i = c % 32
        layer = c // 32
        piece = (i // 8) % 2
        near, far = (i // 4) % 2, (i // 2) % 2
        x_first = piece * (1 - layer // 2)
        from_y = near + x_first * (far - near)
        from_x = far + x_first * (near - far)
        source = from_x * n_blk + 4 * (2 * piece + i % 2) + 2 * from_y + i // 16

        @pl.when(source != me)
        def _():
            pltpu.make_async_remote_copy(
                src_ref=chunk_ref.at[0],
                dst_ref=final_ref.at[j],
                send_sem=chunk_sem.at[0],
                recv_sem=final_sem.at[j],
                device_id=(1 - x, b),
                device_id_type=MESH,
            ).wait_recv()

        wgrad_ref[j] = final_ref[j]

    for step in range(2):
        exchange(step).wait_send()
    for layer in range(3):
        half_copy(layer).wait_send()
        for piece in range(2):
            for hop in range(2):
                part_copy(layer, piece, hop).wait_send()
        for hop in (1, 2, 3):
            piece_copy(layer, hop).wait_send()
        c, dest, copy = chunk_copy(layer)

        @pl.when(dest != me)
        def _():
            copy.wait_send()


def finish(scale, out_ref, gstate_ref, wgrad_ref, out_hbm, gstate_hbm, total_ref, sems):
    copies = [
        pltpu.make_async_copy(out_ref, out_hbm, sems.at[0]),
        pltpu.make_async_copy(gstate_ref, gstate_hbm, sems.at[1]),
    ]
    for copy in copies:
        copy.start()
    total_ref[...] = wgrad_ref[...].astype(F32) * scale
    for copy in copies:
        copy.wait()


def local_fast(n_blk, edge_state, basis, weights, partner, cotangent):
    rows, width = edge_state.shape
    total_edges = rows * 2 * n_blk
    half = width // 2
    blocks = (rows // BLOCK, BLOCK, width)
    vmem = pl.BlockSpec(memory_space=pltpu.VMEM)
    dma = pltpu.SemaphoreType.DMA
    out, gstate, wgrad = pl.pallas_call(
        functools.partial(kernel, n_blk),
        out_shape=(
            jax.ShapeDtypeStruct(blocks, BF16),
            jax.ShapeDtypeStruct(blocks, BF16),
            jax.ShapeDtypeStruct((3, CHUNK, width), BF16),
        ),
        in_specs=[pl.BlockSpec(memory_space=pltpu.HBM)] * 5,
        out_specs=(vmem, vmem, vmem),
        scratch_shapes=[
            pltpu.SMEM(partner.shape, jnp.int32),
            pltpu.VMEM(blocks, BF16),
            pltpu.VMEM((NBR, NBR, basis.shape[0]), BF16),
            pltpu.VMEM(weights.shape, BF16),
            pltpu.VMEM(blocks, BF16),
            pltpu.VMEM((3, rows, width), BF16),
            pltpu.VMEM((3, rows, width), BF16),
            pltpu.VMEM(blocks, BF16),
            pltpu.VMEM(blocks, BF16),
            pltpu.VMEM((2, 2, BLOCK, width), BF16),
            pltpu.VMEM((2, BLOCK, width), BF16),
            pltpu.VMEM((2, BLOCK, width), BF16),
            pltpu.VMEM((3, half, width), BF16),
            pltpu.VMEM((3, half, width), F32),
            pltpu.VMEM((3, half, width), BF16),
            pltpu.VMEM((3, 2, 2, 2, half // 8, width), BF16),
            pltpu.VMEM((3, 2, 2, half // 8, width), BF16),
            pltpu.VMEM((3, 2, 2, half // 8, width), BF16),
            pltpu.VMEM((3, 2, half // 8, width), BF16),
            pltpu.VMEM((3, 4, CHUNK, width), BF16),
            pltpu.VMEM((3, 3, CHUNK, width), BF16),
            pltpu.VMEM((3, CHUNK, width), BF16),
            pltpu.VMEM((3, CHUNK, width), BF16),
            dma((7,)),
            dma((2,)),
            dma((2,)),
            dma((3,)),
            dma((3,)),
            dma((3, 2, 2)),
            dma((3, 2, 2)),
            dma((3, 3)),
            dma((3, 3)),
            dma((3,)),
            dma((3,)),
        ],
        compiler_params=pltpu.CompilerParams(
            collective_id=0, has_side_effects=True, vmem_limit_bytes=36 * 2**20
        ),
    )(
        *[
            pltpu.with_memory_space_constraint(array, pltpu.HBM)
            for array in (
                partner,
                edge_state.reshape(blocks),
                basis.transpose(1, 2, 0),
                weights,
                cotangent.reshape(blocks),
            )
        ]
    )
    hbm = pl.BlockSpec(memory_space=pltpu.HBM)
    out, gstate, wgrad = pl.pallas_call(
        functools.partial(finish, 1.0 / math.sqrt(total_edges)),
        out_shape=(
            jax.ShapeDtypeStruct(blocks, BF16),
            jax.ShapeDtypeStruct(blocks, BF16),
            jax.ShapeDtypeStruct((3, CHUNK, width), F32),
        ),
        in_specs=[vmem, vmem, vmem],
        out_specs=(hbm, hbm, vmem),
        scratch_shapes=[dma((2,))],
        compiler_params=pltpu.CompilerParams(vmem_limit_bytes=8 * 2**20),
    )(out, gstate, wgrad)
    return (
        out.reshape(rows, width),
        gstate.reshape(rows, width),
        wgrad.reshape(3 * CHUNK, width),
    )


def norm_rows(hidden):
    return hidden * lax.rsqrt(jnp.mean(hidden * hidden, axis=-1, keepdims=True) + 1e-06)


def layer_forward(hidden, weight):
    normed = norm_rows(hidden).astype(jnp.bfloat16)
    preact = jnp.dot(normed, weight, preferred_element_type=jnp.float32)
    return (hidden + jax.nn.silu(preact), normed, preact)


def layer_backward(hidden, normed, preact, weight, upstream):
    sigma = jax.nn.sigmoid(preact)
    grad_pre = (upstream * sigma * (1.0 + preact * (1.0 - sigma))).astype(jnp.bfloat16)
    grad_weight = lax.dot_general(
        normed, grad_pre, (((0,), (0,)), ((), ())), preferred_element_type=jnp.float32
    )
    grad_normed = lax.dot_general(
        grad_pre, weight, (((1,), (1,)), ((), ())), preferred_element_type=jnp.float32
    )
    inverse = lax.rsqrt(jnp.mean(hidden * hidden, axis=-1, keepdims=True) + 1e-06)
    unit = hidden * inverse
    inner = jnp.mean(grad_normed * unit, axis=-1, keepdims=True)
    return (upstream + inverse * (grad_normed - unit * inner), grad_weight)


def flip_rows(blocks):
    count, height, width = blocks.shape
    return blocks.reshape(count, height // 2, 2, width)[:, :, ::-1, :].reshape(count, height, width)


def route_plan(partner, own_index, group_count):
    block_count = partner.shape[0]
    target = partner // block_count
    remote = partner % block_count
    order = jnp.arange(block_count)
    same = target[:, None] == target[None, :]
    send_rank = jnp.sum(same & (order[None, :] < order[:, None]), axis=1)
    recv_rank = jnp.sum(same & (remote[None, :] < remote[:, None]), axis=1)
    local_pair = target == own_index
    slots = jnp.arange(group_count * CAP)
    send_slot = target * CAP + send_rank
    recv_slot = target * CAP + recv_rank
    pack_matrix = ((slots[:, None] == send_slot[None, :]) & ~local_pair[None, :]).astype(
        jnp.bfloat16
    )
    unpack_matrix = ((recv_slot[:, None] == slots[None, :]) & ~local_pair[:, None]).astype(
        jnp.bfloat16
    )
    return (pack_matrix, unpack_matrix, local_pair)


def pack_blocks(values, pack_matrix, block_count):
    blocks = values.reshape(block_count, -1, values.shape[1])
    return jnp.einsum("sn,nrd->srd", pack_matrix, blocks, preferred_element_type=jnp.bfloat16)


def unpack_blocks(arrived, unpack_matrix, local_pair, values, block_count):
    blocks = values.reshape(block_count, -1, values.shape[1])
    distant = jnp.einsum("ns,srd->nrd", unpack_matrix, arrived, preferred_element_type=jnp.bfloat16)
    joined = jnp.where(local_pair[:, None, None], blocks, distant)
    return flip_rows(joined).reshape(values.shape)


def local(edge_state, basis, weights, partner, cotangent):
    row_count, width = edge_state.shape
    block_count = partner.shape[0]
    group_count = lax.axis_size("grp")
    own_index = lax.axis_index("grp")
    total_edges = row_count * group_count * lax.axis_size("blk")
    pack_matrix, unpack_matrix, local_pair = route_plan(partner, own_index, group_count)
    mixed = jnp.einsum(
        "aij,ajd->aid",
        basis,
        edge_state.reshape(-1, NBR, width),
        preferred_element_type=jnp.float32,
    ).reshape(row_count, width)
    first, normed_one, pre_one = layer_forward(mixed, weights[0])
    second, normed_two, pre_two = layer_forward(first, weights[1])
    sent = second.astype(jnp.bfloat16)
    arrived = lax.all_to_all(
        pack_blocks(sent, pack_matrix, block_count), "grp", split_axis=0, concat_axis=0, tiled=True
    )
    reversed_state = unpack_blocks(arrived, unpack_matrix, local_pair, sent, block_count)
    summed = second + reversed_state.astype(jnp.float32)
    final, normed_three, pre_three = layer_forward(summed, weights[2])
    edge_out = final.astype(jnp.bfloat16)
    grad_summed, grad_three = layer_backward(
        summed, normed_three, pre_three, weights[2], cotangent.astype(jnp.float32)
    )
    grad_reversed = grad_summed.astype(jnp.bfloat16)
    returned = lax.all_to_all(
        pack_blocks(grad_reversed, pack_matrix, block_count),
        "grp",
        split_axis=0,
        concat_axis=0,
        tiled=True,
    )
    grad_sent = unpack_blocks(returned, unpack_matrix, local_pair, grad_reversed, block_count)
    grad_second = grad_summed + grad_sent.astype(jnp.float32)
    grad_first, grad_two = layer_backward(first, normed_two, pre_two, weights[1], grad_second)
    grad_mixed, grad_one = layer_backward(mixed, normed_one, pre_one, weights[0], grad_first)
    grad_round = grad_mixed.astype(jnp.bfloat16).reshape(-1, NBR, width)
    grad_state = (
        jnp.einsum("aij,aid->ajd", basis, grad_round, preferred_element_type=jnp.float32)
        .reshape(row_count, width)
        .astype(jnp.bfloat16)
    )
    local_grads = jnp.concatenate([grad_one, grad_two, grad_three], axis=0)
    group_part = lax.psum_scatter(
        local_grads.astype(jnp.bfloat16), "grp", scatter_dimension=0, tiled=True
    ).astype(jnp.float32)
    summed_grads = lax.psum_scatter(group_part, "blk", scatter_dimension=0, tiled=True)
    weight_grad = summed_grads * (1.0 / math.sqrt(total_edges))
    return (edge_out, grad_state, weight_grad)


def solution(mesh):
    spread = P(("grp", "blk"))
    wide = P(("grp", "blk"), None)
    in_specs = (wide, P(("grp", "blk"), None, None), P(), spread, wide)
    body = local
    if mesh.shape["grp"] == 2 and mesh.shape["blk"] == 16:
        body = functools.partial(local_fast, mesh.shape["blk"])
    return jax.shard_map(
        body, mesh=mesh, in_specs=in_specs, out_specs=(wide, wide, wide), check_vma=False
    )
```

```python
import functools
import math

import jax
import jax.numpy as jnp
from jax import lax
from jax.experimental import pallas as pl
from jax.experimental.pallas import tpu as pltpu
from jax.sharding import PartitionSpec as P

NBR = 16
CAP = 1
BLOCK = 128
CHUNK = 16
EPS = 1e-06
MESH = pl.DeviceIdType.MESH
BF16 = jnp.bfloat16
F32 = jnp.float32


def dot(a, b, ca=1, cb=0):
    return lax.dot_general(a, b, (((ca,), (cb,)), ((), ())), preferred_element_type=F32)


def inverse_rms(h):
    return lax.rsqrt(jnp.mean(h * h, axis=-1, keepdims=True) + EPS)


def flip(x):
    rows = x.shape[0]
    even = lax.broadcasted_iota(jnp.int32, x.shape, 0) % 2 == 0
    return jnp.where(even, pltpu.roll(x, rows - 1, 0), pltpu.roll(x, 1, 0))


def mixing_matrix(basis, block):
    flat = basis.reshape(NBR * NBR, basis.shape[2])
    rows = BLOCK

    def iota(shape, dim):
        return lax.broadcasted_iota(jnp.int32, shape, dim)

    def mask(hit):
        return hit.astype(F32).astype(BF16)

    atom_shape = (rows, basis.shape[2])
    atom = block * (BLOCK // NBR) + iota(atom_shape, 0) // NBR
    pick = mask(atom == iota(atom_shape, 1))
    own = dot(pick, flat, 1, 1)
    own_shape = (rows, NBR * NBR)
    own = jnp.where(iota(own_shape, 0) % NBR == iota(own_shape, 1) // NBR, own, 0.0).astype(BF16)
    spread_shape = (NBR * NBR, rows)
    spread = mask(iota(spread_shape, 0) % NBR == iota(spread_shape, 1) % NBR)
    wide = dot(own, spread)
    same = iota((rows, rows), 0) // NBR == iota((rows, rows), 1) // NBR
    return jnp.where(same, wide, 0.0).astype(BF16)


def forward(h, w_ref, layer, p, saved):
    n_ref, _, inv_ref, slope_ref = saved
    inv = inverse_rms(h)
    normed = (h * inv).astype(BF16)
    n_ref[layer, pl.ds(p * BLOCK, BLOCK), :] = normed
    inv_ref[layer, p] = inv
    pre = dot(normed, w_ref[layer])
    s = 0.5 * jnp.tanh(0.5 * pre) + 0.5
    slope_ref[layer, p] = s * (1.0 + pre * (1.0 - s))
    return h + pre * s


def backward(h, w_ref, layer, p, saved, g):
    _, d_ref, inv_ref, slope_ref = saved
    inv = inv_ref[layer, p]
    dpre = (g * slope_ref[layer, p]).astype(BF16)
    d_ref[layer, pl.ds(p * BLOCK, BLOCK), :] = dpre
    dn = dot(dpre, w_ref[layer], 1, 1)
    u = h * inv
    inner = jnp.mean(dn * u, axis=-1, keepdims=True)
    return g + inv * (dn - u * inner)


def kernel(
    n_blk,
    partner_hbm,
    state_hbm,
    basis_hbm,
    w_hbm,
    cot_hbm,
    out_ref,
    gstate_ref,
    wgrad_ref,
    partner_ref,
    state_ref,
    basis_ref,
    w_ref,
    cot_ref,
    n_ref,
    d_ref,
    eout_ref,
    gout_ref,
    sent_ref,
    rev_ref,
    mix_ref,
    mixed_ref,
    first_ref,
    second_ref,
    gs_ref,
    inv_ref,
    slope_ref,
    pos_ref,
    pair_ref,
    take_ref,
    half_ref,
    own_ref,
    half_in_ref,
    part_ref,
    part_in_ref,
    quad_ref,
    quad_in_ref,
    piece_ref,
    final_ref,
    in_sem,
    give_sem,
    take_sem,
    half_sem,
    half_in_sem,
    part_sem,
    part_in_sem,
    piece_sem,
    final_sem,
):
    x = lax.axis_index("grp")
    b = lax.axis_index("blk")
    me = x * n_blk + b
    core = b % 2
    y = (b // 2) % 2
    z = b // 4
    count = 2 * n_blk
    width = w_ref.shape[2]

    loads = [
        pltpu.make_async_copy(src, dst, in_sem.at[number])
        for number, (src, dst) in enumerate(
            [
                (partner_hbm, partner_ref),
                (basis_hbm, basis_ref),
                (state_hbm, state_ref),
                (w_hbm.at[0], w_ref.at[0]),
                (w_hbm.at[1], w_ref.at[1]),
                (w_hbm.at[2], w_ref.at[2]),
                (cot_hbm, cot_ref),
            ]
        )
    ]
    for load in loads:
        load.start()

    barrier = pltpu.get_barrier_semaphore()

    def greet(step, carry):
        other = (me + step) % count
        pl.semaphore_signal(
            barrier, inc=1, device_id=(other // n_blk, other % n_blk), device_id_type=MESH
        )
        return carry

    lax.fori_loop(1, count, greet, 0)

    base = x * 3
    loads[0].wait()
    p0, p1, p2 = partner_ref[0], partner_ref[1], partner_ref[2]
    sides = [jnp.minimum(jnp.maximum(p - 2, 0), 1) - x for p in (p0, p1, p2)]
    away0, away1, away2 = (side * side for side in sides)
    first_pos = jnp.minimum(away1 + 2 * away2, 2)
    pos1 = away0
    pos2 = 2 - away2
    shift = away0 * p1 + (1 - away0) * p0 - base - pos1
    swapped = jnp.minimum(shift * shift, 1)
    place = (1 - away0, jnp.minimum(away0 + 2 * away2, 2), 2 - 2 * away2)

    for p, value in enumerate((first_pos, pos1, pos2)):
        pos_ref[p] = value
    for p, value in enumerate((0, 1 + swapped, 2 - swapped)):
        pair_ref[p] = value
    saved = (n_ref, d_ref, inv_ref, slope_ref)

    def exchange(step):
        return pltpu.make_async_remote_copy(
            src_ref=sent_ref.at[step, 0],
            dst_ref=take_ref.at[step],
            send_sem=give_sem.at[step],
            recv_sem=take_sem.at[step],
            device_id=(1 - x, b),
            device_id_type=MESH,
        )

    def half_copy(layer):
        return pltpu.make_async_remote_copy(
            src_ref=half_ref.at[layer],
            dst_ref=half_in_ref.at[layer],
            send_sem=half_sem.at[layer],
            recv_sem=half_in_sem.at[layer],
            device_id=(x, b + 1 - 2 * core),
            device_id_type=MESH,
        )

    half_rows = width // 2
    eighth = half_rows // 8

    def send_half(layer):
        def columns(c):
            return n_ref[layer, :, pl.ds(pl.multiple_of(c * half_rows, half_rows), half_rows)]

        d = d_ref[layer]
        half_ref[layer] = dot(columns(1 - core), d, 0, 0).astype(BF16)
        half_copy(layer).start()
        own_ref[layer] = dot(columns(core), d, 0, 0)

    def sides(layer, piece):
        return (x, y) if piece == 1 and layer < 2 else (y, x)

    def part_copy(layer, piece, hop):
        along_x = (piece == 1 and layer < 2) == (hop == 0)
        near, far = sides(layer, piece)
        if hop == 0:
            src, dst = part_ref.at[layer, piece, 1 - near], part_in_ref.at[layer, piece]
        else:
            src, dst = quad_ref.at[layer, piece, 1 - far], quad_in_ref.at[layer, piece]
        return pltpu.make_async_remote_copy(
            src_ref=src,
            dst_ref=dst,
            send_sem=part_sem.at[layer, piece, hop],
            recv_sem=part_in_sem.at[layer, piece, hop],
            device_id=(1 - x, b) if along_x else (x, b + 2 - 4 * y),
            device_id_type=MESH,
        )

    def send_parts(layer):
        half_copy(layer).wait_recv()
        total = own_ref[layer] + half_in_ref[layer].astype(F32)
        part_ref[layer] = total.astype(BF16).reshape(2, 2, 2, eighth, width)
        for piece in range(2):
            part_copy(layer, piece, 0).start()

    def send_quads(layer):
        for piece in range(2):
            part_copy(layer, piece, 0).wait_recv()
            near, _ = sides(layer, piece)
            total = part_ref[layer, piece, near].astype(F32)
            total = total + part_in_ref[layer, piece].astype(F32)
            quad_ref[layer, piece] = total.astype(BF16)
            part_copy(layer, piece, 1).start()

    def piece_copy(layer, t):
        near, far = sides(layer, t // 2)
        c = 32 * layer + 16 * core + 8 * (t // 2) + 4 * near + 2 * far + t % 2
        dest = c // 3
        copy = pltpu.make_async_remote_copy(
            src_ref=piece_ref.at[layer, t],
            dst_ref=final_ref.at[c % 3, z],
            send_sem=piece_sem.at[layer, t],
            recv_sem=final_sem.at[c % 3, z],
            device_id=(dest // n_blk, dest % n_blk),
            device_id_type=MESH,
        )
        return c, dest, copy

    def send_pieces(layer):
        for piece in range(2):
            part_copy(layer, piece, 1).wait_recv()
            _, far = sides(layer, piece)
            total = quad_ref[layer, piece, far].astype(F32)
            total = total + quad_in_ref[layer, piece].astype(F32)
            piece_ref[layer, pl.ds(2 * piece, 2)] = total.astype(BF16).reshape(2, CHUNK, width)
        for t in range(4):
            c, dest, copy = piece_copy(layer, t)

            @pl.when(dest != me)
            def _():
                copy.start()

            @pl.when(dest == me)
            def _():
                final_ref[c % 3, z] = piece_ref[layer, t]

    def phase_one(p, carry):
        mix = mixing_matrix(basis_ref[...], pos_ref[p])
        mix_ref[p] = mix
        mixed = dot(mix, state_ref[pos_ref[p]])
        mixed_ref[p] = mixed
        first = forward(mixed, w_ref, 0, p, saved)
        first_ref[p] = first
        second = forward(first, w_ref, 1, p, saved)
        second_ref[p] = second
        sent_ref[0, p] = second.astype(BF16)

        @pl.when(p == 0)
        def _():
            pl.semaphore_wait(barrier, count - 1)
            exchange(0).start()

        return carry

    def reverse(step, p):
        @pl.when(p == 0)
        def _():
            exchange(step).wait_recv()
            rev_ref[...] = take_ref[step]

        @pl.when(p > 0)
        def _():
            rev_ref[...] = sent_ref[step, pair_ref[p]]

        return flip(rev_ref[...].astype(F32))

    def phase_two(i, carry):
        p = 1 - i + 3 * (i // 2)
        summed = second_ref[p] + reverse(0, p)
        final = forward(summed, w_ref, 2, p, saved)
        eout_ref[p] = final.astype(BF16)
        g = backward(summed, w_ref, 2, p, saved, cot_ref[pos_ref[p]].astype(F32))
        gs_ref[p] = g
        sent_ref[1, p] = g.astype(BF16)

        @pl.when(p == 0)
        def _():
            exchange(1).start()

        return carry

    def phase_three(i, carry):
        p = (i + 1) % 3
        g = gs_ref[p] + reverse(1, p)
        g = backward(first_ref[p], w_ref, 1, p, saved, g)
        g = backward(mixed_ref[p], w_ref, 0, p, saved, g)
        gout_ref[p] = dot(mix_ref[p], g.astype(BF16), 0, 0).astype(BF16)

        @pl.when(p == 2)
        def _():
            send_parts(2)

        return carry

    for load in loads[1:5]:
        load.wait()
    lax.fori_loop(0, 3, phase_one, 0)
    for load in loads[5:]:
        load.wait()
    lax.fori_loop(0, 3, phase_two, 0)
    send_half(2)
    lax.fori_loop(0, 3, phase_three, 0)
    lax.fori_loop(0, 2, lambda i, carry: (send_half(1 - i), carry)[1], 0)
    send_quads(2)
    send_parts(1)
    send_parts(0)
    send_pieces(2)
    send_quads(1)
    send_quads(0)

    for k in range(3):
        out_ref[k] = eout_ref[place[k]]
        gstate_ref[k] = gout_ref[place[k]]

    send_pieces(1)
    send_pieces(0)

    for j in range(3):
        c = 3 * me + j
        i = c % 32
        near, far = (i // 4) % 2, (i // 2) % 2
        x_first = ((i // 8) % 2) * (1 - c // 64)
        from_y = near + x_first * (far - near)
        from_x = far + x_first * (near - far)
        for plane in range(4):
            source = from_x * n_blk + 4 * plane + 2 * from_y + i // 16

            @pl.when(source != me)
            def _():
                pltpu.make_async_remote_copy(
                    src_ref=piece_ref.at[0, 0],
                    dst_ref=final_ref.at[j, plane],
                    send_sem=piece_sem.at[0, 0],
                    recv_sem=final_sem.at[j, plane],
                    device_id=(1 - x, b),
                    device_id_type=MESH,
                ).wait_recv()

    for j in range(3):
        total = final_ref[j, 0].astype(F32)
        for plane in range(1, 4):
            total = total + final_ref[j, plane].astype(F32)
        wgrad_ref[j] = total

    for step in range(2):
        exchange(step).wait_send()
    for layer in range(3):
        half_copy(layer).wait_send()
        for piece in range(2):
            for hop in range(2):
                part_copy(layer, piece, hop).wait_send()
        for t in range(4):
            c, dest, copy = piece_copy(layer, t)

            @pl.when(dest != me)
            def _():
                copy.wait_send()


def finish(scale, out_ref, gstate_ref, wgrad_ref, out_hbm, gstate_hbm, total_ref, sems):
    copies = [
        pltpu.make_async_copy(out_ref, out_hbm, sems.at[0]),
        pltpu.make_async_copy(gstate_ref, gstate_hbm, sems.at[1]),
    ]
    for copy in copies:
        copy.start()
    total_ref[...] = wgrad_ref[...] * scale
    for copy in copies:
        copy.wait()


def local_fast(n_blk, edge_state, basis, weights, partner, cotangent):
    rows, width = edge_state.shape
    total_edges = rows * 2 * n_blk
    half = width // 2
    blocks = (rows // BLOCK, BLOCK, width)
    vmem = pl.BlockSpec(memory_space=pltpu.VMEM)
    dma = pltpu.SemaphoreType.DMA
    out, gstate, wgrad = pl.pallas_call(
        functools.partial(kernel, n_blk),
        out_shape=(
            jax.ShapeDtypeStruct(blocks, BF16),
            jax.ShapeDtypeStruct(blocks, BF16),
            jax.ShapeDtypeStruct((3, CHUNK, width), F32),
        ),
        in_specs=[pl.BlockSpec(memory_space=pltpu.HBM)] * 5,
        out_specs=(vmem, vmem, vmem),
        scratch_shapes=[
            pltpu.SMEM(partner.shape, jnp.int32),
            pltpu.VMEM(blocks, BF16),
            pltpu.VMEM((NBR, NBR, basis.shape[0]), BF16),
            pltpu.VMEM(weights.shape, BF16),
            pltpu.VMEM(blocks, BF16),
            pltpu.VMEM((3, rows, width), BF16),
            pltpu.VMEM((3, rows, width), BF16),
            pltpu.VMEM(blocks, BF16),
            pltpu.VMEM(blocks, BF16),
            pltpu.VMEM((2, 3, BLOCK, width), BF16),
            pltpu.VMEM((BLOCK, width), BF16),
            pltpu.VMEM((3, BLOCK, BLOCK), BF16),
            pltpu.VMEM(blocks, F32),
            pltpu.VMEM(blocks, F32),
            pltpu.VMEM(blocks, F32),
            pltpu.VMEM(blocks, F32),
            pltpu.VMEM((3, 3, BLOCK, 1), F32),
            pltpu.VMEM((3, 3, BLOCK, width), F32),
            pltpu.SMEM((3,), jnp.int32),
            pltpu.SMEM((3,), jnp.int32),
            pltpu.VMEM((2, BLOCK, width), BF16),
            pltpu.VMEM((3, half, width), BF16),
            pltpu.VMEM((3, half, width), F32),
            pltpu.VMEM((3, half, width), BF16),
            pltpu.VMEM((3, 2, 2, 2, half // 8, width), BF16),
            pltpu.VMEM((3, 2, 2, half // 8, width), BF16),
            pltpu.VMEM((3, 2, 2, half // 8, width), BF16),
            pltpu.VMEM((3, 2, half // 8, width), BF16),
            pltpu.VMEM((3, 4, CHUNK, width), BF16),
            pltpu.VMEM((3, 4, CHUNK, width), BF16),
            dma((7,)),
            dma((2,)),
            dma((2,)),
            dma((3,)),
            dma((3,)),
            dma((3, 2, 2)),
            dma((3, 2, 2)),
            dma((3, 4)),
            dma((3, 4)),
        ],
        compiler_params=pltpu.CompilerParams(
            collective_id=0, has_side_effects=True, vmem_limit_bytes=36 * 2**20
        ),
    )(
        *[
            pltpu.with_memory_space_constraint(array, pltpu.HBM)
            for array in (
                partner,
                edge_state.reshape(blocks),
                basis.transpose(1, 2, 0),
                weights,
                cotangent.reshape(blocks),
            )
        ]
    )
    hbm = pl.BlockSpec(memory_space=pltpu.HBM)
    out, gstate, wgrad = pl.pallas_call(
        functools.partial(finish, 1.0 / math.sqrt(total_edges)),
        out_shape=(
            jax.ShapeDtypeStruct(blocks, BF16),
            jax.ShapeDtypeStruct(blocks, BF16),
            jax.ShapeDtypeStruct((3, CHUNK, width), F32),
        ),
        in_specs=[vmem, vmem, vmem],
        out_specs=(hbm, hbm, vmem),
        scratch_shapes=[dma((2,))],
        compiler_params=pltpu.CompilerParams(vmem_limit_bytes=8 * 2**20),
    )(out, gstate, wgrad)
    return (
        out.reshape(rows, width),
        gstate.reshape(rows, width),
        wgrad.reshape(3 * CHUNK, width),
    )


def norm_rows(hidden):
    return hidden * lax.rsqrt(jnp.mean(hidden * hidden, axis=-1, keepdims=True) + 1e-06)


def layer_forward(hidden, weight):
    normed = norm_rows(hidden).astype(jnp.bfloat16)
    preact = jnp.dot(normed, weight, preferred_element_type=jnp.float32)
    return (hidden + jax.nn.silu(preact), normed, preact)


def layer_backward(hidden, normed, preact, weight, upstream):
    sigma = jax.nn.sigmoid(preact)
    grad_pre = (upstream * sigma * (1.0 + preact * (1.0 - sigma))).astype(jnp.bfloat16)
    grad_weight = lax.dot_general(
        normed, grad_pre, (((0,), (0,)), ((), ())), preferred_element_type=jnp.float32
    )
    grad_normed = lax.dot_general(
        grad_pre, weight, (((1,), (1,)), ((), ())), preferred_element_type=jnp.float32
    )
    inverse = lax.rsqrt(jnp.mean(hidden * hidden, axis=-1, keepdims=True) + 1e-06)
    unit = hidden * inverse
    inner = jnp.mean(grad_normed * unit, axis=-1, keepdims=True)
    return (upstream + inverse * (grad_normed - unit * inner), grad_weight)


def flip_rows(blocks):
    count, height, width = blocks.shape
    return blocks.reshape(count, height // 2, 2, width)[:, :, ::-1, :].reshape(count, height, width)


def route_plan(partner, own_index, group_count):
    block_count = partner.shape[0]
    target = partner // block_count
    remote = partner % block_count
    order = jnp.arange(block_count)
    same = target[:, None] == target[None, :]
    send_rank = jnp.sum(same & (order[None, :] < order[:, None]), axis=1)
    recv_rank = jnp.sum(same & (remote[None, :] < remote[:, None]), axis=1)
    local_pair = target == own_index
    slots = jnp.arange(group_count * CAP)
    send_slot = target * CAP + send_rank
    recv_slot = target * CAP + recv_rank
    pack_matrix = ((slots[:, None] == send_slot[None, :]) & ~local_pair[None, :]).astype(
        jnp.bfloat16
    )
    unpack_matrix = ((recv_slot[:, None] == slots[None, :]) & ~local_pair[:, None]).astype(
        jnp.bfloat16
    )
    return (pack_matrix, unpack_matrix, local_pair)


def pack_blocks(values, pack_matrix, block_count):
    blocks = values.reshape(block_count, -1, values.shape[1])
    return jnp.einsum("sn,nrd->srd", pack_matrix, blocks, preferred_element_type=jnp.bfloat16)


def unpack_blocks(arrived, unpack_matrix, local_pair, values, block_count):
    blocks = values.reshape(block_count, -1, values.shape[1])
    distant = jnp.einsum("ns,srd->nrd", unpack_matrix, arrived, preferred_element_type=jnp.bfloat16)
    joined = jnp.where(local_pair[:, None, None], blocks, distant)
    return flip_rows(joined).reshape(values.shape)


def local(edge_state, basis, weights, partner, cotangent):
    row_count, width = edge_state.shape
    block_count = partner.shape[0]
    group_count = lax.axis_size("grp")
    own_index = lax.axis_index("grp")
    total_edges = row_count * group_count * lax.axis_size("blk")
    pack_matrix, unpack_matrix, local_pair = route_plan(partner, own_index, group_count)
    mixed = jnp.einsum(
        "aij,ajd->aid",
        basis,
        edge_state.reshape(-1, NBR, width),
        preferred_element_type=jnp.float32,
    ).reshape(row_count, width)
    first, normed_one, pre_one = layer_forward(mixed, weights[0])
    second, normed_two, pre_two = layer_forward(first, weights[1])
    sent = second.astype(jnp.bfloat16)
    arrived = lax.all_to_all(
        pack_blocks(sent, pack_matrix, block_count), "grp", split_axis=0, concat_axis=0, tiled=True
    )
    reversed_state = unpack_blocks(arrived, unpack_matrix, local_pair, sent, block_count)
    summed = second + reversed_state.astype(jnp.float32)
    final, normed_three, pre_three = layer_forward(summed, weights[2])
    edge_out = final.astype(jnp.bfloat16)
    grad_summed, grad_three = layer_backward(
        summed, normed_three, pre_three, weights[2], cotangent.astype(jnp.float32)
    )
    grad_reversed = grad_summed.astype(jnp.bfloat16)
    returned = lax.all_to_all(
        pack_blocks(grad_reversed, pack_matrix, block_count),
        "grp",
        split_axis=0,
        concat_axis=0,
        tiled=True,
    )
    grad_sent = unpack_blocks(returned, unpack_matrix, local_pair, grad_reversed, block_count)
    grad_second = grad_summed + grad_sent.astype(jnp.float32)
    grad_first, grad_two = layer_backward(first, normed_two, pre_two, weights[1], grad_second)
    grad_mixed, grad_one = layer_backward(mixed, normed_one, pre_one, weights[0], grad_first)
    grad_round = grad_mixed.astype(jnp.bfloat16).reshape(-1, NBR, width)
    grad_state = (
        jnp.einsum("aij,aid->ajd", basis, grad_round, preferred_element_type=jnp.float32)
        .reshape(row_count, width)
        .astype(jnp.bfloat16)
    )
    local_grads = jnp.concatenate([grad_one, grad_two, grad_three], axis=0)
    group_part = lax.psum_scatter(
        local_grads.astype(jnp.bfloat16), "grp", scatter_dimension=0, tiled=True
    ).astype(jnp.float32)
    summed_grads = lax.psum_scatter(group_part, "blk", scatter_dimension=0, tiled=True)
    weight_grad = summed_grads * (1.0 / math.sqrt(total_edges))
    return (edge_out, grad_state, weight_grad)


def solution(mesh):
    spread = P(("grp", "blk"))
    wide = P(("grp", "blk"), None)
    in_specs = (wide, P(("grp", "blk"), None, None), P(), spread, wide)
    body = local
    if mesh.shape["grp"] == 2 and mesh.shape["blk"] == 16:
        body = functools.partial(local_fast, mesh.shape["blk"])
    return jax.shard_map(
        body, mesh=mesh, in_specs=in_specs, out_specs=(wide, wide, wide), check_vma=False
    )
```

```python
import functools
import math

import jax
import jax.numpy as jnp
from jax import lax
from jax.experimental import pallas as pl
from jax.experimental.pallas import tpu as pltpu
from jax.sharding import PartitionSpec as P

NBR = 16
CAP = 1
BLOCK = 128
CHUNK = 16
EPS = 1e-06
MESH = pl.DeviceIdType.MESH
BF16 = jnp.bfloat16
F32 = jnp.float32


def dot(a, b, ca=1, cb=0):
    return lax.dot_general(a, b, (((ca,), (cb,)), ((), ())), preferred_element_type=F32)


def inverse_rms(h):
    return lax.rsqrt(jnp.mean(h * h, axis=-1, keepdims=True) + EPS)


def flip(x):
    rows = x.shape[0]
    even = lax.broadcasted_iota(jnp.int32, x.shape, 0) % 2 == 0
    return jnp.where(even, pltpu.roll(x, rows - 1, 0), pltpu.roll(x, 1, 0))


def mixing_matrix(basis, block):
    flat = basis.reshape(NBR * NBR, basis.shape[2])
    rows = BLOCK

    def iota(shape, dim):
        return lax.broadcasted_iota(jnp.int32, shape, dim)

    def mask(hit):
        return hit.astype(F32).astype(BF16)

    atom_shape = (rows, basis.shape[2])
    atom = block * (BLOCK // NBR) + iota(atom_shape, 0) // NBR
    pick = mask(atom == iota(atom_shape, 1))
    own = dot(pick, flat, 1, 1)
    own_shape = (rows, NBR * NBR)
    own = jnp.where(iota(own_shape, 0) % NBR == iota(own_shape, 1) // NBR, own, 0.0).astype(BF16)
    spread_shape = (NBR * NBR, rows)
    spread = mask(iota(spread_shape, 0) % NBR == iota(spread_shape, 1) % NBR)
    wide = dot(own, spread)
    same = iota((rows, rows), 0) // NBR == iota((rows, rows), 1) // NBR
    return jnp.where(same, wide, 0.0).astype(BF16)


def forward(h, w_ref, layer, p, saved):
    n_ref, _, inv_ref, slope_ref = saved
    inv = inverse_rms(h)
    normed = (h * inv).astype(BF16)
    n_ref[layer, pl.ds(p * BLOCK, BLOCK), :] = normed
    inv_ref[layer, p] = inv
    pre = dot(normed, w_ref[layer])
    s = 0.5 * jnp.tanh(0.5 * pre) + 0.5
    slope_ref[layer, p] = s * (1.0 + pre * (1.0 - s))
    return h + pre * s


def backward(h, w_ref, layer, p, saved, g):
    _, d_ref, inv_ref, slope_ref = saved
    inv = inv_ref[layer, p]
    dpre = (g * slope_ref[layer, p]).astype(BF16)
    d_ref[layer, pl.ds(p * BLOCK, BLOCK), :] = dpre
    dn = dot(dpre, w_ref[layer], 1, 1)
    u = h * inv
    inner = jnp.mean(dn * u, axis=-1, keepdims=True)
    return g + inv * (dn - u * inner)


def kernel(
    n_blk,
    partner_hbm,
    state_hbm,
    basis_hbm,
    w_hbm,
    cot_hbm,
    out_ref,
    gstate_ref,
    wgrad_ref,
    partner_ref,
    state_ref,
    basis_ref,
    w_ref,
    cot_ref,
    n_ref,
    d_ref,
    eout_ref,
    gout_ref,
    sent_ref,
    rev_ref,
    mix_ref,
    mixed_ref,
    first_ref,
    second_ref,
    gs_ref,
    inv_ref,
    slope_ref,
    pos_ref,
    pair_ref,
    take_ref,
    half_ref,
    own_ref,
    half_in_ref,
    part_ref,
    part_in_ref,
    direct_in_ref,
    quad_ref,
    quad_in_ref,
    piece_ref,
    final_ref,
    in_sem,
    give_sem,
    take_sem,
    half_sem,
    half_in_sem,
    part_sem,
    part_in_sem,
    direct_sem,
    direct_in_sem,
    piece_sem,
    final_sem,
):
    x = lax.axis_index("grp")
    b = lax.axis_index("blk")
    me = x * n_blk + b
    core = b % 2
    y = (b // 2) % 2
    z = b // 4
    count = 2 * n_blk
    width = w_ref.shape[2]

    loads = [
        pltpu.make_async_copy(src, dst, in_sem.at[number])
        for number, (src, dst) in enumerate(
            [
                (partner_hbm, partner_ref),
                (basis_hbm, basis_ref),
                (state_hbm, state_ref),
                (w_hbm.at[0], w_ref.at[0]),
                (w_hbm.at[1], w_ref.at[1]),
                (w_hbm.at[2], w_ref.at[2]),
                (cot_hbm, cot_ref),
            ]
        )
    ]
    for load in loads:
        load.start()

    barrier = pltpu.get_barrier_semaphore()

    def greet(step, carry):
        other = (me + step) % count
        pl.semaphore_signal(
            barrier, inc=1, device_id=(other // n_blk, other % n_blk), device_id_type=MESH
        )
        return carry

    lax.fori_loop(1, count, greet, 0)

    base = x * 3
    loads[0].wait()
    p0, p1, p2 = partner_ref[0], partner_ref[1], partner_ref[2]
    sides = [jnp.minimum(jnp.maximum(p - 2, 0), 1) - x for p in (p0, p1, p2)]
    away0, away1, away2 = (side * side for side in sides)
    first_pos = jnp.minimum(away1 + 2 * away2, 2)
    pos1 = away0
    pos2 = 2 - away2
    shift = away0 * p1 + (1 - away0) * p0 - base - pos1
    swapped = jnp.minimum(shift * shift, 1)
    place = (1 - away0, jnp.minimum(away0 + 2 * away2, 2), 2 - 2 * away2)

    for p, value in enumerate((first_pos, pos1, pos2)):
        pos_ref[p] = value
    for p, value in enumerate((0, 1 + swapped, 2 - swapped)):
        pair_ref[p] = value
    saved = (n_ref, d_ref, inv_ref, slope_ref)

    def exchange(step):
        return pltpu.make_async_remote_copy(
            src_ref=sent_ref.at[step, 0],
            dst_ref=take_ref.at[step],
            send_sem=give_sem.at[step],
            recv_sem=take_sem.at[step],
            device_id=(1 - x, b),
            device_id_type=MESH,
        )

    def half_copy(layer):
        return pltpu.make_async_remote_copy(
            src_ref=half_ref.at[layer],
            dst_ref=half_in_ref.at[layer],
            send_sem=half_sem.at[layer],
            recv_sem=half_in_sem.at[layer],
            device_id=(x, b + 1 - 2 * core),
            device_id_type=MESH,
        )

    half_rows = width // 2
    eighth = half_rows // 8

    def send_half(layer):
        def columns(c):
            return n_ref[layer, :, pl.ds(pl.multiple_of(c * half_rows, half_rows), half_rows)]

        d = d_ref[layer]
        half_ref[layer] = dot(columns(1 - core), d, 0, 0).astype(BF16)
        half_copy(layer).start()
        own_ref[layer] = dot(columns(core), d, 0, 0)

    def direct_copy(r):
        px = 1 - x if r >= 2 else x
        py = 1 - y if r % 2 else y
        return pltpu.make_async_remote_copy(
            src_ref=part_ref.at[0, px, py],
            dst_ref=direct_in_ref.at[r - 1],
            send_sem=direct_sem.at[r - 1],
            recv_sem=direct_in_sem.at[r - 1],
            device_id=(px, 4 * z + 2 * py + core),
            device_id_type=MESH,
        )

    def sides(layer, piece):
        return (x, y) if piece == 1 and layer == 1 else (y, x)

    def part_copy(layer, piece, hop):
        along_x = (piece == 1 and layer == 1) == (hop == 0)
        near, far = sides(layer, piece)
        if hop == 0:
            src, dst = part_ref.at[layer, piece, 1 - near], part_in_ref.at[layer, piece]
        else:
            src, dst = quad_ref.at[layer, piece, 1 - far], quad_in_ref.at[layer, piece]
        return pltpu.make_async_remote_copy(
            src_ref=src,
            dst_ref=dst,
            send_sem=part_sem.at[layer, piece, hop],
            recv_sem=part_in_sem.at[layer, piece, hop],
            device_id=(1 - x, b) if along_x else (x, b + 2 - 4 * y),
            device_id_type=MESH,
        )

    def send_parts(layer):
        half_copy(layer).wait_recv()
        total = own_ref[layer] + half_in_ref[layer].astype(F32)
        part_ref[layer] = total.astype(BF16).reshape(2, 2, 2, eighth, width)
        if layer == 0:
            for r in (3, 2, 1):
                direct_copy(r).start()
        else:
            for piece in range(2):
                part_copy(layer, piece, 0).start()

    def send_quads(layer):
        for piece in range(2):
            part_copy(layer, piece, 0).wait_recv()
            near, _ = sides(layer, piece)
            total = part_ref[layer, piece, near].astype(F32)
            total = total + part_in_ref[layer, piece].astype(F32)
            quad_ref[layer, piece] = total.astype(BF16)
            part_copy(layer, piece, 1).start()

    def piece_copy(layer, t):
        near, far = sides(layer, t // 2)
        if layer == 0:
            c = 16 * core + 8 * x + 4 * y + t
        else:
            c = 32 * layer + 16 * core + 8 * (t // 2) + 4 * near + 2 * far + t % 2
        dest = c // 3
        copy = pltpu.make_async_remote_copy(
            src_ref=piece_ref.at[layer, t],
            dst_ref=final_ref.at[c % 3, z],
            send_sem=piece_sem.at[layer, t],
            recv_sem=final_sem.at[c % 3, z],
            device_id=(dest // n_blk, dest % n_blk),
            device_id_type=MESH,
        )
        return c, dest, copy

    def send_pieces(layer):
        if layer == 0:
            total = part_ref[0, x, y].astype(F32)
            for r in (1, 2, 3):
                direct_copy(r).wait_recv()
                total = total + direct_in_ref[r - 1].astype(F32)
            piece_ref[0] = total.astype(BF16).reshape(4, CHUNK, width)
        else:
            for piece in range(2):
                part_copy(layer, piece, 1).wait_recv()
                _, far = sides(layer, piece)
                total = quad_ref[layer, piece, far].astype(F32)
                total = total + quad_in_ref[layer, piece].astype(F32)
                piece_ref[layer, pl.ds(2 * piece, 2)] = total.astype(BF16).reshape(
                    2, CHUNK, width
                )
        for t in range(4):
            c, dest, copy = piece_copy(layer, t)

            @pl.when(dest != me)
            def _():
                copy.start()

            @pl.when(dest == me)
            def _():
                final_ref[c % 3, z] = piece_ref[layer, t]

    def phase_one(p, carry):
        mix = mixing_matrix(basis_ref[...], pos_ref[p])
        mix_ref[p] = mix
        mixed = dot(mix, state_ref[pos_ref[p]])
        mixed_ref[p] = mixed
        first = forward(mixed, w_ref, 0, p, saved)
        first_ref[p] = first
        second = forward(first, w_ref, 1, p, saved)
        second_ref[p] = second
        sent_ref[0, p] = second.astype(BF16)

        @pl.when(p == 0)
        def _():
            pl.semaphore_wait(barrier, count - 1)
            exchange(0).start()

        return carry

    def reverse(step, p):
        @pl.when(p == 0)
        def _():
            exchange(step).wait_recv()
            rev_ref[...] = take_ref[step]

        @pl.when(p > 0)
        def _():
            rev_ref[...] = sent_ref[step, pair_ref[p]]

        return flip(rev_ref[...].astype(F32))

    def phase_two(i, carry):
        p = 1 - i + 3 * (i // 2)
        summed = second_ref[p] + reverse(0, p)
        final = forward(summed, w_ref, 2, p, saved)
        eout_ref[p] = final.astype(BF16)
        g = backward(summed, w_ref, 2, p, saved, cot_ref[pos_ref[p]].astype(F32))
        gs_ref[p] = g
        sent_ref[1, p] = g.astype(BF16)

        @pl.when(p == 0)
        def _():
            exchange(1).start()

        return carry

    def phase_three(i, carry):
        p = (i + 1) % 3
        g = gs_ref[p] + reverse(1, p)
        g = backward(first_ref[p], w_ref, 1, p, saved, g)
        g = backward(mixed_ref[p], w_ref, 0, p, saved, g)
        gout_ref[p] = dot(mix_ref[p], g.astype(BF16), 0, 0).astype(BF16)

        @pl.when(p == 2)
        def _():
            send_parts(2)

        return carry

    for load in loads[1:5]:
        load.wait()
    lax.fori_loop(0, 3, phase_one, 0)
    for load in loads[5:]:
        load.wait()
    lax.fori_loop(0, 3, phase_two, 0)
    send_half(2)
    lax.fori_loop(0, 3, phase_three, 0)
    lax.fori_loop(0, 2, lambda i, carry: (send_half(i), carry)[1], 0)
    send_parts(0)
    send_quads(2)
    send_parts(1)
    send_pieces(2)
    send_pieces(0)
    send_quads(1)

    for k in range(3):
        out_ref[k] = eout_ref[place[k]]
        gstate_ref[k] = gout_ref[place[k]]

    send_pieces(1)

    for j in range(3):
        c = 3 * me + j
        i = c % 32
        near, far = (i // 4) % 2, (i // 2) % 2
        layer = c // 32
        x_first = ((i // 8) % 2) * (layer % 2)
        from_y = near + x_first * (far - near)
        from_x = far + x_first * (near - far) + ((2 - layer) // 2) * ((i // 8) % 2 - far)
        for plane in range(4):
            source = from_x * n_blk + 4 * plane + 2 * from_y + i // 16

            @pl.when(source != me)
            def _():
                pltpu.make_async_remote_copy(
                    src_ref=piece_ref.at[0, 0],
                    dst_ref=final_ref.at[j, plane],
                    send_sem=piece_sem.at[0, 0],
                    recv_sem=final_sem.at[j, plane],
                    device_id=(1 - x, b),
                    device_id_type=MESH,
                ).wait_recv()

    for j in range(3):
        total = final_ref[j, 0].astype(F32)
        for plane in range(1, 4):
            total = total + final_ref[j, plane].astype(F32)
        wgrad_ref[j] = total

    for step in range(2):
        exchange(step).wait_send()
    for layer in range(3):
        half_copy(layer).wait_send()
        if layer == 0:
            for r in (1, 2, 3):
                direct_copy(r).wait_send()
        else:
            for piece in range(2):
                for hop in range(2):
                    part_copy(layer, piece, hop).wait_send()
        for t in range(4):
            c, dest, copy = piece_copy(layer, t)

            @pl.when(dest != me)
            def _():
                copy.wait_send()


def finish(scale, out_ref, gstate_ref, wgrad_ref, out_hbm, gstate_hbm, total_ref, sems):
    copies = [
        pltpu.make_async_copy(out_ref, out_hbm, sems.at[0]),
        pltpu.make_async_copy(gstate_ref, gstate_hbm, sems.at[1]),
    ]
    for copy in copies:
        copy.start()
    total_ref[...] = wgrad_ref[...] * scale
    for copy in copies:
        copy.wait()


def local_fast(n_blk, edge_state, basis, weights, partner, cotangent):
    rows, width = edge_state.shape
    total_edges = rows * 2 * n_blk
    half = width // 2
    blocks = (rows // BLOCK, BLOCK, width)
    vmem = pl.BlockSpec(memory_space=pltpu.VMEM)
    dma = pltpu.SemaphoreType.DMA
    out, gstate, wgrad = pl.pallas_call(
        functools.partial(kernel, n_blk),
        out_shape=(
            jax.ShapeDtypeStruct(blocks, BF16),
            jax.ShapeDtypeStruct(blocks, BF16),
            jax.ShapeDtypeStruct((3, CHUNK, width), F32),
        ),
        in_specs=[pl.BlockSpec(memory_space=pltpu.HBM)] * 5,
        out_specs=(vmem, vmem, vmem),
        scratch_shapes=[
            pltpu.SMEM(partner.shape, jnp.int32),
            pltpu.VMEM(blocks, BF16),
            pltpu.VMEM((NBR, NBR, basis.shape[0]), BF16),
            pltpu.VMEM(weights.shape, BF16),
            pltpu.VMEM(blocks, BF16),
            pltpu.VMEM((3, rows, width), BF16),
            pltpu.VMEM((3, rows, width), BF16),
            pltpu.VMEM(blocks, BF16),
            pltpu.VMEM(blocks, BF16),
            pltpu.VMEM((2, 3, BLOCK, width), BF16),
            pltpu.VMEM((BLOCK, width), BF16),
            pltpu.VMEM((3, BLOCK, BLOCK), BF16),
            pltpu.VMEM(blocks, F32),
            pltpu.VMEM(blocks, F32),
            pltpu.VMEM(blocks, F32),
            pltpu.VMEM(blocks, F32),
            pltpu.VMEM((3, 3, BLOCK, 1), F32),
            pltpu.VMEM((3, 3, BLOCK, width), F32),
            pltpu.SMEM((3,), jnp.int32),
            pltpu.SMEM((3,), jnp.int32),
            pltpu.VMEM((2, BLOCK, width), BF16),
            pltpu.VMEM((3, half, width), BF16),
            pltpu.VMEM((3, half, width), F32),
            pltpu.VMEM((3, half, width), BF16),
            pltpu.VMEM((3, 2, 2, 2, half // 8, width), BF16),
            pltpu.VMEM((3, 2, 2, half // 8, width), BF16),
            pltpu.VMEM((3, 2, half // 8, width), BF16),
            pltpu.VMEM((3, 2, 2, half // 8, width), BF16),
            pltpu.VMEM((3, 2, half // 8, width), BF16),
            pltpu.VMEM((3, 4, CHUNK, width), BF16),
            pltpu.VMEM((3, 4, CHUNK, width), BF16),
            dma((7,)),
            dma((2,)),
            dma((2,)),
            dma((3,)),
            dma((3,)),
            dma((3, 2, 2)),
            dma((3, 2, 2)),
            dma((3,)),
            dma((3,)),
            dma((3, 4)),
            dma((3, 4)),
        ],
        compiler_params=pltpu.CompilerParams(
            collective_id=0, has_side_effects=True, vmem_limit_bytes=36 * 2**20
        ),
    )(
        *[
            pltpu.with_memory_space_constraint(array, pltpu.HBM)
            for array in (
                partner,
                edge_state.reshape(blocks),
                basis.transpose(1, 2, 0),
                weights,
                cotangent.reshape(blocks),
            )
        ]
    )
    hbm = pl.BlockSpec(memory_space=pltpu.HBM)
    out, gstate, wgrad = pl.pallas_call(
        functools.partial(finish, 1.0 / math.sqrt(total_edges)),
        out_shape=(
            jax.ShapeDtypeStruct(blocks, BF16),
            jax.ShapeDtypeStruct(blocks, BF16),
            jax.ShapeDtypeStruct((3, CHUNK, width), F32),
        ),
        in_specs=[vmem, vmem, vmem],
        out_specs=(hbm, hbm, vmem),
        scratch_shapes=[dma((2,))],
        compiler_params=pltpu.CompilerParams(vmem_limit_bytes=8 * 2**20),
    )(out, gstate, wgrad)
    return (
        out.reshape(rows, width),
        gstate.reshape(rows, width),
        wgrad.reshape(3 * CHUNK, width),
    )


def norm_rows(hidden):
    return hidden * lax.rsqrt(jnp.mean(hidden * hidden, axis=-1, keepdims=True) + 1e-06)


def layer_forward(hidden, weight):
    normed = norm_rows(hidden).astype(jnp.bfloat16)
    preact = jnp.dot(normed, weight, preferred_element_type=jnp.float32)
    return (hidden + jax.nn.silu(preact), normed, preact)


def layer_backward(hidden, normed, preact, weight, upstream):
    sigma = jax.nn.sigmoid(preact)
    grad_pre = (upstream * sigma * (1.0 + preact * (1.0 - sigma))).astype(jnp.bfloat16)
    grad_weight = lax.dot_general(
        normed, grad_pre, (((0,), (0,)), ((), ())), preferred_element_type=jnp.float32
    )
    grad_normed = lax.dot_general(
        grad_pre, weight, (((1,), (1,)), ((), ())), preferred_element_type=jnp.float32
    )
    inverse = lax.rsqrt(jnp.mean(hidden * hidden, axis=-1, keepdims=True) + 1e-06)
    unit = hidden * inverse
    inner = jnp.mean(grad_normed * unit, axis=-1, keepdims=True)
    return (upstream + inverse * (grad_normed - unit * inner), grad_weight)


def flip_rows(blocks):
    count, height, width = blocks.shape
    return blocks.reshape(count, height // 2, 2, width)[:, :, ::-1, :].reshape(count, height, width)


def route_plan(partner, own_index, group_count):
    block_count = partner.shape[0]
    target = partner // block_count
    remote = partner % block_count
    order = jnp.arange(block_count)
    same = target[:, None] == target[None, :]
    send_rank = jnp.sum(same & (order[None, :] < order[:, None]), axis=1)
    recv_rank = jnp.sum(same & (remote[None, :] < remote[:, None]), axis=1)
    local_pair = target == own_index
    slots = jnp.arange(group_count * CAP)
    send_slot = target * CAP + send_rank
    recv_slot = target * CAP + recv_rank
    pack_matrix = ((slots[:, None] == send_slot[None, :]) & ~local_pair[None, :]).astype(
        jnp.bfloat16
    )
    unpack_matrix = ((recv_slot[:, None] == slots[None, :]) & ~local_pair[:, None]).astype(
        jnp.bfloat16
    )
    return (pack_matrix, unpack_matrix, local_pair)


def pack_blocks(values, pack_matrix, block_count):
    blocks = values.reshape(block_count, -1, values.shape[1])
    return jnp.einsum("sn,nrd->srd", pack_matrix, blocks, preferred_element_type=jnp.bfloat16)


def unpack_blocks(arrived, unpack_matrix, local_pair, values, block_count):
    blocks = values.reshape(block_count, -1, values.shape[1])
    distant = jnp.einsum("ns,srd->nrd", unpack_matrix, arrived, preferred_element_type=jnp.bfloat16)
    joined = jnp.where(local_pair[:, None, None], blocks, distant)
    return flip_rows(joined).reshape(values.shape)


def local(edge_state, basis, weights, partner, cotangent):
    row_count, width = edge_state.shape
    block_count = partner.shape[0]
    group_count = lax.axis_size("grp")
    own_index = lax.axis_index("grp")
    total_edges = row_count * group_count * lax.axis_size("blk")
    pack_matrix, unpack_matrix, local_pair = route_plan(partner, own_index, group_count)
    mixed = jnp.einsum(
        "aij,ajd->aid",
        basis,
        edge_state.reshape(-1, NBR, width),
        preferred_element_type=jnp.float32,
    ).reshape(row_count, width)
    first, normed_one, pre_one = layer_forward(mixed, weights[0])
    second, normed_two, pre_two = layer_forward(first, weights[1])
    sent = second.astype(jnp.bfloat16)
    arrived = lax.all_to_all(
        pack_blocks(sent, pack_matrix, block_count), "grp", split_axis=0, concat_axis=0, tiled=True
    )
    reversed_state = unpack_blocks(arrived, unpack_matrix, local_pair, sent, block_count)
    summed = second + reversed_state.astype(jnp.float32)
    final, normed_three, pre_three = layer_forward(summed, weights[2])
    edge_out = final.astype(jnp.bfloat16)
    grad_summed, grad_three = layer_backward(
        summed, normed_three, pre_three, weights[2], cotangent.astype(jnp.float32)
    )
    grad_reversed = grad_summed.astype(jnp.bfloat16)
    returned = lax.all_to_all(
        pack_blocks(grad_reversed, pack_matrix, block_count),
        "grp",
        split_axis=0,
        concat_axis=0,
        tiled=True,
    )
    grad_sent = unpack_blocks(returned, unpack_matrix, local_pair, grad_reversed, block_count)
    grad_second = grad_summed + grad_sent.astype(jnp.float32)
    grad_first, grad_two = layer_backward(first, normed_two, pre_two, weights[1], grad_second)
    grad_mixed, grad_one = layer_backward(mixed, normed_one, pre_one, weights[0], grad_first)
    grad_round = grad_mixed.astype(jnp.bfloat16).reshape(-1, NBR, width)
    grad_state = (
        jnp.einsum("aij,aid->ajd", basis, grad_round, preferred_element_type=jnp.float32)
        .reshape(row_count, width)
        .astype(jnp.bfloat16)
    )
    local_grads = jnp.concatenate([grad_one, grad_two, grad_three], axis=0)
    group_part = lax.psum_scatter(
        local_grads.astype(jnp.bfloat16), "grp", scatter_dimension=0, tiled=True
    ).astype(jnp.float32)
    summed_grads = lax.psum_scatter(group_part, "blk", scatter_dimension=0, tiled=True)
    weight_grad = summed_grads * (1.0 / math.sqrt(total_edges))
    return (edge_out, grad_state, weight_grad)


def solution(mesh):
    spread = P(("grp", "blk"))
    wide = P(("grp", "blk"), None)
    in_specs = (wide, P(("grp", "blk"), None, None), P(), spread, wide)
    body = local
    if mesh.shape["grp"] == 2 and mesh.shape["blk"] == 16:
        body = functools.partial(local_fast, mesh.shape["blk"])
    return jax.shard_map(
        body, mesh=mesh, in_specs=in_specs, out_specs=(wide, wide, wide), check_vma=False
    )
```

```python
import functools
import math

import jax
import jax.numpy as jnp
from jax import lax
from jax.experimental import pallas as pl
from jax.experimental.pallas import tpu as pltpu
from jax.sharding import PartitionSpec as P

NBR = 16
CAP = 1
BLOCK = 128
CHUNK = 16
EPS = 1e-06
MESH = pl.DeviceIdType.MESH
BF16 = jnp.bfloat16
F32 = jnp.float32


def dot(a, b, ca=1, cb=0):
    return lax.dot_general(a, b, (((ca,), (cb,)), ((), ())), preferred_element_type=F32)


def inverse_rms(h):
    return lax.rsqrt(jnp.mean(h * h, axis=-1, keepdims=True) + EPS)


def flip(x):
    rows = x.shape[0]
    even = lax.broadcasted_iota(jnp.int32, x.shape, 0) % 2 == 0
    return jnp.where(even, pltpu.roll(x, rows - 1, 0), pltpu.roll(x, 1, 0))


def mixing_matrix(basis, block):
    flat = basis.reshape(NBR * NBR, basis.shape[2])
    rows = BLOCK

    def iota(shape, dim):
        return lax.broadcasted_iota(jnp.int32, shape, dim)

    def mask(hit):
        return hit.astype(F32).astype(BF16)

    atom_shape = (rows, basis.shape[2])
    atom = block * (BLOCK // NBR) + iota(atom_shape, 0) // NBR
    pick = mask(atom == iota(atom_shape, 1))
    own = dot(pick, flat, 1, 1)
    own_shape = (rows, NBR * NBR)
    own = jnp.where(iota(own_shape, 0) % NBR == iota(own_shape, 1) // NBR, own, 0.0).astype(BF16)
    spread_shape = (NBR * NBR, rows)
    spread = mask(iota(spread_shape, 0) % NBR == iota(spread_shape, 1) % NBR)
    wide = dot(own, spread)
    same = iota((rows, rows), 0) // NBR == iota((rows, rows), 1) // NBR
    return jnp.where(same, wide, 0.0).astype(BF16)


def forward(h, w_ref, layer, p, saved):
    n_ref, _, inv_ref, slope_ref = saved
    inv = inverse_rms(h)
    normed = (h * inv).astype(BF16)
    n_ref[layer, pl.ds(p * BLOCK, BLOCK), :] = normed
    inv_ref[layer, p] = inv
    pre = dot(normed, w_ref[layer])
    s = 0.5 * jnp.tanh(0.5 * pre) + 0.5
    slope_ref[layer, p] = s * (1.0 + pre * (1.0 - s))
    return h + pre * s


def backward(h, w_ref, layer, p, saved, g):
    _, d_ref, inv_ref, slope_ref = saved
    inv = inv_ref[layer, p]
    dpre = (g * slope_ref[layer, p]).astype(BF16)
    d_ref[layer, pl.ds(p * BLOCK, BLOCK), :] = dpre
    dn = dot(dpre, w_ref[layer], 1, 1)
    u = h * inv
    inner = jnp.mean(dn * u, axis=-1, keepdims=True)
    return g + inv * (dn - u * inner)


def kernel(
    n_blk,
    partner_hbm,
    state_hbm,
    basis_hbm,
    w_hbm,
    cot_hbm,
    out_ref,
    gstate_ref,
    wgrad_ref,
    partner_ref,
    state_ref,
    basis_ref,
    w_ref,
    cot_ref,
    n_ref,
    d_ref,
    eout_ref,
    gout_ref,
    sent_ref,
    rev_ref,
    gm_ref,
    mix_ref,
    mixed_ref,
    first_ref,
    second_ref,
    gs_ref,
    inv_ref,
    slope_ref,
    pos_ref,
    pair_ref,
    take_ref,
    half_ref,
    own_ref,
    half_in_ref,
    part_ref,
    part_in_ref,
    direct_in_ref,
    quad_ref,
    quad_in_ref,
    piece_ref,
    final_ref,
    in_sem,
    give_sem,
    take_sem,
    half_sem,
    half_in_sem,
    part_sem,
    part_in_sem,
    direct_sem,
    direct_in_sem,
    piece_sem,
    final_sem,
):
    x = lax.axis_index("grp")
    b = lax.axis_index("blk")
    me = x * n_blk + b
    core = b % 2
    y = (b // 2) % 2
    z = b // 4
    count = 2 * n_blk
    width = w_ref.shape[2]

    loads = [
        pltpu.make_async_copy(src, dst, in_sem.at[number])
        for number, (src, dst) in enumerate(
            [
                (partner_hbm, partner_ref),
                (basis_hbm, basis_ref),
                (state_hbm, state_ref),
                (w_hbm.at[0], w_ref.at[0]),
                (w_hbm.at[1], w_ref.at[1]),
                (w_hbm.at[2], w_ref.at[2]),
                (cot_hbm, cot_ref),
            ]
        )
    ]
    for load in loads:
        load.start()

    barrier = pltpu.get_barrier_semaphore()

    def greet(step, carry):
        other = (me + step) % count
        pl.semaphore_signal(
            barrier, inc=1, device_id=(other // n_blk, other % n_blk), device_id_type=MESH
        )
        return carry

    lax.fori_loop(1, count, greet, 0)

    base = x * 3
    loads[0].wait()
    p0, p1, p2 = partner_ref[0], partner_ref[1], partner_ref[2]
    sides = [jnp.minimum(jnp.maximum(p - 2, 0), 1) - x for p in (p0, p1, p2)]
    away0, away1, away2 = (side * side for side in sides)
    first_pos = jnp.minimum(away1 + 2 * away2, 2)
    pos1 = away0
    pos2 = 2 - away2
    shift = away0 * p1 + (1 - away0) * p0 - base - pos1
    swapped = jnp.minimum(shift * shift, 1)
    place = (1 - away0, jnp.minimum(away0 + 2 * away2, 2), 2 - 2 * away2)

    for p, value in enumerate((first_pos, pos1, pos2)):
        pos_ref[p] = value
    for p, value in enumerate((0, 1 + swapped, 2 - swapped)):
        pair_ref[p] = value
    saved = (n_ref, d_ref, inv_ref, slope_ref)

    def exchange(step):
        return pltpu.make_async_remote_copy(
            src_ref=sent_ref.at[step, 0],
            dst_ref=take_ref.at[step],
            send_sem=give_sem.at[step],
            recv_sem=take_sem.at[step],
            device_id=(1 - x, b),
            device_id_type=MESH,
        )

    def half_copy(layer):
        return pltpu.make_async_remote_copy(
            src_ref=half_ref.at[layer],
            dst_ref=half_in_ref.at[layer],
            send_sem=half_sem.at[layer],
            recv_sem=half_in_sem.at[layer],
            device_id=(x, b + 1 - 2 * core),
            device_id_type=MESH,
        )

    half_rows = width // 2
    eighth = half_rows // 8

    def send_half(layer):
        def columns(c):
            return n_ref[layer, :, pl.ds(pl.multiple_of(c * half_rows, half_rows), half_rows)]

        d = d_ref[layer]
        half_ref[layer] = dot(columns(1 - core), d, 0, 0).astype(BF16)
        half_copy(layer).start()
        own_ref[layer] = dot(columns(core), d, 0, 0)

    def direct_copy(layer, r):
        px = 1 - x if r >= 2 else x
        py = 1 - y if r % 2 else y
        return pltpu.make_async_remote_copy(
            src_ref=part_ref.at[layer, px, py],
            dst_ref=direct_in_ref.at[layer, r - 1],
            send_sem=direct_sem.at[layer, r - 1],
            recv_sem=direct_in_sem.at[layer, r - 1],
            device_id=(px, 4 * z + 2 * py + core),
            device_id_type=MESH,
        )

    def part_copy(layer, piece, hop):
        along_x = hop == 1
        near, far = y, x
        if hop == 0:
            src, dst = part_ref.at[layer, piece, 1 - near], part_in_ref.at[layer, piece]
        else:
            src, dst = quad_ref.at[layer, piece, 1 - far], quad_in_ref.at[layer, piece]
        return pltpu.make_async_remote_copy(
            src_ref=src,
            dst_ref=dst,
            send_sem=part_sem.at[layer, piece, hop],
            recv_sem=part_in_sem.at[layer, piece, hop],
            device_id=(1 - x, b) if along_x else (x, b + 2 - 4 * y),
            device_id_type=MESH,
        )

    def send_parts(layer):
        half_copy(layer).wait_recv()
        total = own_ref[layer] + half_in_ref[layer].astype(F32)
        part_ref[layer] = total.astype(BF16).reshape(2, 2, 2, eighth, width)
        if layer < 2:
            for r in (3, 2, 1):
                direct_copy(layer, r).start()
        else:
            for piece in range(2):
                part_copy(layer, piece, 0).start()

    def send_quads(layer):
        for piece in range(2):
            part_copy(layer, piece, 0).wait_recv()
            total = part_ref[layer, piece, y].astype(F32)
            total = total + part_in_ref[layer, piece].astype(F32)
            quad_ref[layer, piece] = total.astype(BF16)
            part_copy(layer, piece, 1).start()

    def piece_copy(layer, t):
        if layer < 2:
            c = 32 * layer + 16 * core + 8 * x + 4 * y + t
        else:
            c = 32 * layer + 16 * core + 8 * (t // 2) + 4 * y + 2 * x + t % 2
        dest = c // 3
        copy = pltpu.make_async_remote_copy(
            src_ref=piece_ref.at[layer, t],
            dst_ref=final_ref.at[c % 3, z],
            send_sem=piece_sem.at[layer, t],
            recv_sem=final_sem.at[c % 3, z],
            device_id=(dest // n_blk, dest % n_blk),
            device_id_type=MESH,
        )
        return c, dest, copy

    def send_pieces(layer):
        if layer < 2:
            total = part_ref[layer, x, y].astype(F32)
            for r in (1, 2, 3):
                direct_copy(layer, r).wait_recv()
                total = total + direct_in_ref[layer, r - 1].astype(F32)
            piece_ref[layer] = total.astype(BF16).reshape(4, CHUNK, width)
        else:
            for piece in range(2):
                part_copy(layer, piece, 1).wait_recv()
                total = quad_ref[layer, piece, x].astype(F32)
                total = total + quad_in_ref[layer, piece].astype(F32)
                piece_ref[layer, pl.ds(2 * piece, 2)] = total.astype(BF16).reshape(
                    2, CHUNK, width
                )
        for t in range(4):
            c, dest, copy = piece_copy(layer, t)

            @pl.when(dest != me)
            def _():
                copy.start()

            @pl.when(dest == me)
            def _():
                final_ref[c % 3, z] = piece_ref[layer, t]

    def phase_one(p, carry):
        mix = mixing_matrix(basis_ref[...], pos_ref[p])
        mix_ref[p] = mix
        mixed = dot(mix, state_ref[pos_ref[p]])
        mixed_ref[p] = mixed
        first = forward(mixed, w_ref, 0, p, saved)
        first_ref[p] = first
        second = forward(first, w_ref, 1, p, saved)
        second_ref[p] = second
        sent_ref[0, p] = second.astype(BF16)

        @pl.when(p == 0)
        def _():
            pl.semaphore_wait(barrier, count - 1)
            exchange(0).start()

        return carry

    def reverse(step, p):
        @pl.when(p == 0)
        def _():
            exchange(step).wait_recv()
            rev_ref[...] = take_ref[step]

        @pl.when(p > 0)
        def _():
            rev_ref[...] = sent_ref[step, pair_ref[p]]

        return flip(rev_ref[...].astype(F32))

    def phase_two(i, carry):
        p = 1 - i + 3 * (i // 2)
        summed = second_ref[p] + reverse(0, p)
        final = forward(summed, w_ref, 2, p, saved)
        eout_ref[p] = final.astype(BF16)
        g = backward(summed, w_ref, 2, p, saved, cot_ref[pos_ref[p]].astype(F32))
        gs_ref[p] = g
        sent_ref[1, p] = g.astype(BF16)

        @pl.when(p == 0)
        def _():
            exchange(1).start()

        return carry

    def phase_three(i, carry):
        p = (i + 1) % 3
        g = gs_ref[p] + reverse(1, p)
        g = backward(first_ref[p], w_ref, 1, p, saved, g)
        g = backward(mixed_ref[p], w_ref, 0, p, saved, g)
        gm_ref[...] = g.astype(BF16)

        @pl.when(p > 0)
        def _():
            gout_ref[p] = dot(mix_ref[p], gm_ref[...], 0, 0).astype(BF16)

        @pl.when(p == 2)
        def _():
            send_parts(2)

        return carry

    for load in loads[1:5]:
        load.wait()
    lax.fori_loop(0, 3, phase_one, 0)
    for load in loads[5:]:
        load.wait()
    lax.fori_loop(0, 3, phase_two, 0)
    send_half(2)
    lax.fori_loop(0, 3, phase_three, 0)
    lax.fori_loop(0, 2, lambda i, carry: (send_half(i), carry)[1], 0)
    send_parts(0)
    send_quads(2)
    send_parts(1)
    gout_ref[0] = dot(mix_ref[0], gm_ref[...], 0, 0).astype(BF16)
    send_pieces(2)
    send_pieces(0)

    for k in range(3):
        out_ref[k] = eout_ref[place[k]]
        gstate_ref[k] = gout_ref[place[k]]

    send_pieces(1)

    for j in range(3):
        c = 3 * me + j
        i = c % 32
        from_y = (i // 4) % 2
        from_x = (i // 8) % 2 + (c // 64) * ((i // 2) % 2 - (i // 8) % 2)
        for plane in range(4):
            source = from_x * n_blk + 4 * plane + 2 * from_y + i // 16

            @pl.when(source != me)
            def _():
                pltpu.make_async_remote_copy(
                    src_ref=piece_ref.at[0, 0],
                    dst_ref=final_ref.at[j, plane],
                    send_sem=piece_sem.at[0, 0],
                    recv_sem=final_sem.at[j, plane],
                    device_id=(1 - x, b),
                    device_id_type=MESH,
                ).wait_recv()

    for j in range(3):
        total = final_ref[j, 0].astype(F32)
        for plane in range(1, 4):
            total = total + final_ref[j, plane].astype(F32)
        wgrad_ref[j] = total

    for step in range(2):
        exchange(step).wait_send()
    for layer in range(3):
        half_copy(layer).wait_send()
        if layer < 2:
            for r in (1, 2, 3):
                direct_copy(layer, r).wait_send()
        else:
            for piece in range(2):
                for hop in range(2):
                    part_copy(layer, piece, hop).wait_send()
        for t in range(4):
            c, dest, copy = piece_copy(layer, t)

            @pl.when(dest != me)
            def _():
                copy.wait_send()


def finish(
    scale, out_ref, gstate_ref, wgrad_ref, out_hbm, gstate_hbm, total_hbm, total_ref, sems
):
    copies = [
        pltpu.make_async_copy(out_ref, out_hbm, sems.at[0]),
        pltpu.make_async_copy(gstate_ref, gstate_hbm, sems.at[1]),
        pltpu.make_async_copy(total_ref, total_hbm, sems.at[2]),
    ]
    copies[0].start()
    copies[1].start()
    total_ref[...] = wgrad_ref[...] * scale
    copies[2].start()
    for copy in copies:
        copy.wait()


def local_fast(n_blk, edge_state, basis, weights, partner, cotangent):
    rows, width = edge_state.shape
    total_edges = rows * 2 * n_blk
    half = width // 2
    blocks = (rows // BLOCK, BLOCK, width)
    vmem = pl.BlockSpec(memory_space=pltpu.VMEM)
    dma = pltpu.SemaphoreType.DMA
    out, gstate, wgrad = pl.pallas_call(
        functools.partial(kernel, n_blk),
        out_shape=(
            jax.ShapeDtypeStruct(blocks, BF16),
            jax.ShapeDtypeStruct(blocks, BF16),
            jax.ShapeDtypeStruct((3, CHUNK, width), F32),
        ),
        in_specs=[pl.BlockSpec(memory_space=pltpu.HBM)] * 5,
        out_specs=(vmem, vmem, vmem),
        scratch_shapes=[
            pltpu.SMEM(partner.shape, jnp.int32),
            pltpu.VMEM(blocks, BF16),
            pltpu.VMEM((NBR, NBR, basis.shape[0]), BF16),
            pltpu.VMEM(weights.shape, BF16),
            pltpu.VMEM(blocks, BF16),
            pltpu.VMEM((3, rows, width), BF16),
            pltpu.VMEM((3, rows, width), BF16),
            pltpu.VMEM(blocks, BF16),
            pltpu.VMEM(blocks, BF16),
            pltpu.VMEM((2, 3, BLOCK, width), BF16),
            pltpu.VMEM((BLOCK, width), BF16),
            pltpu.VMEM((BLOCK, width), BF16),
            pltpu.VMEM((3, BLOCK, BLOCK), BF16),
            pltpu.VMEM(blocks, F32),
            pltpu.VMEM(blocks, F32),
            pltpu.VMEM(blocks, F32),
            pltpu.VMEM(blocks, F32),
            pltpu.VMEM((3, 3, BLOCK, 1), F32),
            pltpu.VMEM((3, 3, BLOCK, width), F32),
            pltpu.SMEM((3,), jnp.int32),
            pltpu.SMEM((3,), jnp.int32),
            pltpu.VMEM((2, BLOCK, width), BF16),
            pltpu.VMEM((3, half, width), BF16),
            pltpu.VMEM((3, half, width), F32),
            pltpu.VMEM((3, half, width), BF16),
            pltpu.VMEM((3, 2, 2, 2, half // 8, width), BF16),
            pltpu.VMEM((3, 2, 2, half // 8, width), BF16),
            pltpu.VMEM((2, 3, 2, half // 8, width), BF16),
            pltpu.VMEM((3, 2, 2, half // 8, width), BF16),
            pltpu.VMEM((3, 2, half // 8, width), BF16),
            pltpu.VMEM((3, 4, CHUNK, width), BF16),
            pltpu.VMEM((3, 4, CHUNK, width), BF16),
            dma((7,)),
            dma((2,)),
            dma((2,)),
            dma((3,)),
            dma((3,)),
            dma((3, 2, 2)),
            dma((3, 2, 2)),
            dma((2, 3)),
            dma((2, 3)),
            dma((3, 4)),
            dma((3, 4)),
        ],
        compiler_params=pltpu.CompilerParams(
            collective_id=0, has_side_effects=True, vmem_limit_bytes=36 * 2**20
        ),
    )(
        *[
            pltpu.with_memory_space_constraint(array, pltpu.HBM)
            for array in (
                partner,
                edge_state.reshape(blocks),
                basis.transpose(1, 2, 0),
                weights,
                cotangent.reshape(blocks),
            )
        ]
    )
    hbm = pl.BlockSpec(memory_space=pltpu.HBM)
    out, gstate, wgrad = pl.pallas_call(
        functools.partial(finish, 1.0 / math.sqrt(total_edges)),
        out_shape=(
            jax.ShapeDtypeStruct(blocks, BF16),
            jax.ShapeDtypeStruct(blocks, BF16),
            jax.ShapeDtypeStruct((3, CHUNK, width), F32),
        ),
        in_specs=[vmem, vmem, vmem],
        out_specs=(hbm, hbm, hbm),
        scratch_shapes=[pltpu.VMEM((3, CHUNK, width), F32), dma((3,))],
        compiler_params=pltpu.CompilerParams(vmem_limit_bytes=8 * 2**20),
    )(out, gstate, wgrad)
    return (
        out.reshape(rows, width),
        gstate.reshape(rows, width),
        wgrad.reshape(3 * CHUNK, width),
    )


def norm_rows(hidden):
    return hidden * lax.rsqrt(jnp.mean(hidden * hidden, axis=-1, keepdims=True) + 1e-06)


def layer_forward(hidden, weight):
    normed = norm_rows(hidden).astype(jnp.bfloat16)
    preact = jnp.dot(normed, weight, preferred_element_type=jnp.float32)
    return (hidden + jax.nn.silu(preact), normed, preact)


def layer_backward(hidden, normed, preact, weight, upstream):
    sigma = jax.nn.sigmoid(preact)
    grad_pre = (upstream * sigma * (1.0 + preact * (1.0 - sigma))).astype(jnp.bfloat16)
    grad_weight = lax.dot_general(
        normed, grad_pre, (((0,), (0,)), ((), ())), preferred_element_type=jnp.float32
    )
    grad_normed = lax.dot_general(
        grad_pre, weight, (((1,), (1,)), ((), ())), preferred_element_type=jnp.float32
    )
    inverse = lax.rsqrt(jnp.mean(hidden * hidden, axis=-1, keepdims=True) + 1e-06)
    unit = hidden * inverse
    inner = jnp.mean(grad_normed * unit, axis=-1, keepdims=True)
    return (upstream + inverse * (grad_normed - unit * inner), grad_weight)


def flip_rows(blocks):
    count, height, width = blocks.shape
    return blocks.reshape(count, height // 2, 2, width)[:, :, ::-1, :].reshape(count, height, width)


def route_plan(partner, own_index, group_count):
    block_count = partner.shape[0]
    target = partner // block_count
    remote = partner % block_count
    order = jnp.arange(block_count)
    same = target[:, None] == target[None, :]
    send_rank = jnp.sum(same & (order[None, :] < order[:, None]), axis=1)
    recv_rank = jnp.sum(same & (remote[None, :] < remote[:, None]), axis=1)
    local_pair = target == own_index
    slots = jnp.arange(group_count * CAP)
    send_slot = target * CAP + send_rank
    recv_slot = target * CAP + recv_rank
    pack_matrix = ((slots[:, None] == send_slot[None, :]) & ~local_pair[None, :]).astype(
        jnp.bfloat16
    )
    unpack_matrix = ((recv_slot[:, None] == slots[None, :]) & ~local_pair[:, None]).astype(
        jnp.bfloat16
    )
    return (pack_matrix, unpack_matrix, local_pair)


def pack_blocks(values, pack_matrix, block_count):
    blocks = values.reshape(block_count, -1, values.shape[1])
    return jnp.einsum("sn,nrd->srd", pack_matrix, blocks, preferred_element_type=jnp.bfloat16)


def unpack_blocks(arrived, unpack_matrix, local_pair, values, block_count):
    blocks = values.reshape(block_count, -1, values.shape[1])
    distant = jnp.einsum("ns,srd->nrd", unpack_matrix, arrived, preferred_element_type=jnp.bfloat16)
    joined = jnp.where(local_pair[:, None, None], blocks, distant)
    return flip_rows(joined).reshape(values.shape)


def local(edge_state, basis, weights, partner, cotangent):
    row_count, width = edge_state.shape
    block_count = partner.shape[0]
    group_count = lax.axis_size("grp")
    own_index = lax.axis_index("grp")
    total_edges = row_count * group_count * lax.axis_size("blk")
    pack_matrix, unpack_matrix, local_pair = route_plan(partner, own_index, group_count)
    mixed = jnp.einsum(
        "aij,ajd->aid",
        basis,
        edge_state.reshape(-1, NBR, width),
        preferred_element_type=jnp.float32,
    ).reshape(row_count, width)
    first, normed_one, pre_one = layer_forward(mixed, weights[0])
    second, normed_two, pre_two = layer_forward(first, weights[1])
    sent = second.astype(jnp.bfloat16)
    arrived = lax.all_to_all(
        pack_blocks(sent, pack_matrix, block_count), "grp", split_axis=0, concat_axis=0, tiled=True
    )
    reversed_state = unpack_blocks(arrived, unpack_matrix, local_pair, sent, block_count)
    summed = second + reversed_state.astype(jnp.float32)
    final, normed_three, pre_three = layer_forward(summed, weights[2])
    edge_out = final.astype(jnp.bfloat16)
    grad_summed, grad_three = layer_backward(
        summed, normed_three, pre_three, weights[2], cotangent.astype(jnp.float32)
    )
    grad_reversed = grad_summed.astype(jnp.bfloat16)
    returned = lax.all_to_all(
        pack_blocks(grad_reversed, pack_matrix, block_count),
        "grp",
        split_axis=0,
        concat_axis=0,
        tiled=True,
    )
    grad_sent = unpack_blocks(returned, unpack_matrix, local_pair, grad_reversed, block_count)
    grad_second = grad_summed + grad_sent.astype(jnp.float32)
    grad_first, grad_two = layer_backward(first, normed_two, pre_two, weights[1], grad_second)
    grad_mixed, grad_one = layer_backward(mixed, normed_one, pre_one, weights[0], grad_first)
    grad_round = grad_mixed.astype(jnp.bfloat16).reshape(-1, NBR, width)
    grad_state = (
        jnp.einsum("aij,aid->ajd", basis, grad_round, preferred_element_type=jnp.float32)
        .reshape(row_count, width)
        .astype(jnp.bfloat16)
    )
    local_grads = jnp.concatenate([grad_one, grad_two, grad_three], axis=0)
    group_part = lax.psum_scatter(
        local_grads.astype(jnp.bfloat16), "grp", scatter_dimension=0, tiled=True
    ).astype(jnp.float32)
    summed_grads = lax.psum_scatter(group_part, "blk", scatter_dimension=0, tiled=True)
    weight_grad = summed_grads * (1.0 / math.sqrt(total_edges))
    return (edge_out, grad_state, weight_grad)


def solution(mesh):
    spread = P(("grp", "blk"))
    wide = P(("grp", "blk"), None)
    in_specs = (wide, P(("grp", "blk"), None, None), P(), spread, wide)
    body = local
    if mesh.shape["grp"] == 2 and mesh.shape["blk"] == 16:
        body = functools.partial(local_fast, mesh.shape["blk"])
    return jax.shard_map(
        body, mesh=mesh, in_specs=in_specs, out_specs=(wide, wide, wide), check_vma=False
    )
```

```python
import functools
import math

import jax
import jax.numpy as jnp
from jax import lax
from jax.experimental import pallas as pl
from jax.experimental.pallas import tpu as pltpu
from jax.sharding import PartitionSpec as P

NBR = 16
CAP = 1
BLOCK = 128
CHUNK = 16
EPS = 1e-06
MESH = pl.DeviceIdType.MESH
BF16 = jnp.bfloat16
F32 = jnp.float32


def dot(a, b, ca=1, cb=0):
    return lax.dot_general(a, b, (((ca,), (cb,)), ((), ())), preferred_element_type=F32)


def inverse_rms(h):
    return lax.rsqrt(jnp.mean(h * h, axis=-1, keepdims=True) + EPS)


def flip(x):
    rows = x.shape[0]
    even = lax.broadcasted_iota(jnp.int32, x.shape, 0) % 2 == 0
    return jnp.where(even, pltpu.roll(x, rows - 1, 0), pltpu.roll(x, 1, 0))


def mixing_matrix(basis, block):
    flat = basis.reshape(NBR * NBR, basis.shape[2])
    rows = BLOCK

    def iota(shape, dim):
        return lax.broadcasted_iota(jnp.int32, shape, dim)

    def mask(hit):
        return hit.astype(F32).astype(BF16)

    atom_shape = (rows, basis.shape[2])
    atom = block * (BLOCK // NBR) + iota(atom_shape, 0) // NBR
    pick = mask(atom == iota(atom_shape, 1))
    own = dot(pick, flat, 1, 1)
    own_shape = (rows, NBR * NBR)
    own = jnp.where(iota(own_shape, 0) % NBR == iota(own_shape, 1) // NBR, own, 0.0).astype(BF16)
    spread_shape = (NBR * NBR, rows)
    spread = mask(iota(spread_shape, 0) % NBR == iota(spread_shape, 1) % NBR)
    wide = dot(own, spread)
    same = iota((rows, rows), 0) // NBR == iota((rows, rows), 1) // NBR
    return jnp.where(same, wide, 0.0).astype(BF16)


def forward(h, w_ref, layer, p, saved):
    n_ref, _, inv_ref, slope_ref = saved
    inv = inverse_rms(h)
    normed = (h * inv).astype(BF16)
    n_ref[layer, pl.ds(p * BLOCK, BLOCK), :] = normed
    inv_ref[layer, p] = inv
    pre = dot(normed, w_ref[layer])
    s = 0.5 * jnp.tanh(0.5 * pre) + 0.5
    slope_ref[layer, p] = s * (1.0 + pre * (1.0 - s))
    return h + pre * s


def backward(h, w_ref, layer, p, saved, g):
    _, d_ref, inv_ref, slope_ref = saved
    inv = inv_ref[layer, p]
    dpre = (g * slope_ref[layer, p]).astype(BF16)
    d_ref[layer, pl.ds(p * BLOCK, BLOCK), :] = dpre
    dn = dot(dpre, w_ref[layer], 1, 1)
    u = h * inv
    inner = jnp.mean(dn * u, axis=-1, keepdims=True)
    return g + inv * (dn - u * inner)


def kernel(
    n_blk,
    partner_hbm,
    state_hbm,
    basis_hbm,
    w_hbm,
    cot_hbm,
    out_ref,
    gstate_ref,
    wgrad_ref,
    partner_ref,
    state_ref,
    basis_ref,
    w_ref,
    cot_ref,
    n_ref,
    d_ref,
    eout_ref,
    gout_ref,
    sent_ref,
    rev_ref,
    gm_ref,
    mix_ref,
    mixed_ref,
    first_ref,
    second_ref,
    gs_ref,
    inv_ref,
    slope_ref,
    pos_ref,
    pair_ref,
    take_ref,
    half_ref,
    own_ref,
    half_in_ref,
    part_ref,
    part_in_ref,
    direct_in_ref,
    quad_ref,
    quad_in_ref,
    piece_ref,
    final_ref,
    in_sem,
    give_sem,
    take_sem,
    half_sem,
    half_in_sem,
    part_sem,
    part_in_sem,
    direct_sem,
    direct_in_sem,
    piece_sem,
    final_sem,
):
    x = lax.axis_index("grp")
    b = lax.axis_index("blk")
    me = x * n_blk + b
    core = b % 2
    y = (b // 2) % 2
    z = b // 4
    count = 2 * n_blk
    width = w_ref.shape[2]

    loads = [
        pltpu.make_async_copy(src, dst, in_sem.at[number])
        for number, (src, dst) in enumerate(
            [
                (partner_hbm, partner_ref),
                (basis_hbm, basis_ref),
                (state_hbm, state_ref),
                (w_hbm.at[0], w_ref.at[0]),
                (w_hbm.at[1], w_ref.at[1]),
                (w_hbm.at[2], w_ref.at[2]),
                (cot_hbm, cot_ref),
            ]
        )
    ]
    for load in loads:
        load.start()

    barrier = pltpu.get_barrier_semaphore()

    def greet(step, carry):
        other = (me + step) % count
        pl.semaphore_signal(
            barrier, inc=1, device_id=(other // n_blk, other % n_blk), device_id_type=MESH
        )
        return carry

    lax.fori_loop(1, count, greet, 0)

    base = x * 3
    loads[0].wait()
    p0, p1, p2 = partner_ref[0], partner_ref[1], partner_ref[2]
    sides = [jnp.minimum(jnp.maximum(p - 2, 0), 1) - x for p in (p0, p1, p2)]
    away0, away1, away2 = (side * side for side in sides)
    first_pos = jnp.minimum(away1 + 2 * away2, 2)
    pos1 = away0
    pos2 = 2 - away2
    shift = away0 * p1 + (1 - away0) * p0 - base - pos1
    swapped = jnp.minimum(shift * shift, 1)
    place = (1 - away0, jnp.minimum(away0 + 2 * away2, 2), 2 - 2 * away2)

    for p, value in enumerate((first_pos, pos1, pos2)):
        pos_ref[p] = value
    for p, value in enumerate((0, 1 + swapped, 2 - swapped)):
        pair_ref[p] = value
    saved = (n_ref, d_ref, inv_ref, slope_ref)

    def exchange(step):
        return pltpu.make_async_remote_copy(
            src_ref=sent_ref.at[step, 0],
            dst_ref=take_ref.at[step],
            send_sem=give_sem.at[step],
            recv_sem=take_sem.at[step],
            device_id=(1 - x, b),
            device_id_type=MESH,
        )

    def half_copy(layer):
        return pltpu.make_async_remote_copy(
            src_ref=half_ref.at[layer],
            dst_ref=half_in_ref.at[layer],
            send_sem=half_sem.at[layer],
            recv_sem=half_in_sem.at[layer],
            device_id=(x, b + 1 - 2 * core),
            device_id_type=MESH,
        )

    half_rows = width // 2
    eighth = half_rows // 8

    def send_half(layer):
        def columns(c):
            return n_ref[layer, :, pl.ds(pl.multiple_of(c * half_rows, half_rows), half_rows)]

        d = d_ref[layer]
        half_ref[layer] = dot(columns(1 - core), d, 0, 0).astype(BF16)
        half_copy(layer).start()
        own_ref[layer] = dot(columns(core), d, 0, 0)

    def direct_copy(layer, r):
        px = 1 - x if r >= 2 else x
        py = 1 - y if r % 2 else y
        return pltpu.make_async_remote_copy(
            src_ref=part_ref.at[layer, px, py],
            dst_ref=direct_in_ref.at[layer, r - 1],
            send_sem=direct_sem.at[layer, r - 1],
            recv_sem=direct_in_sem.at[layer, r - 1],
            device_id=(px, 4 * z + 2 * py + core),
            device_id_type=MESH,
        )

    def part_copy(layer, piece, hop):
        along_x = hop == 1
        near, far = y, x
        if hop == 0:
            src, dst = part_ref.at[layer, piece, 1 - near], part_in_ref.at[layer, piece]
        else:
            src, dst = quad_ref.at[layer, piece, 1 - far], quad_in_ref.at[layer, piece]
        return pltpu.make_async_remote_copy(
            src_ref=src,
            dst_ref=dst,
            send_sem=part_sem.at[layer, piece, hop],
            recv_sem=part_in_sem.at[layer, piece, hop],
            device_id=(1 - x, b) if along_x else (x, b + 2 - 4 * y),
            device_id_type=MESH,
        )

    def send_parts(layer):
        half_copy(layer).wait_recv()
        total = own_ref[layer] + half_in_ref[layer].astype(F32)
        part_ref[layer] = total.astype(BF16).reshape(2, 2, 2, eighth, width)
        if layer < 2:
            for r in (3, 2, 1):
                direct_copy(layer, r).start()
        else:
            for piece in range(2):
                part_copy(layer, piece, 0).start()

    def send_quads(layer):
        for piece in range(2):
            part_copy(layer, piece, 0).wait_recv()
            total = part_ref[layer, piece, y].astype(F32)
            total = total + part_in_ref[layer, piece].astype(F32)
            quad_ref[layer, piece] = total.astype(BF16)
            part_copy(layer, piece, 1).start()

    def piece_copy(layer, t):
        if layer < 2:
            c = 32 * layer + 16 * core + 8 * x + 4 * y + t
        else:
            c = 32 * layer + 16 * core + 8 * (t // 2) + 4 * y + 2 * x + t % 2
        dest = c // 3
        copy = pltpu.make_async_remote_copy(
            src_ref=piece_ref.at[layer, t],
            dst_ref=final_ref.at[c % 3, z],
            send_sem=piece_sem.at[layer, t],
            recv_sem=final_sem.at[c % 3, z],
            device_id=(dest // n_blk, dest % n_blk),
            device_id_type=MESH,
        )
        return c, dest, copy

    def send_pieces(layer):
        if layer < 2:
            total = part_ref[layer, x, y].astype(F32)
            for r in (1, 2, 3):
                direct_copy(layer, r).wait_recv()
                total = total + direct_in_ref[layer, r - 1].astype(F32)
            piece_ref[layer] = total.astype(BF16).reshape(4, CHUNK, width)
        else:
            for piece in range(2):
                part_copy(layer, piece, 1).wait_recv()
                total = quad_ref[layer, piece, x].astype(F32)
                total = total + quad_in_ref[layer, piece].astype(F32)
                piece_ref[layer, pl.ds(2 * piece, 2)] = total.astype(BF16).reshape(
                    2, CHUNK, width
                )
        for t in range(4):
            c, dest, copy = piece_copy(layer, t)

            @pl.when(dest != me)
            def _():
                copy.start()

            @pl.when(dest == me)
            def _():
                final_ref[c % 3, z] = piece_ref[layer, t]

    def phase_one(p, carry):
        mix = mixing_matrix(basis_ref[...], pos_ref[p])
        mix_ref[p] = mix
        mixed = dot(mix, state_ref[pos_ref[p]])
        mixed_ref[p] = mixed
        first = forward(mixed, w_ref, 0, p, saved)
        first_ref[p] = first
        second = forward(first, w_ref, 1, p, saved)
        second_ref[p] = second
        sent_ref[0, p] = second.astype(BF16)

        @pl.when(p == 0)
        def _():
            pl.semaphore_wait(barrier, count - 1)
            exchange(0).start()

        return carry

    def reverse(step, p):
        @pl.when(p == 0)
        def _():
            exchange(step).wait_recv()
            rev_ref[...] = take_ref[step]

        @pl.when(p > 0)
        def _():
            rev_ref[...] = sent_ref[step, pair_ref[p]]

        return flip(rev_ref[...].astype(F32))

    def phase_two(i, carry):
        p = 1 - i + 3 * (i // 2)
        summed = second_ref[p] + reverse(0, p)
        final = forward(summed, w_ref, 2, p, saved)
        eout_ref[p] = final.astype(BF16)
        g = backward(summed, w_ref, 2, p, saved, cot_ref[pos_ref[p]].astype(F32))
        gs_ref[p] = g
        sent_ref[1, p] = g.astype(BF16)

        @pl.when(p == 0)
        def _():
            exchange(1).start()

        return carry

    def phase_three(i, carry):
        p = (i + 1) % 3
        g = gs_ref[p] + reverse(1, p)
        g = backward(first_ref[p], w_ref, 1, p, saved, g)
        g = backward(mixed_ref[p], w_ref, 0, p, saved, g)
        gm_ref[...] = g.astype(BF16)

        @pl.when(p > 0)
        def _():
            gout_ref[p] = dot(mix_ref[p], gm_ref[...], 0, 0).astype(BF16)

        @pl.when(p == 2)
        def _():
            send_parts(2)

        return carry

    for load in loads[1:5]:
        load.wait()
    lax.fori_loop(0, 3, phase_one, 0)
    for load in loads[5:]:
        load.wait()
    lax.fori_loop(0, 3, phase_two, 0)
    send_half(2)
    lax.fori_loop(0, 3, phase_three, 0)
    lax.fori_loop(0, 2, lambda i, carry: (send_half(i), carry)[1], 0)
    send_parts(0)
    send_quads(2)
    send_parts(1)
    gout_ref[0] = dot(mix_ref[0], gm_ref[...], 0, 0).astype(BF16)

    for k in range(3):
        out_ref[k] = eout_ref[place[k]]
        gstate_ref[k] = gout_ref[place[k]]

    send_pieces(0)
    send_pieces(2)
    send_pieces(1)

    for j in range(3):
        c = 3 * me + j
        i = c % 32
        from_y = (i // 4) % 2
        from_x = (i // 8) % 2 + (c // 64) * ((i // 2) % 2 - (i // 8) % 2)
        for plane in range(4):
            source = from_x * n_blk + 4 * plane + 2 * from_y + i // 16

            @pl.when(source != me)
            def _():
                pltpu.make_async_remote_copy(
                    src_ref=piece_ref.at[0, 0],
                    dst_ref=final_ref.at[j, plane],
                    send_sem=piece_sem.at[0, 0],
                    recv_sem=final_sem.at[j, plane],
                    device_id=(1 - x, b),
                    device_id_type=MESH,
                ).wait_recv()

    for j in range(3):
        total = final_ref[j, 0].astype(F32)
        for plane in range(1, 4):
            total = total + final_ref[j, plane].astype(F32)
        wgrad_ref[j] = total

    for step in range(2):
        exchange(step).wait_send()
    for layer in range(3):
        half_copy(layer).wait_send()
        if layer < 2:
            for r in (1, 2, 3):
                direct_copy(layer, r).wait_send()
        else:
            for piece in range(2):
                for hop in range(2):
                    part_copy(layer, piece, hop).wait_send()
        for t in range(4):
            c, dest, copy = piece_copy(layer, t)

            @pl.when(dest != me)
            def _():
                copy.wait_send()


def finish(
    scale, out_ref, gstate_ref, wgrad_ref, out_hbm, gstate_hbm, total_hbm, total_ref, sems
):
    copies = [
        pltpu.make_async_copy(out_ref, out_hbm, sems.at[0]),
        pltpu.make_async_copy(gstate_ref, gstate_hbm, sems.at[1]),
        pltpu.make_async_copy(total_ref, total_hbm, sems.at[2]),
    ]
    copies[0].start()
    copies[1].start()
    total_ref[...] = wgrad_ref[...] * scale
    copies[2].start()
    for copy in copies:
        copy.wait()


def local_fast(n_blk, edge_state, basis, weights, partner, cotangent):
    rows, width = edge_state.shape
    total_edges = rows * 2 * n_blk
    half = width // 2
    blocks = (rows // BLOCK, BLOCK, width)
    vmem = pl.BlockSpec(memory_space=pltpu.VMEM)
    dma = pltpu.SemaphoreType.DMA
    out, gstate, wgrad = pl.pallas_call(
        functools.partial(kernel, n_blk),
        out_shape=(
            jax.ShapeDtypeStruct(blocks, BF16),
            jax.ShapeDtypeStruct(blocks, BF16),
            jax.ShapeDtypeStruct((3, CHUNK, width), F32),
        ),
        in_specs=[pl.BlockSpec(memory_space=pltpu.HBM)] * 5,
        out_specs=(vmem, vmem, vmem),
        scratch_shapes=[
            pltpu.SMEM(partner.shape, jnp.int32),
            pltpu.VMEM(blocks, BF16),
            pltpu.VMEM((NBR, NBR, basis.shape[0]), BF16),
            pltpu.VMEM(weights.shape, BF16),
            pltpu.VMEM(blocks, BF16),
            pltpu.VMEM((3, rows, width), BF16),
            pltpu.VMEM((3, rows, width), BF16),
            pltpu.VMEM(blocks, BF16),
            pltpu.VMEM(blocks, BF16),
            pltpu.VMEM((2, 3, BLOCK, width), BF16),
            pltpu.VMEM((BLOCK, width), BF16),
            pltpu.VMEM((BLOCK, width), BF16),
            pltpu.VMEM((3, BLOCK, BLOCK), BF16),
            pltpu.VMEM(blocks, F32),
            pltpu.VMEM(blocks, F32),
            pltpu.VMEM(blocks, F32),
            pltpu.VMEM(blocks, F32),
            pltpu.VMEM((3, 3, BLOCK, 1), F32),
            pltpu.VMEM((3, 3, BLOCK, width), F32),
            pltpu.SMEM((3,), jnp.int32),
            pltpu.SMEM((3,), jnp.int32),
            pltpu.VMEM((2, BLOCK, width), BF16),
            pltpu.VMEM((3, half, width), BF16),
            pltpu.VMEM((3, half, width), F32),
            pltpu.VMEM((3, half, width), BF16),
            pltpu.VMEM((3, 2, 2, 2, half // 8, width), BF16),
            pltpu.VMEM((3, 2, 2, half // 8, width), BF16),
            pltpu.VMEM((2, 3, 2, half // 8, width), BF16),
            pltpu.VMEM((3, 2, 2, half // 8, width), BF16),
            pltpu.VMEM((3, 2, half // 8, width), BF16),
            pltpu.VMEM((3, 4, CHUNK, width), BF16),
            pltpu.VMEM((3, 4, CHUNK, width), BF16),
            dma((7,)),
            dma((2,)),
            dma((2,)),
            dma((3,)),
            dma((3,)),
            dma((3, 2, 2)),
            dma((3, 2, 2)),
            dma((2, 3)),
            dma((2, 3)),
            dma((3, 4)),
            dma((3, 4)),
        ],
        compiler_params=pltpu.CompilerParams(
            collective_id=0, has_side_effects=True, vmem_limit_bytes=36 * 2**20
        ),
    )(
        *[
            pltpu.with_memory_space_constraint(array, pltpu.HBM)
            for array in (
                partner,
                edge_state.reshape(blocks),
                basis.transpose(1, 2, 0),
                weights,
                cotangent.reshape(blocks),
            )
        ]
    )
    hbm = pl.BlockSpec(memory_space=pltpu.HBM)
    out, gstate, wgrad = pl.pallas_call(
        functools.partial(finish, 1.0 / math.sqrt(total_edges)),
        out_shape=(
            jax.ShapeDtypeStruct(blocks, BF16),
            jax.ShapeDtypeStruct(blocks, BF16),
            jax.ShapeDtypeStruct((3, CHUNK, width), F32),
        ),
        in_specs=[vmem, vmem, vmem],
        out_specs=(hbm, hbm, hbm),
        scratch_shapes=[pltpu.VMEM((3, CHUNK, width), F32), dma((3,))],
        compiler_params=pltpu.CompilerParams(vmem_limit_bytes=8 * 2**20),
    )(out, gstate, wgrad)
    return (
        out.reshape(rows, width),
        gstate.reshape(rows, width),
        wgrad.reshape(3 * CHUNK, width),
    )


def norm_rows(hidden):
    return hidden * lax.rsqrt(jnp.mean(hidden * hidden, axis=-1, keepdims=True) + 1e-06)


def layer_forward(hidden, weight):
    normed = norm_rows(hidden).astype(jnp.bfloat16)
    preact = jnp.dot(normed, weight, preferred_element_type=jnp.float32)
    return (hidden + jax.nn.silu(preact), normed, preact)


def layer_backward(hidden, normed, preact, weight, upstream):
    sigma = jax.nn.sigmoid(preact)
    grad_pre = (upstream * sigma * (1.0 + preact * (1.0 - sigma))).astype(jnp.bfloat16)
    grad_weight = lax.dot_general(
        normed, grad_pre, (((0,), (0,)), ((), ())), preferred_element_type=jnp.float32
    )
    grad_normed = lax.dot_general(
        grad_pre, weight, (((1,), (1,)), ((), ())), preferred_element_type=jnp.float32
    )
    inverse = lax.rsqrt(jnp.mean(hidden * hidden, axis=-1, keepdims=True) + 1e-06)
    unit = hidden * inverse
    inner = jnp.mean(grad_normed * unit, axis=-1, keepdims=True)
    return (upstream + inverse * (grad_normed - unit * inner), grad_weight)


def flip_rows(blocks):
    count, height, width = blocks.shape
    return blocks.reshape(count, height // 2, 2, width)[:, :, ::-1, :].reshape(count, height, width)


def route_plan(partner, own_index, group_count):
    block_count = partner.shape[0]
    target = partner // block_count
    remote = partner % block_count
    order = jnp.arange(block_count)
    same = target[:, None] == target[None, :]
    send_rank = jnp.sum(same & (order[None, :] < order[:, None]), axis=1)
    recv_rank = jnp.sum(same & (remote[None, :] < remote[:, None]), axis=1)
    local_pair = target == own_index
    slots = jnp.arange(group_count * CAP)
    send_slot = target * CAP + send_rank
    recv_slot = target * CAP + recv_rank
    pack_matrix = ((slots[:, None] == send_slot[None, :]) & ~local_pair[None, :]).astype(
        jnp.bfloat16
    )
    unpack_matrix = ((recv_slot[:, None] == slots[None, :]) & ~local_pair[:, None]).astype(
        jnp.bfloat16
    )
    return (pack_matrix, unpack_matrix, local_pair)


def pack_blocks(values, pack_matrix, block_count):
    blocks = values.reshape(block_count, -1, values.shape[1])
    return jnp.einsum("sn,nrd->srd", pack_matrix, blocks, preferred_element_type=jnp.bfloat16)


def unpack_blocks(arrived, unpack_matrix, local_pair, values, block_count):
    blocks = values.reshape(block_count, -1, values.shape[1])
    distant = jnp.einsum("ns,srd->nrd", unpack_matrix, arrived, preferred_element_type=jnp.bfloat16)
    joined = jnp.where(local_pair[:, None, None], blocks, distant)
    return flip_rows(joined).reshape(values.shape)


def local(edge_state, basis, weights, partner, cotangent):
    row_count, width = edge_state.shape
    block_count = partner.shape[0]
    group_count = lax.axis_size("grp")
    own_index = lax.axis_index("grp")
    total_edges = row_count * group_count * lax.axis_size("blk")
    pack_matrix, unpack_matrix, local_pair = route_plan(partner, own_index, group_count)
    mixed = jnp.einsum(
        "aij,ajd->aid",
        basis,
        edge_state.reshape(-1, NBR, width),
        preferred_element_type=jnp.float32,
    ).reshape(row_count, width)
    first, normed_one, pre_one = layer_forward(mixed, weights[0])
    second, normed_two, pre_two = layer_forward(first, weights[1])
    sent = second.astype(jnp.bfloat16)
    arrived = lax.all_to_all(
        pack_blocks(sent, pack_matrix, block_count), "grp", split_axis=0, concat_axis=0, tiled=True
    )
    reversed_state = unpack_blocks(arrived, unpack_matrix, local_pair, sent, block_count)
    summed = second + reversed_state.astype(jnp.float32)
    final, normed_three, pre_three = layer_forward(summed, weights[2])
    edge_out = final.astype(jnp.bfloat16)
    grad_summed, grad_three = layer_backward(
        summed, normed_three, pre_three, weights[2], cotangent.astype(jnp.float32)
    )
    grad_reversed = grad_summed.astype(jnp.bfloat16)
    returned = lax.all_to_all(
        pack_blocks(grad_reversed, pack_matrix, block_count),
        "grp",
        split_axis=0,
        concat_axis=0,
        tiled=True,
    )
    grad_sent = unpack_blocks(returned, unpack_matrix, local_pair, grad_reversed, block_count)
    grad_second = grad_summed + grad_sent.astype(jnp.float32)
    grad_first, grad_two = layer_backward(first, normed_two, pre_two, weights[1], grad_second)
    grad_mixed, grad_one = layer_backward(mixed, normed_one, pre_one, weights[0], grad_first)
    grad_round = grad_mixed.astype(jnp.bfloat16).reshape(-1, NBR, width)
    grad_state = (
        jnp.einsum("aij,aid->ajd", basis, grad_round, preferred_element_type=jnp.float32)
        .reshape(row_count, width)
        .astype(jnp.bfloat16)
    )
    local_grads = jnp.concatenate([grad_one, grad_two, grad_three], axis=0)
    group_part = lax.psum_scatter(
        local_grads.astype(jnp.bfloat16), "grp", scatter_dimension=0, tiled=True
    ).astype(jnp.float32)
    summed_grads = lax.psum_scatter(group_part, "blk", scatter_dimension=0, tiled=True)
    weight_grad = summed_grads * (1.0 / math.sqrt(total_edges))
    return (edge_out, grad_state, weight_grad)


def solution(mesh):
    spread = P(("grp", "blk"))
    wide = P(("grp", "blk"), None)
    in_specs = (wide, P(("grp", "blk"), None, None), P(), spread, wide)
    body = local
    if mesh.shape["grp"] == 2 and mesh.shape["blk"] == 16:
        body = functools.partial(local_fast, mesh.shape["blk"])
    return jax.shard_map(
        body, mesh=mesh, in_specs=in_specs, out_specs=(wide, wide, wide), check_vma=False
    )
```

```python
import functools
import math

import jax
import jax.numpy as jnp
from jax import lax
from jax.experimental import pallas as pl
from jax.experimental.pallas import tpu as pltpu
from jax.sharding import PartitionSpec as P

NBR = 16
CAP = 1
BLOCK = 128
CHUNK = 16
EPS = 1e-06
MESH = pl.DeviceIdType.MESH
BF16 = jnp.bfloat16
F32 = jnp.float32


def dot(a, b, ca=1, cb=0):
    return lax.dot_general(a, b, (((ca,), (cb,)), ((), ())), preferred_element_type=F32)


def inverse_rms(h):
    return lax.rsqrt(jnp.mean(h * h, axis=-1, keepdims=True) + EPS)


def flip(x):
    rows = x.shape[0]
    even = lax.broadcasted_iota(jnp.int32, x.shape, 0) % 2 == 0
    return jnp.where(even, pltpu.roll(x, rows - 1, 0), pltpu.roll(x, 1, 0))


def mixing_matrix(basis, block):
    flat = basis.reshape(NBR * NBR, basis.shape[2])
    rows = BLOCK

    def iota(shape, dim):
        return lax.broadcasted_iota(jnp.int32, shape, dim)

    def mask(hit):
        return hit.astype(F32).astype(BF16)

    atom_shape = (rows, basis.shape[2])
    atom = block * (BLOCK // NBR) + iota(atom_shape, 0) // NBR
    pick = mask(atom == iota(atom_shape, 1))
    own = dot(pick, flat, 1, 1)
    own_shape = (rows, NBR * NBR)
    own = jnp.where(iota(own_shape, 0) % NBR == iota(own_shape, 1) // NBR, own, 0.0).astype(BF16)
    spread_shape = (NBR * NBR, rows)
    spread = mask(iota(spread_shape, 0) % NBR == iota(spread_shape, 1) % NBR)
    wide = dot(own, spread)
    same = iota((rows, rows), 0) // NBR == iota((rows, rows), 1) // NBR
    return jnp.where(same, wide, 0.0).astype(BF16)


def forward(h, w_ref, layer, p, saved):
    n_ref, _, inv_ref, slope_ref = saved
    inv = inverse_rms(h)
    normed = (h * inv).astype(BF16)
    n_ref[layer, pl.ds(p * BLOCK, BLOCK), :] = normed
    inv_ref[layer, p] = inv
    pre = dot(normed, w_ref[layer])
    s = 0.5 * jnp.tanh(0.5 * pre) + 0.5
    slope_ref[layer, p] = s * (1.0 + pre * (1.0 - s))
    return h + pre * s


def backward(h, w_ref, layer, p, saved, g):
    _, d_ref, inv_ref, slope_ref = saved
    inv = inv_ref[layer, p]
    dpre = (g * slope_ref[layer, p]).astype(BF16)
    d_ref[layer, pl.ds(p * BLOCK, BLOCK), :] = dpre
    dn = dot(dpre, w_ref[layer], 1, 1)
    u = h * inv
    inner = jnp.mean(dn * u, axis=-1, keepdims=True)
    return g + inv * (dn - u * inner)


def kernel(
    n_blk,
    partner_hbm,
    state_hbm,
    basis_hbm,
    w_hbm,
    cot_hbm,
    out_ref,
    gstate_ref,
    wgrad_ref,
    partner_ref,
    state_ref,
    basis_ref,
    w_ref,
    cot_ref,
    n_ref,
    d_ref,
    eout_ref,
    gout_ref,
    sent_ref,
    rev_ref,
    gm_ref,
    mix_ref,
    mixed_ref,
    first_ref,
    second_ref,
    gs_ref,
    inv_ref,
    slope_ref,
    pos_ref,
    pair_ref,
    take_ref,
    half_ref,
    own_ref,
    half_in_ref,
    part_ref,
    part_in_ref,
    direct_in_ref,
    quad_ref,
    quad_in_ref,
    piece_ref,
    final_ref,
    in_sem,
    give_sem,
    take_sem,
    half_sem,
    half_in_sem,
    part_sem,
    part_in_sem,
    direct_sem,
    direct_in_sem,
    piece_sem,
    final_sem,
):
    x = lax.axis_index("grp")
    b = lax.axis_index("blk")
    me = x * n_blk + b
    core = b % 2
    y = (b // 2) % 2
    z = b // 4
    count = 2 * n_blk
    width = w_ref.shape[2]

    loads = [
        pltpu.make_async_copy(src, dst, in_sem.at[number])
        for number, (src, dst) in enumerate(
            [
                (partner_hbm, partner_ref),
                (basis_hbm, basis_ref),
                (state_hbm, state_ref),
                (w_hbm.at[0], w_ref.at[0]),
                (w_hbm.at[1], w_ref.at[1]),
                (w_hbm.at[2], w_ref.at[2]),
                (cot_hbm, cot_ref),
            ]
        )
    ]
    for load in loads:
        load.start()

    barrier = pltpu.get_barrier_semaphore()

    def greet(step, carry):
        other = (me + step) % count
        pl.semaphore_signal(
            barrier, inc=1, device_id=(other // n_blk, other % n_blk), device_id_type=MESH
        )
        return carry

    lax.fori_loop(1, count, greet, 0)

    base = x * 3
    loads[0].wait()
    p0, p1, p2 = partner_ref[0], partner_ref[1], partner_ref[2]
    sides = [jnp.minimum(jnp.maximum(p - 2, 0), 1) - x for p in (p0, p1, p2)]
    away0, away1, away2 = (side * side for side in sides)
    first_pos = jnp.minimum(away1 + 2 * away2, 2)
    pos1 = away0
    pos2 = 2 - away2
    shift = away0 * p1 + (1 - away0) * p0 - base - pos1
    swapped = jnp.minimum(shift * shift, 1)
    place = (1 - away0, jnp.minimum(away0 + 2 * away2, 2), 2 - 2 * away2)

    for p, value in enumerate((first_pos, pos1, pos2)):
        pos_ref[p] = value
    for p, value in enumerate((0, 1 + swapped, 2 - swapped)):
        pair_ref[p] = value
    saved = (n_ref, d_ref, inv_ref, slope_ref)

    def exchange(step):
        return pltpu.make_async_remote_copy(
            src_ref=sent_ref.at[step, 0],
            dst_ref=take_ref.at[step],
            send_sem=give_sem.at[step],
            recv_sem=take_sem.at[step],
            device_id=(1 - x, b),
            device_id_type=MESH,
        )

    def half_copy(layer):
        return pltpu.make_async_remote_copy(
            src_ref=half_ref.at[layer],
            dst_ref=half_in_ref.at[layer],
            send_sem=half_sem.at[layer],
            recv_sem=half_in_sem.at[layer],
            device_id=(x, b + 1 - 2 * core),
            device_id_type=MESH,
        )

    half_rows = width // 2
    eighth = half_rows // 8

    def send_half(layer):
        def columns(c):
            return n_ref[layer, :, pl.ds(pl.multiple_of(c * half_rows, half_rows), half_rows)]

        d = d_ref[layer]
        half_ref[layer] = dot(columns(1 - core), d, 0, 0).astype(BF16)
        half_copy(layer).start()
        own_ref[layer] = dot(columns(core), d, 0, 0)

    def row_group(layer, px, py, pc):
        first, second = (2 - layer) // 2, layer % 2
        turn = first * px * (1 - pc) + second * (1 - (px - pc) * (px - pc))
        return py + turn * (1 - 2 * py)

    def direct_copy(layer, r):
        px = 1 - x if r >= 2 else x
        py = 1 - y if r % 2 else y
        return pltpu.make_async_remote_copy(
            src_ref=part_ref.at[layer, px, row_group(layer, px, py, core)],
            dst_ref=direct_in_ref.at[layer, r - 1],
            send_sem=direct_sem.at[layer, r - 1],
            recv_sem=direct_in_sem.at[layer, r - 1],
            device_id=(px, 4 * z + 2 * py + core),
            device_id_type=MESH,
        )

    def part_copy(layer, piece, hop):
        along_x = hop == 1
        near, far = y, x
        if hop == 0:
            src, dst = part_ref.at[layer, piece, 1 - near], part_in_ref.at[layer, piece]
        else:
            src, dst = quad_ref.at[layer, piece, 1 - far], quad_in_ref.at[layer, piece]
        return pltpu.make_async_remote_copy(
            src_ref=src,
            dst_ref=dst,
            send_sem=part_sem.at[layer, piece, hop],
            recv_sem=part_in_sem.at[layer, piece, hop],
            device_id=(1 - x, b) if along_x else (x, b + 2 - 4 * y),
            device_id_type=MESH,
        )

    def send_parts(layer):
        half_copy(layer).wait_recv()
        total = own_ref[layer] + half_in_ref[layer].astype(F32)
        part_ref[layer] = total.astype(BF16).reshape(2, 2, 2, eighth, width)
        if layer < 2:
            for r in (3, 2, 1):
                direct_copy(layer, r).start()
        else:
            for piece in range(2):
                part_copy(layer, piece, 0).start()

    def send_quads(layer):
        for piece in range(2):
            part_copy(layer, piece, 0).wait_recv()
            total = part_ref[layer, piece, y].astype(F32)
            total = total + part_in_ref[layer, piece].astype(F32)
            quad_ref[layer, piece] = total.astype(BF16)
            part_copy(layer, piece, 1).start()

    def piece_copy(layer, t):
        if layer < 2:
            c = 32 * layer + 16 * core + 8 * x + 4 * row_group(layer, x, y, core) + t
        else:
            c = 32 * layer + 16 * core + 8 * (t // 2) + 4 * y + 2 * x + t % 2
        dest = c // 3
        copy = pltpu.make_async_remote_copy(
            src_ref=piece_ref.at[layer, t],
            dst_ref=final_ref.at[c % 3, z],
            send_sem=piece_sem.at[layer, t],
            recv_sem=final_sem.at[c % 3, z],
            device_id=(dest // n_blk, dest % n_blk),
            device_id_type=MESH,
        )
        return c, dest, copy

    def send_pieces(layer):
        if layer < 2:
            total = part_ref[layer, x, row_group(layer, x, y, core)].astype(F32)
            for r in (1, 2, 3):
                direct_copy(layer, r).wait_recv()
                total = total + direct_in_ref[layer, r - 1].astype(F32)
            piece_ref[layer] = total.astype(BF16).reshape(4, CHUNK, width)
        else:
            for piece in range(2):
                part_copy(layer, piece, 1).wait_recv()
                total = quad_ref[layer, piece, x].astype(F32)
                total = total + quad_in_ref[layer, piece].astype(F32)
                piece_ref[layer, pl.ds(2 * piece, 2)] = total.astype(BF16).reshape(
                    2, CHUNK, width
                )
        for t in range(4):
            c, dest, copy = piece_copy(layer, t)

            @pl.when(dest != me)
            def _():
                copy.start()

            @pl.when(dest == me)
            def _():
                final_ref[c % 3, z] = piece_ref[layer, t]

    def phase_one(p, carry):
        mix = mixing_matrix(basis_ref[...], pos_ref[p])
        mix_ref[p] = mix
        mixed = dot(mix, state_ref[pos_ref[p]])
        mixed_ref[p] = mixed
        first = forward(mixed, w_ref, 0, p, saved)
        first_ref[p] = first
        second = forward(first, w_ref, 1, p, saved)
        second_ref[p] = second
        sent_ref[0, p] = second.astype(BF16)

        @pl.when(p == 0)
        def _():
            pl.semaphore_wait(barrier, count - 1)
            exchange(0).start()

        return carry

    def reverse(step, p):
        @pl.when(p == 0)
        def _():
            exchange(step).wait_recv()
            rev_ref[...] = take_ref[step]

        @pl.when(p > 0)
        def _():
            rev_ref[...] = sent_ref[step, pair_ref[p]]

        return flip(rev_ref[...].astype(F32))

    def phase_two(i, carry):
        p = 1 - i + 3 * (i // 2)
        summed = second_ref[p] + reverse(0, p)
        final = forward(summed, w_ref, 2, p, saved)
        eout_ref[p] = final.astype(BF16)
        g = backward(summed, w_ref, 2, p, saved, cot_ref[pos_ref[p]].astype(F32))
        gs_ref[p] = g
        sent_ref[1, p] = g.astype(BF16)

        @pl.when(p == 0)
        def _():
            exchange(1).start()

        return carry

    def phase_three(i, carry):
        p = (i + 1) % 3
        g = gs_ref[p] + reverse(1, p)
        g = backward(first_ref[p], w_ref, 1, p, saved, g)
        g = backward(mixed_ref[p], w_ref, 0, p, saved, g)
        gm_ref[...] = g.astype(BF16)

        @pl.when(p > 0)
        def _():
            gout_ref[p] = dot(mix_ref[p], gm_ref[...], 0, 0).astype(BF16)

        @pl.when(p == 2)
        def _():
            send_parts(2)

        return carry

    for load in loads[1:5]:
        load.wait()
    lax.fori_loop(0, 3, phase_one, 0)
    for load in loads[5:]:
        load.wait()
    lax.fori_loop(0, 3, phase_two, 0)
    send_half(2)
    lax.fori_loop(0, 3, phase_three, 0)
    lax.fori_loop(0, 2, lambda i, carry: (send_half(i), carry)[1], 0)
    send_parts(0)
    send_quads(2)
    send_parts(1)
    gout_ref[0] = dot(mix_ref[0], gm_ref[...], 0, 0).astype(BF16)
    send_pieces(2)
    send_pieces(0)

    for k in range(3):
        out_ref[k] = eout_ref[place[k]]
        gstate_ref[k] = gout_ref[place[k]]

    send_pieces(1)

    for j in range(3):
        c = 3 * me + j
        i = c % 32
        from_y = row_group(c // 32, (i // 8) % 2, (i // 4) % 2, i // 16)
        from_x = (i // 8) % 2 + (c // 64) * ((i // 2) % 2 - (i // 8) % 2)
        for plane in range(4):
            source = from_x * n_blk + 4 * plane + 2 * from_y + i // 16

            @pl.when(source != me)
            def _():
                pltpu.make_async_remote_copy(
                    src_ref=piece_ref.at[0, 0],
                    dst_ref=final_ref.at[j, plane],
                    send_sem=piece_sem.at[0, 0],
                    recv_sem=final_sem.at[j, plane],
                    device_id=(1 - x, b),
                    device_id_type=MESH,
                ).wait_recv()

    for j in range(3):
        total = final_ref[j, 0].astype(F32)
        for plane in range(1, 4):
            total = total + final_ref[j, plane].astype(F32)
        wgrad_ref[j] = total

    for step in range(2):
        exchange(step).wait_send()
    for layer in range(3):
        half_copy(layer).wait_send()
        if layer < 2:
            for r in (1, 2, 3):
                direct_copy(layer, r).wait_send()
        else:
            for piece in range(2):
                for hop in range(2):
                    part_copy(layer, piece, hop).wait_send()
        for t in range(4):
            c, dest, copy = piece_copy(layer, t)

            @pl.when(dest != me)
            def _():
                copy.wait_send()


def finish(
    scale, out_ref, gstate_ref, wgrad_ref, out_hbm, gstate_hbm, total_hbm, total_ref, sems
):
    copies = [
        pltpu.make_async_copy(out_ref, out_hbm, sems.at[0]),
        pltpu.make_async_copy(gstate_ref, gstate_hbm, sems.at[1]),
        pltpu.make_async_copy(total_ref, total_hbm, sems.at[2]),
    ]
    copies[0].start()
    copies[1].start()
    total_ref[...] = wgrad_ref[...] * scale
    copies[2].start()
    for copy in copies:
        copy.wait()


def local_fast(n_blk, edge_state, basis, weights, partner, cotangent):
    rows, width = edge_state.shape
    total_edges = rows * 2 * n_blk
    half = width // 2
    blocks = (rows // BLOCK, BLOCK, width)
    vmem = pl.BlockSpec(memory_space=pltpu.VMEM)
    dma = pltpu.SemaphoreType.DMA
    out, gstate, wgrad = pl.pallas_call(
        functools.partial(kernel, n_blk),
        out_shape=(
            jax.ShapeDtypeStruct(blocks, BF16),
            jax.ShapeDtypeStruct(blocks, BF16),
            jax.ShapeDtypeStruct((3, CHUNK, width), F32),
        ),
        in_specs=[pl.BlockSpec(memory_space=pltpu.HBM)] * 5,
        out_specs=(vmem, vmem, vmem),
        scratch_shapes=[
            pltpu.SMEM(partner.shape, jnp.int32),
            pltpu.VMEM(blocks, BF16),
            pltpu.VMEM((NBR, NBR, basis.shape[0]), BF16),
            pltpu.VMEM(weights.shape, BF16),
            pltpu.VMEM(blocks, BF16),
            pltpu.VMEM((3, rows, width), BF16),
            pltpu.VMEM((3, rows, width), BF16),
            pltpu.VMEM(blocks, BF16),
            pltpu.VMEM(blocks, BF16),
            pltpu.VMEM((2, 3, BLOCK, width), BF16),
            pltpu.VMEM((BLOCK, width), BF16),
            pltpu.VMEM((BLOCK, width), BF16),
            pltpu.VMEM((3, BLOCK, BLOCK), BF16),
            pltpu.VMEM(blocks, F32),
            pltpu.VMEM(blocks, F32),
            pltpu.VMEM(blocks, F32),
            pltpu.VMEM(blocks, F32),
            pltpu.VMEM((3, 3, BLOCK, 1), F32),
            pltpu.VMEM((3, 3, BLOCK, width), F32),
            pltpu.SMEM((3,), jnp.int32),
            pltpu.SMEM((3,), jnp.int32),
            pltpu.VMEM((2, BLOCK, width), BF16),
            pltpu.VMEM((3, half, width), BF16),
            pltpu.VMEM((3, half, width), F32),
            pltpu.VMEM((3, half, width), BF16),
            pltpu.VMEM((3, 2, 2, 2, half // 8, width), BF16),
            pltpu.VMEM((3, 2, 2, half // 8, width), BF16),
            pltpu.VMEM((2, 3, 2, half // 8, width), BF16),
            pltpu.VMEM((3, 2, 2, half // 8, width), BF16),
            pltpu.VMEM((3, 2, half // 8, width), BF16),
            pltpu.VMEM((3, 4, CHUNK, width), BF16),
            pltpu.VMEM((3, 4, CHUNK, width), BF16),
            dma((7,)),
            dma((2,)),
            dma((2,)),
            dma((3,)),
            dma((3,)),
            dma((3, 2, 2)),
            dma((3, 2, 2)),
            dma((2, 3)),
            dma((2, 3)),
            dma((3, 4)),
            dma((3, 4)),
        ],
        compiler_params=pltpu.CompilerParams(
            collective_id=0, has_side_effects=True, vmem_limit_bytes=36 * 2**20
        ),
    )(
        *[
            pltpu.with_memory_space_constraint(array, pltpu.HBM)
            for array in (
                partner,
                edge_state.reshape(blocks),
                basis.transpose(1, 2, 0),
                weights,
                cotangent.reshape(blocks),
            )
        ]
    )
    hbm = pl.BlockSpec(memory_space=pltpu.HBM)
    out, gstate, wgrad = pl.pallas_call(
        functools.partial(finish, 1.0 / math.sqrt(total_edges)),
        out_shape=(
            jax.ShapeDtypeStruct(blocks, BF16),
            jax.ShapeDtypeStruct(blocks, BF16),
            jax.ShapeDtypeStruct((3, CHUNK, width), F32),
        ),
        in_specs=[vmem, vmem, vmem],
        out_specs=(hbm, hbm, hbm),
        scratch_shapes=[pltpu.VMEM((3, CHUNK, width), F32), dma((3,))],
        compiler_params=pltpu.CompilerParams(vmem_limit_bytes=8 * 2**20),
    )(out, gstate, wgrad)
    return (
        out.reshape(rows, width),
        gstate.reshape(rows, width),
        wgrad.reshape(3 * CHUNK, width),
    )


def norm_rows(hidden):
    return hidden * lax.rsqrt(jnp.mean(hidden * hidden, axis=-1, keepdims=True) + 1e-06)


def layer_forward(hidden, weight):
    normed = norm_rows(hidden).astype(jnp.bfloat16)
    preact = jnp.dot(normed, weight, preferred_element_type=jnp.float32)
    return (hidden + jax.nn.silu(preact), normed, preact)


def layer_backward(hidden, normed, preact, weight, upstream):
    sigma = jax.nn.sigmoid(preact)
    grad_pre = (upstream * sigma * (1.0 + preact * (1.0 - sigma))).astype(jnp.bfloat16)
    grad_weight = lax.dot_general(
        normed, grad_pre, (((0,), (0,)), ((), ())), preferred_element_type=jnp.float32
    )
    grad_normed = lax.dot_general(
        grad_pre, weight, (((1,), (1,)), ((), ())), preferred_element_type=jnp.float32
    )
    inverse = lax.rsqrt(jnp.mean(hidden * hidden, axis=-1, keepdims=True) + 1e-06)
    unit = hidden * inverse
    inner = jnp.mean(grad_normed * unit, axis=-1, keepdims=True)
    return (upstream + inverse * (grad_normed - unit * inner), grad_weight)


def flip_rows(blocks):
    count, height, width = blocks.shape
    return blocks.reshape(count, height // 2, 2, width)[:, :, ::-1, :].reshape(count, height, width)


def route_plan(partner, own_index, group_count):
    block_count = partner.shape[0]
    target = partner // block_count
    remote = partner % block_count
    order = jnp.arange(block_count)
    same = target[:, None] == target[None, :]
    send_rank = jnp.sum(same & (order[None, :] < order[:, None]), axis=1)
    recv_rank = jnp.sum(same & (remote[None, :] < remote[:, None]), axis=1)
    local_pair = target == own_index
    slots = jnp.arange(group_count * CAP)
    send_slot = target * CAP + send_rank
    recv_slot = target * CAP + recv_rank
    pack_matrix = ((slots[:, None] == send_slot[None, :]) & ~local_pair[None, :]).astype(
        jnp.bfloat16
    )
    unpack_matrix = ((recv_slot[:, None] == slots[None, :]) & ~local_pair[:, None]).astype(
        jnp.bfloat16
    )
    return (pack_matrix, unpack_matrix, local_pair)


def pack_blocks(values, pack_matrix, block_count):
    blocks = values.reshape(block_count, -1, values.shape[1])
    return jnp.einsum("sn,nrd->srd", pack_matrix, blocks, preferred_element_type=jnp.bfloat16)


def unpack_blocks(arrived, unpack_matrix, local_pair, values, block_count):
    blocks = values.reshape(block_count, -1, values.shape[1])
    distant = jnp.einsum("ns,srd->nrd", unpack_matrix, arrived, preferred_element_type=jnp.bfloat16)
    joined = jnp.where(local_pair[:, None, None], blocks, distant)
    return flip_rows(joined).reshape(values.shape)


def local(edge_state, basis, weights, partner, cotangent):
    row_count, width = edge_state.shape
    block_count = partner.shape[0]
    group_count = lax.axis_size("grp")
    own_index = lax.axis_index("grp")
    total_edges = row_count * group_count * lax.axis_size("blk")
    pack_matrix, unpack_matrix, local_pair = route_plan(partner, own_index, group_count)
    mixed = jnp.einsum(
        "aij,ajd->aid",
        basis,
        edge_state.reshape(-1, NBR, width),
        preferred_element_type=jnp.float32,
    ).reshape(row_count, width)
    first, normed_one, pre_one = layer_forward(mixed, weights[0])
    second, normed_two, pre_two = layer_forward(first, weights[1])
    sent = second.astype(jnp.bfloat16)
    arrived = lax.all_to_all(
        pack_blocks(sent, pack_matrix, block_count), "grp", split_axis=0, concat_axis=0, tiled=True
    )
    reversed_state = unpack_blocks(arrived, unpack_matrix, local_pair, sent, block_count)
    summed = second + reversed_state.astype(jnp.float32)
    final, normed_three, pre_three = layer_forward(summed, weights[2])
    edge_out = final.astype(jnp.bfloat16)
    grad_summed, grad_three = layer_backward(
        summed, normed_three, pre_three, weights[2], cotangent.astype(jnp.float32)
    )
    grad_reversed = grad_summed.astype(jnp.bfloat16)
    returned = lax.all_to_all(
        pack_blocks(grad_reversed, pack_matrix, block_count),
        "grp",
        split_axis=0,
        concat_axis=0,
        tiled=True,
    )
    grad_sent = unpack_blocks(returned, unpack_matrix, local_pair, grad_reversed, block_count)
    grad_second = grad_summed + grad_sent.astype(jnp.float32)
    grad_first, grad_two = layer_backward(first, normed_two, pre_two, weights[1], grad_second)
    grad_mixed, grad_one = layer_backward(mixed, normed_one, pre_one, weights[0], grad_first)
    grad_round = grad_mixed.astype(jnp.bfloat16).reshape(-1, NBR, width)
    grad_state = (
        jnp.einsum("aij,aid->ajd", basis, grad_round, preferred_element_type=jnp.float32)
        .reshape(row_count, width)
        .astype(jnp.bfloat16)
    )
    local_grads = jnp.concatenate([grad_one, grad_two, grad_three], axis=0)
    group_part = lax.psum_scatter(
        local_grads.astype(jnp.bfloat16), "grp", scatter_dimension=0, tiled=True
    ).astype(jnp.float32)
    summed_grads = lax.psum_scatter(group_part, "blk", scatter_dimension=0, tiled=True)
    weight_grad = summed_grads * (1.0 / math.sqrt(total_edges))
    return (edge_out, grad_state, weight_grad)


def solution(mesh):
    spread = P(("grp", "blk"))
    wide = P(("grp", "blk"), None)
    in_specs = (wide, P(("grp", "blk"), None, None), P(), spread, wide)
    body = local
    if mesh.shape["grp"] == 2 and mesh.shape["blk"] == 16:
        body = functools.partial(local_fast, mesh.shape["blk"])
    return jax.shard_map(
        body, mesh=mesh, in_specs=in_specs, out_specs=(wide, wide, wide), check_vma=False
    )
```
